32 devices in a mesh: seq: 8 (over z, y), mp: 4 (over x, core).
Axes of the slice: x: 2, y: 2, z: 4, core: 2. Of those that a mesh axis runs over, the one named last changes fastest.
Arguments:
- ids: int32 [1024], P('seq'), may hold values from 0 to 3
- hidden_fwd: bfloat16 [1024, 1024], P('seq', 'mp'), may hold values from -8 to 8
- hidden_rc: bfloat16 [1024, 1024], P('seq', 'mp'), may hold values from -8 to 8
- embed: float32 [4, 1024], P(None, 'mp'), may hold values from -4 to 4
- ln1_gain: float32 [1024], replicated, may hold values from 0.1 to 1.9
- ln2_gain: float32 [1024], replicated, may hold values from 0.1 to 1.9
- mixing: float32 [5, 1024], replicated, may hold values from 0 to 1
- w_receptance: bfloat16 [1024, 1024], P(None, 'mp'), may hold values from -0.1875 to 0.1875
- w_key: bfloat16 [1024, 1024], P(None, 'mp'), may hold values from -0.1875 to 0.1875
- w_value: bfloat16 [1024, 1024], P(None, 'mp'), may hold values from -0.1875 to 0.1875
- decay_first_weight: bfloat16 [1024, 64], replicated, may hold values from -0.1875 to 0.1875
- decay_base: float32 [1024], P('mp'), may hold values from -11 to 1
- decay_second_weight: bfloat16 [64, 1024], P(None, 'mp'), may hold values from -0.75 to 0.75
- context_rate_first_weight: bfloat16 [1024, 64], replicated, may hold values from -0.1875 to 0.1875
- iclr_base: float32 [1024], P('mp'), may hold values from -9 to 1
- context_rate_second_weight: bfloat16 [64, 1024], P(None, 'mp'), may hold values from -0.75 to 0.75
- group_gain: float32 [1024], P('mp'), may hold values from 0.1 to 1.9
- w_output: bfloat16 [1024, 1024], P('mp'), may hold values from -0.1875 to 0.1875
- ffn_key: bfloat16 [1024, 4096], P(None, 'mp'), may hold values from -0.1875 to 0.1875
- ffn_value: bfloat16 [4096, 1024], P('mp'), may hold values from -0.09375 to 0.09375
Outputs:
- merged: bfloat16 [1024, 1024], P('seq', 'mp')
The draws below stay inside these ranges and needn't reach their ends.
Inputs may be any that keep to these rules, and one draw needn't show every extreme that they name: `ids`: bases A, C, G, T are 0, 1, 2, 3; the complement of base c is 3 - c.
All inputs are finite; a program needn't handle non-finite values.
Results may differ from the reference program's by a relative error of at most 0.01.
Values may be sent and summed in bfloat16 or wider, within the bound.
No kernel may reach another device: no remote copies, remote signals or barrier semaphores. Data moves between devices by JAX's collectives and lax.ppermute only.
A program may use at most 64 MiB of HBM per device.

```python
import jax
import jax.numpy as jnp
from jax import lax

MODEL_WIDTH = 1024
HEADS = 16
HEAD = 64
FF = 4096
RANK_WIDTH = 64
LENGTH = 1024


def stream_draw(key, salt):
    base_key = jax.random.fold_in(key, salt)
    noise_key = jax.random.fold_in(base_key, 1)
    rough_key = jax.random.fold_in(base_key, 2)
    column = jnp.arange(MODEL_WIDTH, dtype=jnp.float32) / (MODEL_WIDTH - 1)
    rough = jnp.exp(jax.random.uniform(rough_key, (MODEL_WIDTH,), jnp.float32, -0.2877, 0.2877))
    noise = jnp.clip(jax.random.normal(noise_key, (LENGTH, MODEL_WIDTH), jnp.float32), -3.0, 3.0)
    scales = 0.4 * jnp.exp(jnp.log(5.0) * column) * rough
    centre = -0.6 + 1.5 * column
    values = centre[None, :] + scales[None, :] * noise
    return jnp.clip(values, -8.0, 8.0).astype(jnp.bfloat16)


def draw_hidden_fwd(key, part):
    return stream_draw(key, 101)


def draw_hidden_rc(key, part):
    return stream_draw(key, 202)


def place_ends(drawn, rng, least, largest):
    index_at = [jax.random.randint(jax.random.fold_in(rng, axis), (), 0, length) for axis, length in enumerate(drawn.shape)]
    widest = drawn.shape.index(max(drawn.shape))
    beside = index_at[:widest] + [(index_at[widest] + 1) % drawn.shape[widest]] + index_at[widest + 1:]
    return drawn.at[tuple(index_at)].set(least).at[tuple(beside)].set(largest)


def block_levels(own_key, extent, cuts, least, top_value):
    level, own = 1.0, jax.random.fold_in(own_key, 6)
    for position, shards_of in cuts:
        draws = jnp.exp(jax.random.uniform(jax.random.fold_in(own, position), (shards_of,), jnp.float32, least / len(cuts), top_value / len(cuts)))
        level = level * jnp.repeat(draws, extent[position] // shards_of).reshape([-1 if axis == position else 1 for axis in range(len(extent))])
    return level


def bell_draw(stream_key, shape, deviation, limit, shards=(), kind=jnp.bfloat16):
    loudness = block_levels(stream_key, shape, shards, -0.22, 0.18) if shards else 1.0
    values = jax.random.normal(stream_key, shape, jnp.float32) * deviation * loudness
    return jnp.minimum(jnp.maximum(values, -limit), limit).astype(kind)


def setup_inputs(seed: int = 0) -> dict:
    arg_keys = jax.random.split(jax.random.key(seed), 21)
    ids = place_ends(jax.random.randint(arg_keys[0], (LENGTH,), 0, 4), jax.random.fold_in(arg_keys[0], 1), 0, 3).astype(jnp.int32)
    hidden_fwd = draw_hidden_fwd(jax.random.fold_in(arg_keys[20], 71), 0)
    hidden_rc = draw_hidden_rc(jax.random.fold_in(arg_keys[20], 71), 0)
    embed = bell_draw(arg_keys[3], (4, MODEL_WIDTH), 1.0, 4.0, ((1, 4),), jnp.float32)
    ln1_gain = jnp.clip(1.0 + 0.18 * jax.random.normal(arg_keys[4], (MODEL_WIDTH,), jnp.float32), 0.1, 1.9)
    ln2_gain = jnp.clip(1.0 + 0.18 * jax.random.normal(arg_keys[5], (MODEL_WIDTH,), jnp.float32), 0.1, 1.9)
    mixing = jnp.clip(jax.random.uniform(arg_keys[6], (5, MODEL_WIDTH), jnp.float32, 0.0, 1.0), 0.0, 1.0)
    w_receptance = bell_draw(arg_keys[7], (MODEL_WIDTH, MODEL_WIDTH), MODEL_WIDTH ** -0.5, 0.1875, ((1, 4),))
    w_key = bell_draw(arg_keys[8], (MODEL_WIDTH, MODEL_WIDTH), MODEL_WIDTH ** -0.5, 0.1875, ((1, 4),))
    w_value = bell_draw(arg_keys[9], (MODEL_WIDTH, MODEL_WIDTH), MODEL_WIDTH ** -0.5, 0.1875, ((1, 4),))
    decay_first_weight = bell_draw(arg_keys[10], (MODEL_WIDTH, RANK_WIDTH), MODEL_WIDTH ** -0.5, 0.1875)
    decay_base = jnp.clip(-11.0 + 12.0 * jax.random.uniform(arg_keys[11], (MODEL_WIDTH,), jnp.float32) ** block_levels(arg_keys[11], (MODEL_WIDTH,), ((0, 4),), -0.2, 0.2), -11.0, 1.0)
    decay_second_weight = bell_draw(arg_keys[12], (RANK_WIDTH, MODEL_WIDTH), RANK_WIDTH ** -0.5, 0.75, ((1, 4),))
    context_rate_first_weight = bell_draw(arg_keys[13], (MODEL_WIDTH, RANK_WIDTH), MODEL_WIDTH ** -0.5, 0.1875)
    iclr_base = jnp.clip(-9.0 + 10.0 * jax.random.uniform(arg_keys[14], (MODEL_WIDTH,), jnp.float32) ** block_levels(arg_keys[14], (MODEL_WIDTH,), ((0, 4),), -0.2, 0.2), -9.0, 1.0)
    context_rate_second_weight = bell_draw(arg_keys[15], (RANK_WIDTH, MODEL_WIDTH), RANK_WIDTH ** -0.5, 0.75, ((1, 4),))
    group_gain = jnp.clip(1.0 + 0.18 * jax.random.normal(arg_keys[16], (MODEL_WIDTH,), jnp.float32), 0.1, 1.9)
    w_output = bell_draw(arg_keys[17], (MODEL_WIDTH, MODEL_WIDTH), MODEL_WIDTH ** -0.5, 0.1875, ((0, 4),))
    ffn_key = bell_draw(arg_keys[18], (MODEL_WIDTH, FF), MODEL_WIDTH ** -0.5, 0.1875, ((1, 4),))
    ffn_value = bell_draw(arg_keys[19], (FF, MODEL_WIDTH), FF ** -0.5, 0.09375, ((0, 4),))
    return dict(ids=ids, hidden_fwd=hidden_fwd, hidden_rc=hidden_rc, embed=embed, ln1_gain=ln1_gain, ln2_gain=ln2_gain, mixing=mixing, w_receptance=w_receptance, w_key=w_key, w_value=w_value, decay_first_weight=decay_first_weight, decay_base=decay_base, decay_second_weight=decay_second_weight, context_rate_first_weight=context_rate_first_weight, iclr_base=iclr_base, context_rate_second_weight=context_rate_second_weight, group_gain=group_gain, w_output=w_output, ffn_key=ffn_key, ffn_value=ffn_value)


PRECISE = lax.Precision.HIGHEST
DECAY_SCALE = 0.606531
NORM_EPS = 1e-05
GROUP_EPS = 0.00064
UNIT_EPS = 1e-06

def layer_norm(values, gain):
    row_mean = lax.optimization_barrier(jnp.mean(values, axis=-1, keepdims=True))
    centered = values - row_mean
    spread = lax.optimization_barrier(jnp.mean(centered * centered, axis=-1, keepdims=True))
    return centered * lax.rsqrt(spread + NORM_EPS) * gain

def project(layer_input, weight):
    flat = layer_input.reshape(-1, layer_input.shape[-1])
    result = jnp.dot(flat, weight, preferred_element_type=jnp.float32)
    return result.reshape(layer_input.shape[:-1] + (weight.shape[1],))

def wkv_step(wkv_state, layer_input):
    receptance, decay_rate, key_vec, value_vec, unit_key, iclr_rate = layer_input
    pulled = jnp.einsum('abhvk,abhk->abhv', wkv_state, unit_key, precision=PRECISE)
    wkv_state = wkv_state * decay_rate[..., None, :] - pulled[..., :, None] * (iclr_rate * unit_key)[..., None, :] + value_vec[..., :, None] * key_vec[..., None, :]
    return (wkv_state, jnp.einsum('abhvk,abhk->abhv', wkv_state, receptance, precision=PRECISE))

def timeline(array):
    ordered = jnp.stack([array[0], array[1][:, ::-1]])
    return jnp.moveaxis(ordered, 2, 0)

def reference(ids, hidden_fwd, hidden_rc, embed, ln1_gain, ln2_gain, mixing, w_receptance, w_key, w_value, decay_first_weight, decay_base, decay_second_weight, context_rate_first_weight, iclr_base, context_rate_second_weight, group_gain, w_output, ffn_key, ffn_value):
    letters = jnp.arange(4, dtype=jnp.int32)
    onehot_fwd = (ids[:, None] == letters[None, :]).astype(jnp.float32)
    onehot_rc = ((3 - ids[::-1])[:, None] == letters[None, :]).astype(jnp.float32)
    strands = jnp.stack([hidden_fwd.astype(jnp.float32) + jnp.dot(onehot_fwd, embed, precision=PRECISE), hidden_rc.astype(jnp.float32) + jnp.dot(onehot_rc, embed, precision=PRECISE)]).astype(jnp.bfloat16)
    strands = lax.optimization_barrier(strands)
    normed = layer_norm(strands.astype(jnp.float32), ln1_gain)
    zero_row = jnp.zeros((2, 1, MODEL_WIDTH), jnp.float32)
    before = jnp.concatenate([zero_row, normed[:, :-1]], axis=1)
    after_row = jnp.concatenate([normed[:, 1:], zero_row], axis=1)
    neighbours = jnp.stack([before, after_row])
    center = normed[None]

    def mixed_input(mix_index):
        return (center + (neighbours - center) * mixing[mix_index]).astype(jnp.bfloat16)
    receptance = project(mixed_input(0), w_receptance)
    key_vec = project(mixed_input(1), w_key)
    value_vec = project(mixed_input(2), w_value)
    decay_low = jnp.tanh(project(mixed_input(3), decay_first_weight)).astype(jnp.bfloat16)
    log_decay = -DECAY_SCALE * jax.nn.sigmoid(decay_base + project(decay_low, decay_second_weight))
    iclr_low = project(mixed_input(4), context_rate_first_weight).astype(jnp.bfloat16)
    iclr_rate = jax.nn.sigmoid(iclr_base + project(iclr_low, context_rate_second_weight))
    head_shape = (2, 2, LENGTH, HEADS, HEAD)
    per_head = [array.reshape(head_shape) for array in (receptance, log_decay, key_vec, value_vec, iclr_rate)]
    key_square = lax.optimization_barrier(jnp.sum(per_head[2] * per_head[2], axis=-1, keepdims=True))
    unit_key = per_head[2] * lax.rsqrt(key_square + UNIT_EPS)
    sequence_in = (timeline(per_head[0]), timeline(jnp.exp(per_head[1])), timeline(per_head[2]), timeline(per_head[3]), timeline(unit_key), timeline(per_head[4]))
    start_state = jnp.zeros((2, 2, HEADS, HEAD, HEAD), jnp.float32)
    _, wkv_out = lax.scan(wkv_step, start_state, sequence_in)
    wkv_out = jnp.moveaxis(wkv_out, 0, 2)
    wkv_out = jnp.stack([wkv_out[0], wkv_out[1][:, ::-1]])
    head_mean = lax.optimization_barrier(jnp.mean(wkv_out, axis=-1, keepdims=True))
    centered = wkv_out - head_mean
    head_spread = lax.optimization_barrier(jnp.mean(centered * centered, axis=-1, keepdims=True))
    grouped = (centered * lax.rsqrt(head_spread + GROUP_EPS)).reshape(2, 2, LENGTH, MODEL_WIDTH) * group_gain
    joined = (grouped[0] + grouped[1]).astype(jnp.bfloat16)
    residual = strands.astype(jnp.float32) + project(joined, w_output)
    ffn_in = layer_norm(residual, ln2_gain).astype(jnp.bfloat16)
    activated = jnp.square(jax.nn.relu(project(ffn_in, ffn_key))).astype(jnp.bfloat16)
    strand_out = residual + project(activated, ffn_value)
    rc_final = lax.optimization_barrier(strand_out[1].astype(jnp.bfloat16))
    return (strand_out[0] + rc_final[::-1].astype(jnp.float32)).astype(jnp.bfloat16)
```

```python
import functools

import jax
import jax.numpy as jnp
from jax import lax
from jax.experimental import pallas as pl
from jax.experimental.pallas import tpu as pltpu
from jax.sharding import PartitionSpec as P

HEAD = 64
DECAY_SCALE = 0.606531
NORM_EPS = 1e-05
GROUP_EPS = 0.00064
UNIT_EPS = 1e-06
RADIX = 4
F32 = jnp.float32
BF16 = jnp.bfloat16
VMEM_BYTES = 40 * 1024 * 1024


def mm(left, right):
    return jnp.dot(left, right, preferred_element_type=F32)


def mm_rows(left, right):
    return lax.dot_general(left, right, (((1,), (1,)), ((), ())), preferred_element_type=F32)


def mm_cols(left, right):
    return lax.dot_general(left, right, (((0,), (0,)), ((), ())), preferred_element_type=F32)


def halves(value):
    high = value.astype(BF16)
    return high, (value - high.astype(F32)).astype(BF16)


def head_sum(value, ones):
    high, low = halves(value)
    return mm(high, ones) + mm(low, ones)


def ids_of(shape, dim):
    return lax.broadcasted_iota(jnp.int32, shape, dim)


def block_ones(width):
    same = ids_of((width, width), 0) // HEAD == ids_of((width, width), 1) // HEAD
    return same


def spread(packed, same_head):
    tiled = jnp.concatenate([packed] * (packed.shape[1] // HEAD), axis=0)
    return jnp.where(same_head, tiled, jnp.zeros_like(tiled))


def layer_norm(values, gain):
    row_mean = jnp.mean(values, axis=-1, keepdims=True)
    centered = values - row_mean
    variance = jnp.mean(centered * centered, axis=-1, keepdims=True)
    return centered * lax.rsqrt(variance + NORM_EPS) * gain


def strands_kernel(ids_ref, fwd_ref, rc_ref, embed_ref, out_ref):
    rows = fwd_ref.shape[0]
    ids = ids_ref[...]
    letters = ids_of((embed_ref.shape[0], rows), 0)
    embed = embed_ref[...]

    def looked_up(values):
        onehot = (values == letters).astype(F32)
        return lax.dot_general(
            onehot,
            embed,
            (((0,), (0,)), ((), ())),
            precision=lax.Precision.HIGHEST,
            preferred_element_type=F32,
        )

    out_ref[0] = (fwd_ref[...].astype(F32) + looked_up(ids)).astype(BF16)
    flip = (ids_of((rows, rows), 0) + ids_of((rows, rows), 1) == rows - 1).astype(F32)
    turned = mm(flip.astype(BF16), rc_ref[...])
    out_ref[1] = (turned + looked_up(3 - ids)).astype(BF16)


def inverse_of(pulls, rows):
    row_ids, col_ids = ids_of((rows, rows), 0), ids_of((rows, rows), 1)
    eye = (row_ids == col_ids).astype(F32)
    size = 1
    inverses = None
    while size < rows:
        within = (row_ids // (2 * size) == col_ids // (2 * size)) & (row_ids // size != col_ids // size)
        parts = [jnp.where(within, pull, 0.0) for pull in pulls]
        if size == 1:
            inverses = [eye + part for part in parts]
        else:
            lows = [inverse.astype(BF16) for inverse in inverses]
            products = [mm(part.astype(BF16), low).astype(BF16) for part, low in zip(parts, lows)]
            inverses = [inverse + mm(low, product) for inverse, low, product in zip(inverses, lows, products)]
        size *= 2
    return inverses


def chunk_kernel(
    x_ref,
    before_ref,
    after_ref,
    gain_ref,
    mixing_ref,
    w_r_ref,
    w_k_ref,
    w_v_ref,
    w_d1_ref,
    d_base_ref,
    w_d2_ref,
    w_c1_ref,
    c_base_ref,
    w_c2_ref,
    local_ref,
    map_ref,
    up_ref,
    down_ref,
    normed,
    mixed,
    r_buf,
    k_buf,
    v_buf,
    d_buf,
    a_buf,
):
    strands, rows, _ = x_ref.shape
    width = w_r_ref.shape[1]
    heads = width // HEAD
    pad = 8
    gain = gain_ref[...]
    before = layer_norm(before_ref[...].astype(F32), gain)
    after = layer_norm(after_ref[...].astype(F32), gain)
    for s in range(strands):
        normed[s, pad : pad + rows, :] = layer_norm(x_ref[s].astype(F32), gain)
        normed[s, pad - 1 : pad, :] = before[s : s + 1]
        normed[s, pad + rows : pad + rows + 1, :] = after[s : s + 1]

    def mix(index):
        weight = mixing_ref[index : index + 1, :]
        for s in range(strands):
            center = normed[s, pad : pad + rows, :]
            for d in range(2):
                shift = pad - 1 + 2 * d
                neighbour = normed[s, shift : shift + rows, :]
                start = (d * strands + s) * rows
                mixed[start : start + rows, :] = (center + (neighbour - center) * weight).astype(BF16)
        return mixed[...]

    groups = 2 * strands
    shape = (groups, rows, width)
    r_buf[...] = mm(mix(0), w_r_ref[...]).reshape(shape)
    k_buf[...] = mm(mix(1), w_k_ref[...]).reshape(shape)
    v_buf[...] = mm(mix(2), w_v_ref[...]).reshape(shape)
    decay_low = jnp.tanh(mm(mix(3), w_d1_ref[...])).astype(BF16)
    d_buf[...] = (-DECAY_SCALE * jax.nn.sigmoid(d_base_ref[...] + mm(decay_low, w_d2_ref[...]))).reshape(shape)
    rate_low = mm(mix(4), w_c1_ref[...]).astype(BF16)
    a_buf[...] = jax.nn.sigmoid(c_base_ref[...] + mm(rate_low, w_c2_ref[...])).reshape(shape)

    def group(g):
        d = g // strands
        sign = 1 - 2 * d
        order = (ids_of((rows, rows), 0) - ids_of((rows, rows), 1)) * sign
        strict, inclusive = order > 0, order >= 0
        same = block_ones(width)
        ones = same.astype(F32).astype(BF16)
        lane_head = ids_of((1, width), 1) // HEAD

        def of_heads(value):
            return jnp.concatenate(
                [jnp.where(lane_head == h, value, 0.0).astype(BF16) for h in range(heads)], axis=0
            )

        receptance, key, value = r_buf[g], k_buf[g], v_buf[g]
        log_decay, rate = d_buf[g], a_buf[g]
        unit = key * lax.rsqrt(head_sum(key * key, ones) + UNIT_EPS)
        tri = inclusive.astype(F32).astype(BF16)
        high, low = halves(log_decay)
        totals = mm(tri, high) + mm(tri, low)
        middle = totals[rows // 2 : rows // 2 + 1]
        final = jnp.where(d == 0, totals[rows - 1 : rows], totals[0:1])
        here = jnp.exp(totals - middle)
        there = jnp.exp(middle - totals)
        left_prev = -unit * jnp.exp(totals - log_decay - middle)
        left_here = receptance * here
        right_insert = rate * unit * there
        right_key = key * there
        from_start = jnp.exp(middle)
        to_end = jnp.exp(final - middle)
        left = jnp.concatenate([left_prev, left_here], axis=0).astype(BF16)
        insert_pulls, key_pulls, insert_reads, key_reads = [], [], [], []
        for h in range(heads):
            mask = lane_head == h
            right = jnp.concatenate(
                [jnp.where(mask, right_insert, 0.0), jnp.where(mask, right_key, 0.0)], axis=0
            ).astype(BF16)
            scores = mm_rows(left, right)
            insert_pulls.append(jnp.where(strict, scores[:rows, :rows], 0.0))
            key_pulls.append(jnp.where(strict, scores[:rows, rows:], 0.0).astype(BF16))
            insert_reads.append(jnp.where(inclusive, scores[rows:, :rows], 0.0).astype(BF16))
            key_reads.append(jnp.where(inclusive, scores[rows:, rows:], 0.0).astype(BF16))
        values = of_heads(value)
        value_pull = mm(jnp.concatenate(key_pulls, axis=1), values)
        inverses = inverse_of(insert_pulls, rows)
        inverse = jnp.concatenate([item.astype(BF16) for item in inverses], axis=1)
        local_pull = mm(inverse, of_heads(value_pull))
        start_pull = mm(inverse, of_heads(left_prev * from_start))
        insert_read = jnp.concatenate(insert_reads, axis=1)
        key_read = jnp.concatenate(key_reads, axis=1)
        local_ref[g] = mm(insert_read, of_heads(local_pull)) + mm(key_read, values)
        map_ref[g] = (left_here * from_start + mm(insert_read, of_heads(start_pull))).astype(BF16)
        tail_insert = (right_insert * to_end).astype(BF16)
        tail_key = (right_key * to_end).astype(BF16)
        ends = mm_cols(tail_insert, local_pull.astype(BF16)) + mm_cols(tail_key, value.astype(BF16))
        maps = mm_cols(tail_insert, start_pull.astype(BF16))
        ends = jnp.where(same, ends, 0.0)
        maps = jnp.where(same, maps, 0.0)
        end = sum(ends[h * HEAD : (h + 1) * HEAD] for h in range(heads))
        across = sum(maps[h * HEAD : (h + 1) * HEAD] for h in range(heads))
        diagonal = ids_of((HEAD, width), 0) == ids_of((HEAD, width), 1) % HEAD
        across = across + jnp.where(diagonal, jnp.exp(final), 0.0)
        return jnp.concatenate([end, across], axis=0).astype(BF16)

    def up_group(s, carry):
        up_ref[s] = group(s)
        return carry

    def down_group(s, carry):
        down_ref[s] = group(s + strands)
        return carry

    lax.fori_loop(0, strands, up_group, 0)
    lax.fori_loop(0, strands, down_group, 0)


def composed(later, earlier, same_head, state_only=False):
    across = later[HEAD:].astype(BF16)
    state = mm(across, spread(earlier[:HEAD].astype(BF16), same_head)) + later[:HEAD].astype(F32)
    if state_only:
        return state
    return jnp.concatenate([state, mm(across, spread(earlier[HEAD:].astype(BF16), same_head))], axis=0)


def window_of(received, same_head, state_only):
    total = received[-1].astype(F32)
    for item in reversed(received[:-1]):
        total = composed(item, total, same_head, state_only)
    return total


def advance_kernel(has_window, count, state_only, *refs):
    taken = 1 + int(has_window) + count
    for d in range(2):
        ins = refs[d * taken : (d + 1) * taken]
        window_ref, current_ref = refs[2 * taken + 2 * d : 2 * taken + 2 * d + 2]
        same_head = block_ones(ins[0].shape[2])
        for s in range(ins[0].shape[0]):
            parts = [ref[s] for ref in ins]
            window = window_of(parts[taken - count :], same_head, False)
            current_ref[s] = composed(parts[0], window, same_head, state_only).astype(BF16)
            if has_window:
                window = composed(parts[1], window, same_head)
            window_ref[s] = window


def finish_kernel(has_window, count, state_only, *refs):
    taken = int(has_window) + count
    local_ref, map_ref, gain_ref, out_ref = refs[2 * taken :]
    strands, _, width = out_ref.shape
    same_head = block_ones(width)
    ones = same_head.astype(F32).astype(BF16)
    gain = gain_ref[...]
    for s in range(strands):
        joined = 0.0
        for d in range(2):
            parts = [ref[s] for ref in refs[d * taken : (d + 1) * taken]]
            state = window_of(parts[int(has_window) :], same_head, state_only)[:HEAD]
            if has_window:
                state = composed(parts[0], state, same_head, True)
            g = d * strands + s
            wkv = local_ref[g] + mm(map_ref[g], spread(state.astype(BF16), same_head))
            centered = wkv - head_sum(wkv, ones) * (1.0 / HEAD)
            variance = head_sum(centered * centered, ones) * (1.0 / HEAD)
            joined = joined + centered * lax.rsqrt(variance + GROUP_EPS)
        out_ref[s] = (joined * gain).astype(BF16)


def mix_kernel(index_ref, joined_ref, x_ref, w_ref, gain_ref, up_ref, down_ref, own_ref, *rest):
    *sent_refs, partial, total = rest
    strands, rows, _ = x_ref.shape
    width = own_ref.shape[1]
    gain = gain_ref[...]
    joined = jnp.concatenate([joined_ref[s] for s in range(strands)], axis=0)
    attention = mm(joined, w_ref[...])
    residuals = [x_ref[s].astype(F32) + attention[s * rows : (s + 1) * rows] for s in range(strands)]
    inner = jnp.concatenate([layer_norm(item, gain).astype(BF16) for item in residuals], axis=0)
    active = jnp.square(jnp.maximum(mm(inner, up_ref[...]), 0.0)).astype(BF16).astype(F32)
    added = sum(active[s * rows : (s + 1) * rows] for s in range(strands)).astype(BF16)
    partial[...] = mm(added, down_ref[...])
    total[...] = sum(residuals)

    def part(ref, which):
        return ref[:, pl.ds(pl.multiple_of(which * width, width), width)]

    me = index_ref[0]
    own_ref[...] = part(total, me) + part(partial, me)
    size = len(sent_refs) + 1
    for step, ref in enumerate(sent_refs):
        ref[...] = part(partial, lax.rem(me + step + 1, size)).astype(BF16)


def call(kernel, out_shape, scratch=(), **kwargs):
    return pl.pallas_call(
        kernel,
        out_shape=out_shape,
        scratch_shapes=list(scratch),
        compiler_params=pltpu.CompilerParams(vmem_limit_bytes=VMEM_BYTES),
        **kwargs,
    )


def shifted(value, axis, distance):
    devices = range(lax.axis_size(axis))
    return lax.ppermute(value, axis, [(i, i + distance) for i in devices if i + distance in devices])


def on_device(
    ids,
    hidden_fwd,
    hidden_rc,
    embed,
    ln1_gain,
    ln2_gain,
    mixing,
    w_receptance,
    w_key,
    w_value,
    decay_first_weight,
    decay_base,
    decay_second_weight,
    context_rate_first_weight,
    iclr_base,
    context_rate_second_weight,
    group_gain,
    w_output,
    ffn_key,
    ffn_value,
):
    rows, width = hidden_fwd.shape
    seq_count, mp_count = lax.axis_size("seq"), lax.axis_size("mp")
    strands, full = 2, ffn_key.shape[0]
    struct = jax.ShapeDtypeStruct

    mirror = [(i, seq_count - 1 - i) for i in range(seq_count)]
    rc_here = lax.ppermute(hidden_rc, "seq", mirror)
    local = call(strands_kernel, struct((strands, rows, width), BF16))(
        ids.reshape(1, rows), hidden_fwd, rc_here, embed
    )
    whole = lax.all_gather(local, "mp", axis=2, tiled=True)
    before = shifted(whole[:, rows - 1], "seq", 1)
    after = shifted(whole[:, 0], "seq", -1)
    w_output_whole = lax.all_gather(w_output, "mp", axis=0, tiled=True)

    groups = 2 * strands
    state_shape = (strands, 2 * HEAD, width)
    lanes = pltpu.VMEM((groups, rows, width), F32)
    local_out, start_map, up, down = call(
        chunk_kernel,
        (
            struct((groups, rows, width), F32),
            struct((groups, rows, width), BF16),
            struct(state_shape, BF16),
            struct(state_shape, BF16),
        ),
        scratch=[
            pltpu.VMEM((strands, rows + 16, full), F32),
            pltpu.VMEM((groups * rows, full), BF16),
            lanes,
            lanes,
            lanes,
            lanes,
            lanes,
        ],
    )(
        whole,
        before,
        after,
        ln1_gain.reshape(1, full),
        mixing,
        w_receptance,
        w_key,
        w_value,
        decay_first_weight,
        decay_base.reshape(1, width),
        decay_second_weight,
        context_rate_first_weight,
        iclr_base.reshape(1, width),
        context_rate_second_weight,
    )

    currents, windows = [up, down], [None, None]
    distance = 1
    while True:
        steps = [step for step in range(1, RADIX) if step * distance < seq_count]
        received = [
            [shifted(current, "seq", sign * step * distance) for step in steps]
            for current, sign in zip(currents, (1, -1))
        ]
        has_window = windows[0] is not None
        reach = distance * RADIX
        if reach >= seq_count:
            break
        state_only = 2 * reach >= seq_count
        current_struct = struct((strands, HEAD, width) if state_only else state_shape, BF16)
        operands = []
        for d in range(2):
            operands += [currents[d]] + ([windows[d]] if has_window else []) + received[d]
        outs = call(
            functools.partial(advance_kernel, has_window, len(steps), state_only),
            (struct(state_shape, F32), current_struct) * 2,
        )(*operands)
        windows, currents = [outs[0], outs[2]], [outs[1], outs[3]]
        distance = reach

    operands = []
    for d in range(2):
        operands += ([windows[d]] if has_window else []) + received[d]
    joined = call(
        functools.partial(finish_kernel, has_window, len(steps), len(steps) == 1),
        struct((strands, rows, width), BF16),
    )(*operands, local_out, start_map, group_gain.reshape(1, width))
    joined_whole = lax.all_gather(joined, "mp", axis=2, tiled=True)

    position = lax.axis_index("mp").astype(jnp.int32).reshape(1)
    vmem = pl.BlockSpec(memory_space=pltpu.VMEM)
    own, *sent = call(
        mix_kernel,
        (struct((rows, width), F32),) + (struct((rows, width), BF16),) * (mp_count - 1),
        scratch=[pltpu.VMEM((rows, full), F32), pltpu.VMEM((rows, full), F32)],
        in_specs=[pl.BlockSpec(memory_space=pltpu.SMEM)] + [vmem] * 6,
    )(position, joined_whole, whole, w_output_whole, ln2_gain.reshape(1, full), ffn_key, ffn_value)
    merged = own
    for step, item in enumerate(sent):
        pairs = [(i, (i + step + 1) % mp_count) for i in range(mp_count)]
        merged = merged + lax.ppermute(item, "mp", pairs).astype(F32)
    return merged.astype(BF16)


def solution(mesh):
    in_specs = (
        P("seq"),
        P("seq", "mp"),
        P("seq", "mp"),
        P(None, "mp"),
        P(),
        P(),
        P(),
        P(None, "mp"),
        P(None, "mp"),
        P(None, "mp"),
        P(),
        P("mp"),
        P(None, "mp"),
        P(),
        P("mp"),
        P(None, "mp"),
        P("mp"),
        P("mp", None),
        P(None, "mp"),
        P("mp", None),
    )
    out_specs = P("seq", "mp")
    return jax.shard_map(
        on_device, mesh=mesh, in_specs=in_specs, out_specs=out_specs, check_vma=False
    )
```

```python
import functools

import jax
import jax.numpy as jnp
from jax import lax
from jax.experimental import pallas as pl
from jax.experimental.pallas import tpu as pltpu
from jax.sharding import PartitionSpec as P

HEAD = 64
DECAY_SCALE = 0.606531
NORM_EPS = 1e-05
GROUP_EPS = 0.00064
UNIT_EPS = 1e-06
RADIX = 4
F32 = jnp.float32
BF16 = jnp.bfloat16
VMEM_BYTES = 32 * 1024 * 1024
VMEM_SPEC = pl.BlockSpec(memory_space=pltpu.VMEM)
SMEM_SPEC = pl.BlockSpec(memory_space=pltpu.SMEM)
ANY_SPEC = pl.BlockSpec(memory_space=pl.ANY)


def mm(left, right):
    return jnp.dot(left, right, preferred_element_type=F32)


def mm_rows(left, right):
    return lax.dot_general(left, right, (((1,), (1,)), ((), ())), preferred_element_type=F32)


def mm_cols(left, right):
    return lax.dot_general(left, right, (((0,), (0,)), ((), ())), preferred_element_type=F32)


def halves(value):
    high = value.astype(BF16)
    return high, (value - high.astype(F32)).astype(BF16)


def head_sum(value, ones):
    high, low = halves(value)
    return mm(high, ones) + mm(low, ones)


def ids_of(shape, dim):
    return lax.broadcasted_iota(jnp.int32, shape, dim)


def block_ones(width):
    same = ids_of((width, width), 0) // HEAD == ids_of((width, width), 1) // HEAD
    return same


def spread(packed, same_head):
    tiled = jnp.concatenate([packed] * (packed.shape[1] // HEAD), axis=0)
    return jnp.where(same_head, tiled, jnp.zeros_like(tiled))


def layer_norm(values, gain):
    row_mean = jnp.mean(values, axis=-1, keepdims=True)
    centered = values - row_mean
    variance = jnp.mean(centered * centered, axis=-1, keepdims=True)
    return centered * lax.rsqrt(variance + NORM_EPS) * gain


def strands_kernel(*refs):
    ins, out_ref, locals_, sems = refs[:4], refs[4], refs[5:9], refs[9]
    arrived(copied(ins, locals_, sems))
    ids_ref, fwd_ref, rc_ref, embed_ref = locals_
    rows = fwd_ref.shape[0]
    ids = ids_ref[...]
    letters = ids_of((embed_ref.shape[0], rows), 0)
    embed = embed_ref[...]

    def looked_up(values):
        onehot = (values == letters).astype(F32)
        return lax.dot_general(
            onehot,
            embed,
            (((0,), (0,)), ((), ())),
            precision=lax.Precision.HIGHEST,
            preferred_element_type=F32,
        )

    out_ref[0] = (fwd_ref[...].astype(F32) + looked_up(ids)).astype(BF16)
    flip = (ids_of((rows, rows), 0) + ids_of((rows, rows), 1) == rows - 1).astype(F32)
    turned = mm(flip.astype(BF16), rc_ref[...])
    out_ref[1] = (turned + looked_up(3 - ids)).astype(BF16)


def inverse_of(pulls, rows):
    row_ids, col_ids = ids_of((rows, rows), 0), ids_of((rows, rows), 1)
    eye = (row_ids == col_ids).astype(F32)
    size = 1
    inverses = None
    while size < rows:
        within = (row_ids // (2 * size) == col_ids // (2 * size)) & (row_ids // size != col_ids // size)
        parts = [jnp.where(within, pull, 0.0) for pull in pulls]
        if size == 1:
            inverses = [eye + part for part in parts]
        else:
            lows = [inverse.astype(BF16) for inverse in inverses]
            products = [mm(part.astype(BF16), low).astype(BF16) for part, low in zip(parts, lows)]
            inverses = [inverse + mm(low, product) for inverse, low, product in zip(inverses, lows, products)]
        size *= 2
    return inverses


def copied(sources, targets, sems):
    copies = [pltpu.make_async_copy(src, dst, sems.at[i]) for i, (src, dst) in enumerate(zip(sources, targets))]
    for item in copies:
        item.start()
    return copies


def arrived(copies):
    for item in copies:
        item.wait()


def gates(decay_mix, rate_mix, d_base, w_d2, c_base, w_c2, w_d1, w_c1):
    decay_low = jnp.tanh(mm_rows(decay_mix, w_d1)).astype(BF16)
    log_decay = -DECAY_SCALE * jax.nn.sigmoid(d_base + mm(decay_low, w_d2))
    rate_low = mm_rows(rate_mix, w_c1).astype(BF16)
    return log_decay, jax.nn.sigmoid(c_base + mm(rate_low, w_c2))


def project_kernel(x_ref, w_r_ref, w_k_ref, w_v_ref, *refs):
    smalls, refs = refs[:8], refs[8:]
    outs, edge_ref = refs[:5], refs[5]
    normed, mixed = refs[6:8]
    locals_, sems = refs[8:16], refs[16]
    gain_ref, mixing_ref, w_d1, w_c1, d_base, w_d2, c_base, w_c2 = locals_
    copies = copied(smalls, locals_, sems)
    strands, rows, _ = x_ref.shape
    width = w_r_ref.shape[1]
    pad = 8
    arrived(copies[:2])
    gain = gain_ref[...]
    for s in range(strands):
        values = layer_norm(x_ref[s].astype(F32), gain)
        normed[s, pad : pad + rows, :] = values
        normed[s, pad - 1 : pad, :] = jnp.zeros_like(values[:1])
        normed[s, pad + rows : pad + rows + 1, :] = jnp.zeros_like(values[:1])
        edge_ref[s : s + 1, :] = values[:1]
        edge_ref[strands + s : strands + s + 1, :] = values[rows - 1 :]

    def mix(index):
        weight = mixing_ref[index : index + 1, :]
        for s in range(strands):
            center = normed[s, pad : pad + rows, :]
            for d in range(2):
                shift = pad - 1 + 2 * d
                neighbour = normed[s, shift : shift + rows, :]
                start = (d * strands + s) * rows
                mixed[start : start + rows, :] = (center + (neighbour - center) * weight).astype(BF16)
        return mixed[...]

    shape = (2 * strands, rows, width)
    for index, w_ref in enumerate((w_r_ref, w_k_ref, w_v_ref)):
        outs[index][...] = mm(mix(index), w_ref[...]).reshape(shape)
    arrived(copies[2:])
    log_decay, rate = gates(
        mix(3), mix(4), d_base[...], w_d2[...], c_base[...], w_c2[...], w_d1[...], w_c1[...]
    )
    outs[3][...] = log_decay.reshape(shape)
    outs[4][...] = rate.reshape(shape)


def masked_heads(value, lane_head, heads):
    return jnp.concatenate([jnp.where(lane_head == h, value, 0.0).astype(BF16) for h in range(heads)], axis=0)


def chunk_kernel(first, direction_ref, *refs):
    lanes, refs = refs[:5], refs[5:]
    if first:
        before_ref, after_ref, edge_ref, w_r_ref, w_k_ref, w_v_ref = refs[:6]
        smalls, refs = refs[6:14], refs[14:]
    else:
        edges_ref, refs = refs[0], refs[1:]
    state_ref, here_ref, insert_ref, key_ref, value_ref, pull_ref, start_ref, read_ref = refs[:8]
    refs = refs[8:]
    if first:
        edges_ref, refs = refs[0], refs[1:]
    r_buf, k_buf, v_buf, d_buf, a_buf = refs[:5]
    sems, refs = refs[5], refs[6:]
    strands, rows, width = r_buf.shape
    heads = width // HEAD
    d = direction_ref[0]
    copies = copied([ref.at[pl.ds(d * strands, strands)] for ref in lanes], (r_buf, k_buf, v_buf, d_buf, a_buf), sems)
    if first:
        locals_, small_sems = refs[:8], refs[8]
        small_copies = copied(smalls, locals_, small_sems)
        gain_ref, mixing_ref, w_d1, w_c1, d_base, w_d2, c_base, w_c2 = locals_
        arrived(small_copies)
        gain = gain_ref[...]
        center = edge_ref[...]
        halo = jnp.concatenate([before_ref[...], after_ref[...]], axis=0).astype(F32)
        change = layer_norm(halo, gain) - center

        def mix(index):
            return (center + change * mixing_ref[index : index + 1, :]).astype(BF16)

        for index, w_ref in enumerate((w_r_ref, w_k_ref, w_v_ref)):
            edges_ref[index] = mm(mix(index), w_ref[...])
        log_decay, rate = gates(
            mix(3), mix(4), d_base[...], w_d2[...], c_base[...], w_c2[...], w_d1[...], w_c1[...]
        )
        edges_ref[3] = log_decay
        edges_ref[4] = rate
    arrived(copies)
    edge_row = d * (rows - 1)
    at_edge = ids_of((rows, width), 0) == edge_row
    order = (ids_of((rows, rows), 0) - ids_of((rows, rows), 1)) * (1 - 2 * d)
    strict, inclusive = order > 0, order >= 0
    same = block_ones(width)
    ones = same.astype(F32).astype(BF16)
    lane_head = ids_of((1, width), 1) // HEAD
    tri = inclusive.astype(F32).astype(BF16)

    def of_heads(value):
        return masked_heads(value, lane_head, heads)

    def group(s, carry):
        def lane(index, buf):
            return jnp.where(at_edge, edges_ref[index, pl.ds(d * strands + s, 1), :], buf[s])

        receptance, key, value = lane(0, r_buf), lane(1, k_buf), lane(2, v_buf)
        log_decay, rate = lane(3, d_buf), lane(4, a_buf)
        unit = key * lax.rsqrt(head_sum(key * key, ones) + UNIT_EPS)
        high, low = halves(log_decay)
        totals = mm(tri, high) + mm(tri, low)
        middle = totals[rows // 2 : rows // 2 + 1]
        final = jnp.where(d == 0, totals[rows - 1 : rows], totals[0:1])
        there = jnp.exp(middle - totals)
        left_prev = -unit * jnp.exp(totals - log_decay - middle)
        left_here = receptance * jnp.exp(totals - middle)
        right_insert = rate * unit * there
        right_key = key * there
        from_start = jnp.exp(middle)
        to_end = jnp.exp(final - middle)
        left = left_prev.astype(BF16)
        insert_pulls, key_pulls = [], []
        for h in range(heads):
            mask = lane_head == h
            right = jnp.concatenate(
                [jnp.where(mask, right_insert, 0.0), jnp.where(mask, right_key, 0.0)], axis=0
            ).astype(BF16)
            scores = mm_rows(left, right)
            insert_pulls.append(jnp.where(strict, scores[:, :rows], 0.0))
            key_pulls.append(jnp.where(strict, scores[:, rows:], 0.0).astype(BF16))
        value_pull = mm(jnp.concatenate(key_pulls, axis=1), of_heads(value))
        inverses = inverse_of(insert_pulls, rows)
        inverse = jnp.concatenate([item.astype(BF16) for item in inverses], axis=1)
        local_pull = mm(inverse, of_heads(value_pull)).astype(BF16)
        start_pull = mm(inverse, of_heads(left_prev * from_start)).astype(BF16)
        value = value.astype(BF16)
        here_ref[s] = left_here.astype(BF16)
        insert_ref[s] = right_insert.astype(BF16)
        key_ref[s] = right_key.astype(BF16)
        value_ref[s] = value
        pull_ref[s] = local_pull
        start_ref[s] = start_pull
        read_ref[s] = (left_here * from_start).astype(BF16)
        tail_insert = (right_insert * to_end).astype(BF16)
        tail_key = (right_key * to_end).astype(BF16)
        ends = mm_cols(tail_insert, local_pull) + mm_cols(tail_key, value)
        maps = mm_cols(tail_insert, start_pull)
        ends = jnp.where(same, ends, 0.0)
        maps = jnp.where(same, maps, 0.0)
        end = sum(ends[h * HEAD : (h + 1) * HEAD] for h in range(heads))
        across = sum(maps[h * HEAD : (h + 1) * HEAD] for h in range(heads))
        diagonal = ids_of((HEAD, width), 0) == ids_of((HEAD, width), 1) % HEAD
        across = across + jnp.where(diagonal, jnp.exp(final), 0.0)
        state_ref[s] = jnp.concatenate([end, across], axis=0).astype(BF16)
        return carry

    lax.fori_loop(0, strands, group, 0)


def read_kernel(*refs):
    direction_ref, refs = refs[0], refs[1:]
    roles, (local_ref, map_ref) = (refs[:7], refs[7:14]), refs[14:]
    strands, rows, width = roles[0][0].shape
    heads = width // HEAD
    lane_head = ids_of((1, width), 1) // HEAD
    for role, (here_ref, insert_ref, key_ref, value_ref, pull_ref, start_ref, read_ref) in enumerate(roles):
        sign = (1 - 2 * direction_ref[0]) * (1 - 2 * role)
        inclusive = (ids_of((rows, rows), 0) - ids_of((rows, rows), 1)) * sign >= 0

        def group(s, carry):
            here, insert, key = here_ref[s], insert_ref[s], key_ref[s]
            reads = []
            for source in (insert, key):
                scores = mm_rows(here, masked_heads(source, lane_head, heads))
                parts = [scores[:, h * rows : (h + 1) * rows] for h in range(heads)]
                reads.append(jnp.concatenate([jnp.where(inclusive, p, 0.0).astype(BF16) for p in parts], axis=1))
            pull, start, value = [
                masked_heads(ref[s], lane_head, heads) for ref in (pull_ref, start_ref, value_ref)
            ]
            g = role * strands + s
            local_ref[g] = mm(reads[0], pull) + mm(reads[1], value)
            map_ref[g] = (read_ref[s].astype(F32) + mm(reads[0], start)).astype(BF16)
            return carry

        lax.fori_loop(0, strands, group, 0)


def composed(later, earlier, same_head, state_only=False):
    across = later[HEAD:].astype(BF16)
    state = mm(across, spread(earlier[:HEAD].astype(BF16), same_head)) + later[:HEAD].astype(F32)
    if state_only:
        return state
    return jnp.concatenate([state, mm(across, spread(earlier[HEAD:].astype(BF16), same_head))], axis=0)


def window_of(received, same_head, state_only):
    total = received[-1].astype(F32)
    for item in reversed(received[:-1]):
        total = composed(item, total, same_head, state_only)
    return total


def pair_kernel(keep_ref, from_ref, pair_ref, state_ref):
    same_head = block_ones(keep_ref.shape[2])
    for s in range(keep_ref.shape[0]):
        pair = composed(keep_ref[s], from_ref[s], same_head).astype(BF16)
        pair_ref[s] = pair
        state_ref[s] = pair[:HEAD]


def advance_kernel(has_window, *refs):
    *ins, window_ref, current_ref, state_ref = refs
    same_head = block_ones(ins[0].shape[2])
    for s in range(ins[0].shape[0]):
        parts = [ref[s] for ref in ins]
        window = window_of(parts[1 + int(has_window) :], same_head, False)
        current = composed(parts[0], window, same_head).astype(BF16)
        current_ref[s] = current
        state_ref[s] = current[:HEAD]
        if has_window:
            window = composed(parts[1], window, same_head)
        window_ref[s] = window


def entry_kernel(has_window, *refs):
    *ins, entry_ref = refs
    same_head = block_ones(entry_ref.shape[2])
    for s in range(entry_ref.shape[0]):
        parts = [ref[s] for ref in ins]
        entry = window_of(parts[int(has_window) :], same_head, True)[:HEAD]
        if has_window:
            entry = composed(parts[0], entry, same_head, True)
        entry_ref[s] = entry.astype(BF16)


def finish_kernel(entry_ref, from_ref, other_ref, local_ref, map_ref, gain_ref, out_ref):
    strands, _, width = out_ref.shape
    same_head = block_ones(width)
    ones = same_head.astype(F32).astype(BF16)
    gain = gain_ref[...]
    for s in range(strands):
        kept = composed(from_ref[s], entry_ref[s], same_head, True).astype(BF16)
        joined = 0.0
        for role, state in enumerate((other_ref[s], kept)):
            g = role * strands + s
            wkv = local_ref[g] + mm(map_ref[g], spread(state, same_head))
            centered = wkv - head_sum(wkv, ones) * (1.0 / HEAD)
            variance = head_sum(centered * centered, ones) * (1.0 / HEAD)
            joined = joined + centered * lax.rsqrt(variance + GROUP_EPS)
        out_ref[s] = (joined * gain).astype(BF16)


def mix_kernel(index_ref, joined_ref, x_ref, w_ref, gain_ref, up_hbm, down_hbm, own_ref, *rest):
    *sent_refs, partial, total, up_ref, down_ref, sems = rest
    copies = copied((up_hbm, down_hbm), (up_ref, down_ref), sems)
    strands, rows, _ = x_ref.shape
    width = own_ref.shape[1]
    gain = gain_ref[...]
    joined = jnp.concatenate([joined_ref[s] for s in range(strands)], axis=0)
    attention = mm(joined, w_ref[...])
    residuals = [x_ref[s].astype(F32) + attention[s * rows : (s + 1) * rows] for s in range(strands)]
    inner = jnp.concatenate([layer_norm(item, gain).astype(BF16) for item in residuals], axis=0)
    copies[0].wait()
    active = jnp.square(jnp.maximum(mm(inner, up_ref[...]), 0.0)).astype(BF16).astype(F32)
    added = sum(active[s * rows : (s + 1) * rows] for s in range(strands)).astype(BF16)
    copies[1].wait()
    partial[...] = mm(added, down_ref[...])
    total[...] = sum(residuals)

    def part(ref, which):
        return ref[:, pl.ds(pl.multiple_of(which * width, width), width)]

    me = index_ref[0]
    own_ref[...] = part(total, me) + part(partial, me)
    size = len(sent_refs) + 1
    for step, ref in enumerate(sent_refs):
        ref[...] = part(partial, lax.rem(me + step + 1, size)).astype(BF16)


def call(kernel, out_shape, scratch=(), **kwargs):
    return pl.pallas_call(
        kernel,
        out_shape=out_shape,
        scratch_shapes=list(scratch),
        compiler_params=pltpu.CompilerParams(vmem_limit_bytes=VMEM_BYTES),
        **kwargs,
    )


def shifted(value, axis, distance):
    devices = range(lax.axis_size(axis))
    return lax.ppermute(value, axis, [(i, i + distance) for i in devices if i + distance in devices])


def on_device(
    ids,
    hidden_fwd,
    hidden_rc,
    embed,
    ln1_gain,
    ln2_gain,
    mixing,
    w_receptance,
    w_key,
    w_value,
    decay_first_weight,
    decay_base,
    decay_second_weight,
    context_rate_first_weight,
    iclr_base,
    context_rate_second_weight,
    group_gain,
    w_output,
    ffn_key,
    ffn_value,
):
    rows, width = hidden_fwd.shape
    seq_count, mp_count = lax.axis_size("seq"), lax.axis_size("mp")
    strands, full = 2, ffn_key.shape[0]
    struct = jax.ShapeDtypeStruct

    mirror = [(i, seq_count - 1 - i) for i in range(seq_count)]
    rc_here = lax.ppermute(hidden_rc, "seq", mirror)
    firsts = (ids.reshape(1, rows), hidden_fwd, rc_here, embed)
    local = call(
        strands_kernel,
        struct((strands, rows, width), BF16),
        scratch=[pltpu.VMEM(item.shape, item.dtype) for item in firsts] + [pltpu.SemaphoreType.DMA((4,))],
        in_specs=[ANY_SPEC] * 4,
    )(*firsts)
    whole = lax.all_gather(local, "mp", axis=2, tiled=True)
    before = shifted(whole[:, rows - 1], "seq", 1)
    after = shifted(whole[:, 0], "seq", -1)
    w_output_whole = lax.all_gather(w_output, "mp", axis=0, tiled=True)

    groups = 2 * strands
    f32_lanes, bf16_lanes = struct((groups, rows, width), F32), struct((strands, rows, width), BF16)
    state_struct = struct((strands, 2 * HEAD, width), BF16)
    entry_struct = struct((strands, HEAD, width), BF16)
    smalls = (
        ln1_gain.reshape(1, full),
        mixing,
        decay_first_weight.T,
        context_rate_first_weight.T,
        decay_base.reshape(1, width),
        decay_second_weight,
        iclr_base.reshape(1, width),
        context_rate_second_weight,
    )
    small_scratch = [pltpu.VMEM(item.shape, item.dtype) for item in smalls] + [pltpu.SemaphoreType.DMA((8,))]
    *lanes, edge = call(
        project_kernel,
        (f32_lanes,) * 5 + (struct((groups, full), F32),),
        scratch=[
            pltpu.VMEM((strands, rows + 16, full), F32),
            pltpu.VMEM((groups * rows, full), BF16),
        ]
        + small_scratch,
        in_specs=[VMEM_SPEC] * 4 + [ANY_SPEC] * 8,
    )(whole, w_receptance, w_key, w_value, *smalls)

    parity = (lax.axis_index("seq") % 2).astype(jnp.int32).reshape(1)
    lane_scratch = [pltpu.VMEM((strands, rows, width), F32)] * 5 + [pltpu.SemaphoreType.DMA((5,))]
    sent, *sent_parts, edges = call(
        functools.partial(chunk_kernel, True),
        (state_struct,) + (bf16_lanes,) * 7 + (struct((5, groups, width), F32),),
        scratch=lane_scratch + small_scratch,
        in_specs=[SMEM_SPEC] + [ANY_SPEC] * 5 + [VMEM_SPEC] * 6 + [ANY_SPEC] * 8,
    )(parity, *lanes, before, after, edge, w_receptance, w_key, w_value, *smalls)
    partner = [(i, i ^ 1) for i in range(seq_count)]
    from_partner = lax.ppermute(sent, "seq", partner)
    kept, *kept_parts = call(
        functools.partial(chunk_kernel, False),
        (state_struct,) + (bf16_lanes,) * 7,
        scratch=lane_scratch,
        in_specs=[SMEM_SPEC] + [ANY_SPEC] * 5 + [VMEM_SPEC],
    )(1 - parity, *lanes, edges)

    def onward(value, pairs):
        route = [(i, i + 2 * pairs if i % 2 else i - 2 * pairs) for i in range(seq_count)]
        return lax.ppermute(value, "seq", [(i, j) for i, j in route if 0 <= j < seq_count])

    current, state = call(pair_kernel, (state_struct, entry_struct))(kept, from_partner)
    window = []
    distance, count = 1, seq_count // 2
    while True:
        steps = [step for step in range(1, RADIX) if step * distance < count]
        last = distance * RADIX >= count
        received = [
            onward(state if last and step == steps[-1] else current, step * distance) for step in steps
        ]
        if last:
            break
        wide, current, state = call(
            functools.partial(advance_kernel, bool(window)),
            (struct(state_struct.shape, F32), state_struct, entry_struct),
        )(current, *window, *received)
        window = [wide]
        distance *= RADIX
    local_out, start_map = call(
        read_kernel,
        (f32_lanes, struct(f32_lanes.shape, BF16)),
        in_specs=[SMEM_SPEC] + [VMEM_SPEC] * 14,
    )(parity, *sent_parts, *kept_parts)
    entry = call(functools.partial(entry_kernel, bool(window)), entry_struct)(*window, *received)
    other = lax.ppermute(entry, "seq", partner)
    joined = call(finish_kernel, bf16_lanes)(
        entry, from_partner, other, local_out, start_map, group_gain.reshape(1, width)
    )
    joined_whole = lax.all_gather(joined, "mp", axis=2, tiled=True)

    position = lax.axis_index("mp").astype(jnp.int32).reshape(1)
    own, *sent = call(
        mix_kernel,
        (struct((rows, width), F32),) + (struct((rows, width), BF16),) * (mp_count - 1),
        scratch=[
            pltpu.VMEM((rows, full), F32),
            pltpu.VMEM((rows, full), F32),
            pltpu.VMEM(ffn_key.shape, BF16),
            pltpu.VMEM(ffn_value.shape, BF16),
            pltpu.SemaphoreType.DMA((2,)),
        ],
        in_specs=[SMEM_SPEC] + [VMEM_SPEC] * 4 + [ANY_SPEC] * 2,
    )(position, joined_whole, whole, w_output_whole, ln2_gain.reshape(1, full), ffn_key, ffn_value)
    merged = own
    for step, item in enumerate(sent):
        pairs = [(i, (i + step + 1) % mp_count) for i in range(mp_count)]
        merged = merged + lax.ppermute(item, "mp", pairs).astype(F32)
    return merged.astype(BF16)


def solution(mesh):
    in_specs = (
        P("seq"),
        P("seq", "mp"),
        P("seq", "mp"),
        P(None, "mp"),
        P(),
        P(),
        P(),
        P(None, "mp"),
        P(None, "mp"),
        P(None, "mp"),
        P(),
        P("mp"),
        P(None, "mp"),
        P(),
        P("mp"),
        P(None, "mp"),
        P("mp"),
        P("mp", None),
        P(None, "mp"),
        P("mp", None),
    )
    out_specs = P("seq", "mp")
    return jax.shard_map(
        on_device, mesh=mesh, in_specs=in_specs, out_specs=out_specs, check_vma=False
    )
```

```python
import functools

import jax
import jax.numpy as jnp
from jax import lax
from jax.experimental import pallas as pl
from jax.experimental.pallas import tpu as pltpu
from jax.sharding import PartitionSpec as P

HEAD = 64
DECAY_SCALE = 0.606531
NORM_EPS = 1e-05
GROUP_EPS = 0.00064
UNIT_EPS = 1e-06
RADIX = 4
F32 = jnp.float32
BF16 = jnp.bfloat16
MIB = 1024 * 1024
VMEM_SPEC = pl.BlockSpec(memory_space=pltpu.VMEM)
SMEM_SPEC = pl.BlockSpec(memory_space=pltpu.SMEM)
HBM_SPEC = pl.BlockSpec(memory_space=pltpu.HBM)


def mm(left, right):
    return jnp.dot(left, right, preferred_element_type=F32)


def mm_rows(left, right):
    return lax.dot_general(left, right, (((1,), (1,)), ((), ())), preferred_element_type=F32)


def mm_cols(left, right):
    return lax.dot_general(left, right, (((0,), (0,)), ((), ())), preferred_element_type=F32)


def halves(value):
    high = value.astype(BF16)
    return high, (value - high.astype(F32)).astype(BF16)


def head_sum(value, ones):
    high, low = halves(value)
    return mm(high, ones) + mm(low, ones)


def ids_of(shape, dim):
    return lax.broadcasted_iota(jnp.int32, shape, dim)


def block_ones(width):
    same = ids_of((width, width), 0) // HEAD == ids_of((width, width), 1) // HEAD
    return same


def spread(packed, same_head):
    tiled = jnp.concatenate([packed] * (packed.shape[1] // HEAD), axis=0)
    return jnp.where(same_head, tiled, jnp.zeros_like(tiled))


def layer_norm(values, gain):
    row_mean = jnp.mean(values, axis=-1, keepdims=True)
    centered = values - row_mean
    variance = jnp.mean(centered * centered, axis=-1, keepdims=True)
    return centered * lax.rsqrt(variance + NORM_EPS) * gain


def strands_kernel(*refs):
    rc_ref, ins, out_ref, locals_, sems = refs[0], refs[1:4], refs[4], refs[5:8], refs[8]
    arrived(copied(ins, locals_, sems))
    ids_ref, fwd_ref, embed_ref = locals_
    rows = fwd_ref.shape[0]
    ids = ids_ref[...]
    letters = ids_of((embed_ref.shape[0], rows), 0)
    embed = embed_ref[...]

    def looked_up(values):
        onehot = (values == letters).astype(F32)
        return lax.dot_general(
            onehot,
            embed,
            (((0,), (0,)), ((), ())),
            precision=lax.Precision.HIGHEST,
            preferred_element_type=F32,
        )

    out_ref[0] = (fwd_ref[...].astype(F32) + looked_up(ids)).astype(BF16)
    flip = (ids_of((rows, rows), 0) + ids_of((rows, rows), 1) == rows - 1).astype(F32)
    turned = mm(flip.astype(BF16), rc_ref[...])
    out_ref[1] = (turned + looked_up(3 - ids)).astype(BF16)


def inverse_of(pulls, rows):
    row_ids, col_ids = ids_of((rows, rows), 0), ids_of((rows, rows), 1)
    eye = (row_ids == col_ids).astype(F32)
    size = 1
    inverses = None
    while size < rows:
        within = (row_ids // (2 * size) == col_ids // (2 * size)) & (row_ids // size != col_ids // size)
        parts = [jnp.where(within, pull, 0.0) for pull in pulls]
        if size == 1:
            inverses = [eye + part for part in parts]
        else:
            lows = [inverse.astype(BF16) for inverse in inverses]
            products = [mm(part.astype(BF16), low).astype(BF16) for part, low in zip(parts, lows)]
            inverses = [inverse + mm(low, product) for inverse, low, product in zip(inverses, lows, products)]
        size *= 2
    return inverses


def copied(sources, targets, sems):
    copies = [pltpu.make_async_copy(src, dst, sems.at[i]) for i, (src, dst) in enumerate(zip(sources, targets))]
    for item in copies:
        item.start()
    return copies


def arrived(copies):
    for item in copies:
        item.wait()


def gates(decay_mix, rate_mix, d_base, w_d2, c_base, w_c2, w_d1, w_c1):
    decay_low = jnp.tanh(mm_rows(decay_mix, w_d1)).astype(BF16)
    log_decay = -DECAY_SCALE * jax.nn.sigmoid(d_base + mm(decay_low, w_d2))
    rate_low = mm_rows(rate_mix, w_c1).astype(BF16)
    return log_decay, jax.nn.sigmoid(c_base + mm(rate_low, w_c2))


def project_kernel(x_ref, *refs):
    params, refs = refs[:11], refs[11:]
    outs, edge_ref = refs[:5], refs[5]
    normed, mixed = refs[6:8]
    locals_, sems = refs[8:19], refs[19]
    gain_ref, mixing_ref, w_r_ref, w_k_ref, w_v_ref, w_d1, w_c1, d_base, w_d2, c_base, w_c2 = locals_
    copies = copied(params, locals_, sems)
    strands, rows, _ = x_ref.shape
    width = w_r_ref.shape[1]
    pad = 8
    arrived(copies[:2])
    gain = gain_ref[...]
    for s in range(strands):
        values = layer_norm(x_ref[s].astype(F32), gain)
        normed[s, pad : pad + rows, :] = values
        normed[s, pad - 1 : pad, :] = jnp.zeros_like(values[:1])
        normed[s, pad + rows : pad + rows + 1, :] = jnp.zeros_like(values[:1])
        edge_ref[s : s + 1, :] = values[:1]
        edge_ref[strands + s : strands + s + 1, :] = values[rows - 1 :]

    def mix(index):
        weight = mixing_ref[index : index + 1, :]
        for s in range(strands):
            center = normed[s, pad : pad + rows, :]
            for d in range(2):
                shift = pad - 1 + 2 * d
                neighbour = normed[s, shift : shift + rows, :]
                start = (d * strands + s) * rows
                mixed[start : start + rows, :] = (center + (neighbour - center) * weight).astype(BF16)
        return mixed[...]

    shape = (2 * strands, rows, width)
    for index, w_ref in enumerate((w_r_ref, w_k_ref, w_v_ref)):
        copies[2 + index].wait()
        outs[index][...] = mm(mix(index), w_ref[...]).reshape(shape)
    arrived(copies[5:])
    log_decay, rate = gates(
        mix(3), mix(4), d_base[...], w_d2[...], c_base[...], w_c2[...], w_d1[...], w_c1[...]
    )
    outs[3][...] = log_decay.reshape(shape)
    outs[4][...] = rate.reshape(shape)


def masked_heads(value, lane_head, heads):
    return jnp.concatenate([jnp.where(lane_head == h, value, 0.0).astype(BF16) for h in range(heads)], axis=0)


def chunk_kernel(first, direction_ref, *refs):
    lanes, refs = refs[:5], refs[5:]
    if first:
        before_ref, after_ref, edge_ref = refs[:3]
        params, refs = refs[3:14], refs[14:]
        state_ref, parts_ref, edges_ref = refs[:3]
        locals_, sems = refs[3:14], refs[14]
    else:
        edges_ref, state_ref, parts_ref = refs
    strands, _, rows, width = parts_ref.shape
    heads = width // HEAD
    d = direction_ref[0]
    if first:
        arrived(copied(params, locals_, sems))
        gain_ref, mixing_ref, w_r_ref, w_k_ref, w_v_ref, w_d1, w_c1, d_base, w_d2, c_base, w_c2 = locals_
        gain = gain_ref[...]
        center = edge_ref[...]
        halo = jnp.concatenate([before_ref[...], after_ref[...]], axis=0).astype(F32)
        change = layer_norm(halo, gain) - center

        def mix(index):
            return (center + change * mixing_ref[index : index + 1, :]).astype(BF16)

        for index, w_ref in enumerate((w_r_ref, w_k_ref, w_v_ref)):
            edges_ref[index] = mm(mix(index), w_ref[...])
        log_decay, rate = gates(
            mix(3), mix(4), d_base[...], w_d2[...], c_base[...], w_c2[...], w_d1[...], w_c1[...]
        )
        edges_ref[3] = log_decay
        edges_ref[4] = rate
    edge_row = d * (rows - 1)
    at_edge = ids_of((rows, width), 0) == edge_row
    order = (ids_of((rows, rows), 0) - ids_of((rows, rows), 1)) * (1 - 2 * d)
    strict, inclusive = order > 0, order >= 0
    same = block_ones(width)
    ones = same.astype(F32).astype(BF16)
    lane_head = ids_of((1, width), 1) // HEAD
    tri = inclusive.astype(F32).astype(BF16)

    def of_heads(value):
        return masked_heads(value, lane_head, heads)

    def group(s, carry):
        g = d * strands + s

        def lane(index, ref):
            return jnp.where(at_edge, edges_ref[index, pl.ds(g, 1), :], ref[g])

        receptance, key, value, log_decay, rate = [lane(index, ref) for index, ref in enumerate(lanes)]
        unit = key * lax.rsqrt(head_sum(key * key, ones) + UNIT_EPS)
        high, low = halves(log_decay)
        totals = mm(tri, high) + mm(tri, low)
        middle = totals[rows // 2 : rows // 2 + 1]
        final = jnp.where(d == 0, totals[rows - 1 : rows], totals[0:1])
        there = jnp.exp(middle - totals)
        left_prev = -unit * jnp.exp(totals - log_decay - middle)
        left_here = receptance * jnp.exp(totals - middle)
        right_insert = rate * unit * there
        right_key = key * there
        from_start = jnp.exp(middle)
        to_end = jnp.exp(final - middle)
        left = left_prev.astype(BF16)
        insert_pulls, key_pulls = [], []
        for h in range(heads):
            mask = lane_head == h
            right = jnp.concatenate(
                [jnp.where(mask, right_insert, 0.0), jnp.where(mask, right_key, 0.0)], axis=0
            ).astype(BF16)
            scores = mm_rows(left, right)
            insert_pulls.append(jnp.where(strict, scores[:, :rows], 0.0))
            key_pulls.append(jnp.where(strict, scores[:, rows:], 0.0).astype(BF16))
        value_pull = mm(jnp.concatenate(key_pulls, axis=1), of_heads(value))
        inverses = inverse_of(insert_pulls, rows)
        inverse = jnp.concatenate([item.astype(BF16) for item in inverses], axis=1)
        local_pull = mm(inverse, of_heads(value_pull)).astype(BF16)
        start_pull = mm(inverse, of_heads(left_prev * from_start)).astype(BF16)
        value = value.astype(BF16)
        parts_ref[s, 0] = left_here.astype(BF16)
        parts_ref[s, 1] = right_insert.astype(BF16)
        parts_ref[s, 2] = right_key.astype(BF16)
        parts_ref[s, 3] = value
        parts_ref[s, 4] = local_pull
        parts_ref[s, 5] = start_pull
        parts_ref[s, 6] = (left_here * from_start).astype(BF16)
        tail_insert = (right_insert * to_end).astype(BF16)
        tail_key = (right_key * to_end).astype(BF16)
        ends = mm_cols(tail_insert, local_pull) + mm_cols(tail_key, value)
        maps = mm_cols(tail_insert, start_pull)
        ends = jnp.where(same, ends, 0.0)
        maps = jnp.where(same, maps, 0.0)
        end = sum(ends[h * HEAD : (h + 1) * HEAD] for h in range(heads))
        across = sum(maps[h * HEAD : (h + 1) * HEAD] for h in range(heads))
        diagonal = ids_of((HEAD, width), 0) == ids_of((HEAD, width), 1) % HEAD
        across = across + jnp.where(diagonal, jnp.exp(final), 0.0)
        state_ref[s] = jnp.concatenate([end, across], axis=0).astype(BF16)
        return carry

    lax.fori_loop(0, strands, group, 0)


def read_kernel(direction_ref, sent_ref, kept_ref, local_ref, map_ref):
    strands, _, rows, width = sent_ref.shape
    heads = width // HEAD
    lane_head = ids_of((1, width), 1) // HEAD
    for role, parts_ref in enumerate((sent_ref, kept_ref)):
        sign = (1 - 2 * direction_ref[0]) * (1 - 2 * role)
        inclusive = (ids_of((rows, rows), 0) - ids_of((rows, rows), 1)) * sign >= 0

        def group(s, carry):
            here, insert, key, value, pull, start, read = [parts_ref[s, i] for i in range(7)]
            reads = []
            for source in (insert, key):
                scores = mm_rows(here, masked_heads(source, lane_head, heads))
                parts = [scores[:, h * rows : (h + 1) * rows] for h in range(heads)]
                reads.append(jnp.concatenate([jnp.where(inclusive, p, 0.0).astype(BF16) for p in parts], axis=1))
            pull, start, value = [
                masked_heads(item, lane_head, heads) for item in (pull, start, value)
            ]
            g = role * strands + s
            local_ref[g] = mm(reads[0], pull) + mm(reads[1], value)
            map_ref[g] = (read.astype(F32) + mm(reads[0], start)).astype(BF16)
            return carry

        lax.fori_loop(0, strands, group, 0)


def composed(later, earlier, same_head, state_only=False):
    across = later[HEAD:].astype(BF16)
    state = mm(across, spread(earlier[:HEAD].astype(BF16), same_head)) + later[:HEAD].astype(F32)
    if state_only:
        return state
    return jnp.concatenate([state, mm(across, spread(earlier[HEAD:].astype(BF16), same_head))], axis=0)


def window_of(received, same_head, state_only):
    total = received[-1].astype(F32)
    for item in reversed(received[:-1]):
        total = composed(item, total, same_head, state_only)
    return total


def pair_kernel(keep_ref, from_ref, pair_ref, state_ref):
    same_head = block_ones(keep_ref.shape[2])
    for s in range(keep_ref.shape[0]):
        pair = composed(keep_ref[s], from_ref[s], same_head).astype(BF16)
        pair_ref[s] = pair
        state_ref[s] = pair[:HEAD]


def advance_kernel(has_window, *refs):
    *ins, window_ref, current_ref, state_ref = refs
    same_head = block_ones(ins[0].shape[2])
    for s in range(ins[0].shape[0]):
        parts = [ref[s] for ref in ins]
        window = window_of(parts[1 + int(has_window) :], same_head, False)
        current = composed(parts[0], window, same_head).astype(BF16)
        current_ref[s] = current
        state_ref[s] = current[:HEAD]
        if has_window:
            window = composed(parts[1], window, same_head)
        window_ref[s] = window


def entry_kernel(has_window, *refs):
    *ins, entry_ref = refs
    same_head = block_ones(entry_ref.shape[2])
    for s in range(entry_ref.shape[0]):
        parts = [ref[s] for ref in ins]
        entry = window_of(parts[int(has_window) :], same_head, True)[:HEAD]
        if has_window:
            entry = composed(parts[0], entry, same_head, True)
        entry_ref[s] = entry.astype(BF16)


def finish_kernel(entry_ref, from_ref, other_ref, local_ref, map_ref, gain_ref, out_ref):
    strands, _, width = out_ref.shape
    same_head = block_ones(width)
    ones = same_head.astype(F32).astype(BF16)
    gain = gain_ref[...]
    for s in range(strands):
        kept = composed(from_ref[s], entry_ref[s], same_head, True).astype(BF16)
        joined = 0.0
        for role, state in enumerate((other_ref[s], kept)):
            g = role * strands + s
            wkv = local_ref[g] + mm(map_ref[g], spread(state, same_head))
            centered = wkv - head_sum(wkv, ones) * (1.0 / HEAD)
            variance = head_sum(centered * centered, ones) * (1.0 / HEAD)
            joined = joined + centered * lax.rsqrt(variance + GROUP_EPS)
        out_ref[s] = (joined * gain).astype(BF16)


def mix_kernel(index_ref, joined_ref, x_ref, w_ref, gain_ref, up_hbm, down_hbm, own_ref, *rest):
    *sent_refs, partial, total, up_ref, down_ref, sems = rest
    copies = copied((up_hbm, down_hbm), (up_ref, down_ref), sems)
    strands, rows, _ = x_ref.shape
    width = own_ref.shape[1]
    gain = gain_ref[...]
    joined = jnp.concatenate([joined_ref[s] for s in range(strands)], axis=0)
    attention = mm(joined, w_ref[...])
    residuals = [x_ref[s].astype(F32) + attention[s * rows : (s + 1) * rows] for s in range(strands)]
    inner = jnp.concatenate([layer_norm(item, gain).astype(BF16) for item in residuals], axis=0)
    copies[0].wait()
    active = jnp.square(jnp.maximum(mm(inner, up_ref[...]), 0.0)).astype(BF16).astype(F32)
    added = sum(active[s * rows : (s + 1) * rows] for s in range(strands)).astype(BF16)
    copies[1].wait()
    partial[...] = mm(added, down_ref[...])
    total[...] = sum(residuals)

    def part(ref, which):
        return ref[:, pl.ds(pl.multiple_of(which * width, width), width)]

    me = index_ref[0]
    own_ref[...] = part(total, me) + part(partial, me)
    size = len(sent_refs) + 1
    for step, ref in enumerate(sent_refs):
        ref[...] = part(partial, lax.rem(me + step + 1, size)).astype(BF16)


def call(kernel, out_shape, scratch=(), mib=12, **kwargs):
    return pl.pallas_call(
        kernel,
        out_shape=out_shape,
        scratch_shapes=list(scratch),
        compiler_params=pltpu.CompilerParams(vmem_limit_bytes=mib * MIB),
        **kwargs,
    )


def shifted(value, axis, distance):
    devices = range(lax.axis_size(axis))
    return lax.ppermute(value, axis, [(i, i + distance) for i in devices if i + distance in devices])


def on_device(
    ids,
    hidden_fwd,
    hidden_rc,
    embed,
    ln1_gain,
    ln2_gain,
    mixing,
    w_receptance,
    w_key,
    w_value,
    decay_first_weight,
    decay_base,
    decay_second_weight,
    context_rate_first_weight,
    iclr_base,
    context_rate_second_weight,
    group_gain,
    w_output,
    ffn_key,
    ffn_value,
):
    rows, width = hidden_fwd.shape
    seq_count, mp_count = lax.axis_size("seq"), lax.axis_size("mp")
    strands, full = 2, ffn_key.shape[0]
    struct = jax.ShapeDtypeStruct

    mirror = [(i, seq_count - 1 - i) for i in range(seq_count)]
    rc_here = lax.ppermute(hidden_rc, "seq", mirror)
    firsts = (ids.reshape(1, rows), hidden_fwd, embed)
    local = call(
        strands_kernel,
        struct((strands, rows, width), BF16),
        scratch=[pltpu.VMEM(item.shape, item.dtype) for item in firsts] + [pltpu.SemaphoreType.DMA((3,))],
        in_specs=[VMEM_SPEC] + [HBM_SPEC] * 3,
    )(rc_here, *firsts)
    whole = lax.all_gather(local, "mp", axis=2, tiled=True)
    before = shifted(whole[:, rows - 1], "seq", 1)
    after = shifted(whole[:, 0], "seq", -1)
    w_output, _ = lax.optimization_barrier((w_output, whole))
    w_output_whole = lax.all_gather(w_output, "mp", axis=0, tiled=True)

    groups = 2 * strands
    f32_lanes, bf16_lanes = struct((groups, rows, width), F32), struct((strands, rows, width), BF16)
    parts_struct = struct((strands, 7, rows, width), BF16)
    state_struct = struct((strands, 2 * HEAD, width), BF16)
    entry_struct = struct((strands, HEAD, width), BF16)
    params = (
        ln1_gain.reshape(1, full),
        mixing,
        w_receptance,
        w_key,
        w_value,
        decay_first_weight.T,
        context_rate_first_weight.T,
        decay_base.reshape(1, width),
        decay_second_weight,
        iclr_base.reshape(1, width),
        context_rate_second_weight,
    )
    param_scratch = [pltpu.VMEM(item.shape, item.dtype) for item in params]
    param_scratch += [pltpu.SemaphoreType.DMA((len(params),))]
    *lanes, edge = call(
        project_kernel,
        (f32_lanes,) * 5 + (struct((groups, full), F32),),
        scratch=[
            pltpu.VMEM((strands, rows + 16, full), F32),
            pltpu.VMEM((groups * rows, full), BF16),
        ]
        + param_scratch,
        in_specs=[VMEM_SPEC] + [HBM_SPEC] * len(params),
    )(whole, *params)

    parity = (lax.axis_index("seq") % 2).astype(jnp.int32).reshape(1)
    sent, sent_parts, edges = call(
        functools.partial(chunk_kernel, True),
        (state_struct, parts_struct, struct((5, groups, width), F32)),
        scratch=param_scratch,
        in_specs=[SMEM_SPEC] + [VMEM_SPEC] * 8 + [HBM_SPEC] * len(params),
    )(parity, *lanes, before, after, edge, *params)
    partner = [(i, i ^ 1) for i in range(seq_count)]
    from_partner = lax.ppermute(sent, "seq", partner)
    kept, kept_parts = call(
        functools.partial(chunk_kernel, False),
        (state_struct, parts_struct),
        in_specs=[SMEM_SPEC] + [VMEM_SPEC] * 6,
    )(1 - parity, *lanes, edges)

    def onward(value, pairs):
        route = [(i, i + 2 * pairs if i % 2 else i - 2 * pairs) for i in range(seq_count)]
        return lax.ppermute(value, "seq", [(i, j) for i, j in route if 0 <= j < seq_count])

    current, state = call(pair_kernel, (state_struct, entry_struct))(kept, from_partner)
    window = []
    distance, count = 1, seq_count // 2
    while True:
        steps = [step for step in range(1, RADIX) if step * distance < count]
        last = distance * RADIX >= count
        received = [
            onward(state if last and step == steps[-1] else current, step * distance) for step in steps
        ]
        if last:
            break
        wide, current, state = call(
            functools.partial(advance_kernel, bool(window)),
            (struct(state_struct.shape, F32), state_struct, entry_struct),
        )(current, *window, *received)
        window = [wide]
        distance *= RADIX
    local_out, start_map = call(
        read_kernel,
        (f32_lanes, struct(f32_lanes.shape, BF16)),
        in_specs=[SMEM_SPEC] + [VMEM_SPEC] * 2,
    )(parity, sent_parts, kept_parts)
    received, local_out, start_map = lax.optimization_barrier((received, local_out, start_map))
    entry = call(functools.partial(entry_kernel, bool(window)), entry_struct)(*window, *received)
    other = lax.ppermute(entry, "seq", partner)
    joined = call(finish_kernel, bf16_lanes)(
        entry, from_partner, other, local_out, start_map, group_gain.reshape(1, width)
    )
    joined_whole = lax.all_gather(joined, "mp", axis=2, tiled=True)

    position = lax.axis_index("mp").astype(jnp.int32).reshape(1)
    own, *sent = call(
        mix_kernel,
        (struct((rows, width), F32),) + (struct((rows, width), BF16),) * (mp_count - 1),
        scratch=[
            pltpu.VMEM((rows, full), F32),
            pltpu.VMEM((rows, full), F32),
            pltpu.VMEM(ffn_key.shape, BF16),
            pltpu.VMEM(ffn_value.shape, BF16),
            pltpu.SemaphoreType.DMA((2,)),
        ],
        mib=24,
        in_specs=[SMEM_SPEC] + [VMEM_SPEC] * 4 + [HBM_SPEC] * 2,
    )(position, joined_whole, whole, w_output_whole, ln2_gain.reshape(1, full), ffn_key, ffn_value)
    merged = own
    for step, item in enumerate(sent):
        pairs = [(i, (i + step + 1) % mp_count) for i in range(mp_count)]
        merged = merged + lax.ppermute(item, "mp", pairs).astype(F32)
    return merged.astype(BF16)


def solution(mesh):
    in_specs = (
        P("seq"),
        P("seq", "mp"),
        P("seq", "mp"),
        P(None, "mp"),
        P(),
        P(),
        P(),
        P(None, "mp"),
        P(None, "mp"),
        P(None, "mp"),
        P(),
        P("mp"),
        P(None, "mp"),
        P(),
        P("mp"),
        P(None, "mp"),
        P("mp"),
        P("mp", None),
        P(None, "mp"),
        P("mp", None),
    )
    out_specs = P("seq", "mp")
    return jax.shard_map(
        on_device, mesh=mesh, in_specs=in_specs, out_specs=out_specs, check_vma=False
    )
```

```python
import functools

import jax
import jax.numpy as jnp
from jax import lax
from jax.experimental import pallas as pl
from jax.experimental.pallas import tpu as pltpu
from jax.sharding import PartitionSpec as P

HEAD = 64
DECAY_SCALE = 0.606531
NORM_EPS = 1e-05
GROUP_EPS = 0.00064
UNIT_EPS = 1e-06
RADIX = 4
F32 = jnp.float32
BF16 = jnp.bfloat16
MIB = 1024 * 1024
VMEM_SPEC = pl.BlockSpec(memory_space=pltpu.VMEM)
SMEM_SPEC = pl.BlockSpec(memory_space=pltpu.SMEM)


def mm(left, right):
    return jnp.dot(left, right, preferred_element_type=F32)


def mm_rows(left, right):
    return lax.dot_general(left, right, (((1,), (1,)), ((), ())), preferred_element_type=F32)


def mm_cols(left, right):
    return lax.dot_general(left, right, (((0,), (0,)), ((), ())), preferred_element_type=F32)


def halves(value):
    high = value.astype(BF16)
    return high, (value - high.astype(F32)).astype(BF16)


def head_sum(value, ones):
    high, low = halves(value)
    return mm(high, ones) + mm(low, ones)


def ids_of(shape, dim):
    return lax.broadcasted_iota(jnp.int32, shape, dim)


def block_ones(width):
    same = ids_of((width, width), 0) // HEAD == ids_of((width, width), 1) // HEAD
    return same


def spread(packed, same_head):
    tiled = jnp.concatenate([packed] * (packed.shape[1] // HEAD), axis=0)
    return jnp.where(same_head, tiled, jnp.zeros_like(tiled))


def layer_norm(values, gain):
    row_mean = jnp.mean(values, axis=-1, keepdims=True)
    centered = values - row_mean
    variance = jnp.mean(centered * centered, axis=-1, keepdims=True)
    return centered * lax.rsqrt(variance + NORM_EPS) * gain


def embed_kernel(ids_ref, fwd_ref, embed_ref, strand_ref, other_ref):
    rows = fwd_ref.shape[0]
    ids = ids_ref[...]
    letters = ids_of((embed_ref.shape[0], rows), 0)
    embed = embed_ref[...]

    def looked_up(values):
        onehot = (values == letters).astype(F32)
        return lax.dot_general(
            onehot,
            embed,
            (((0,), (0,)), ((), ())),
            precision=lax.Precision.HIGHEST,
            preferred_element_type=F32,
        )

    strand_ref[...] = (fwd_ref[...].astype(F32) + looked_up(ids)).astype(BF16)
    other_ref[...] = looked_up(3 - ids)


def strands_kernel(rc_ref, strand_ref, other_ref, out_ref):
    rows = rc_ref.shape[0]
    out_ref[0] = strand_ref[...]
    flip = (ids_of((rows, rows), 0) + ids_of((rows, rows), 1) == rows - 1).astype(F32)
    out_ref[1] = (mm(flip.astype(BF16), rc_ref[...]) + other_ref[...]).astype(BF16)


def inverse_of(pulls, rows):
    row_ids, col_ids = ids_of((rows, rows), 0), ids_of((rows, rows), 1)
    eye = (row_ids == col_ids).astype(F32)
    size = 1
    inverses = None
    while size < rows:
        within = (row_ids // (2 * size) == col_ids // (2 * size)) & (row_ids // size != col_ids // size)
        parts = [jnp.where(within, pull, 0.0) for pull in pulls]
        if size == 1:
            inverses = [eye + part for part in parts]
        else:
            lows = [inverse.astype(BF16) for inverse in inverses]
            products = [mm(part.astype(BF16), low).astype(BF16) for part, low in zip(parts, lows)]
            inverses = [inverse + mm(low, product) for inverse, low, product in zip(inverses, lows, products)]
        size *= 2
    return inverses


def project_all(mix, params):
    w_r, w_k, w_v, w_d1, w_c1, w_d2, w_c2, d_base, c_base = params
    for index, weight in enumerate((w_r, w_k, w_v)):
        yield mm(mix(index), weight[...])
    decay_low = jnp.tanh(mm_rows(mix(3), w_d1[...])).astype(BF16)
    yield -DECAY_SCALE * jax.nn.sigmoid(d_base[...] + mm(decay_low, w_d2[...]))
    rate_low = mm_rows(mix(4), w_c1[...]).astype(BF16)
    yield jax.nn.sigmoid(c_base[...] + mm(rate_low, w_c2[...]))


def project_kernel(x_ref, *refs):
    (gain_ref, mixing_ref), params = refs[:2], refs[2:11]
    outs, edge_ref, (normed, mixed) = refs[11:16], refs[16], refs[17:]
    strands, rows, _ = x_ref.shape
    width = outs[0].shape[2]
    pad = 8
    gain = gain_ref[...]
    for s in range(strands):
        values = layer_norm(x_ref[s].astype(F32), gain)
        normed[s, pad : pad + rows, :] = values
        normed[s, pad - 1 : pad, :] = jnp.zeros_like(values[:1])
        normed[s, pad + rows : pad + rows + 1, :] = jnp.zeros_like(values[:1])
        edge_ref[s : s + 1, :] = values[:1]
        edge_ref[strands + s : strands + s + 1, :] = values[rows - 1 :]

    def mix(index):
        weight = mixing_ref[index : index + 1, :]
        for s in range(strands):
            center = normed[s, pad : pad + rows, :]
            for d in range(2):
                shift = pad - 1 + 2 * d
                neighbour = normed[s, shift : shift + rows, :]
                start = (d * strands + s) * rows
                mixed[start : start + rows, :] = (center + (neighbour - center) * weight).astype(BF16)
        return mixed[...]

    shape = (2 * strands, rows, width)
    for out_ref, result in zip(outs, project_all(mix, params)):
        out_ref[...] = result.reshape(shape)


def masked_heads(value, lane_head, heads):
    return jnp.concatenate([jnp.where(lane_head == h, value, 0.0).astype(BF16) for h in range(heads)], axis=0)


def chunk_kernel(first, direction_ref, *refs):
    lanes, refs = refs[:5], refs[5:]
    if first:
        before_ref, after_ref, edge_ref, gain_ref, mixing_ref, *params, state_ref, parts_ref, edges_ref = refs
    else:
        edges_ref, state_ref, parts_ref = refs
    strands, _, rows, width = parts_ref.shape
    heads = width // HEAD
    d = direction_ref[0]
    if first:
        center = edge_ref[...]
        halo = jnp.concatenate([before_ref[...], after_ref[...]], axis=0).astype(F32)
        change = layer_norm(halo, gain_ref[...]) - center

        def mix(index):
            return (center + change * mixing_ref[index : index + 1, :]).astype(BF16)

        for index, result in enumerate(project_all(mix, params)):
            edges_ref[index] = result
    edge_row = d * (rows - 1)
    at_edge = ids_of((rows, width), 0) == edge_row
    order = (ids_of((rows, rows), 0) - ids_of((rows, rows), 1)) * (1 - 2 * d)
    strict, inclusive = order > 0, order >= 0
    same = block_ones(width)
    ones = same.astype(F32).astype(BF16)
    lane_head = ids_of((1, width), 1) // HEAD
    tri = inclusive.astype(F32).astype(BF16)

    def of_heads(value):
        return masked_heads(value, lane_head, heads)

    def group(s, carry):
        g = d * strands + s

        def lane(index, ref):
            return jnp.where(at_edge, edges_ref[index, pl.ds(g, 1), :], ref[g])

        receptance, key, value, log_decay, rate = [lane(index, ref) for index, ref in enumerate(lanes)]
        unit = key * lax.rsqrt(head_sum(key * key, ones) + UNIT_EPS)
        high, low = halves(log_decay)
        totals = mm(tri, high) + mm(tri, low)
        middle = totals[rows // 2 : rows // 2 + 1]
        final = jnp.where(d == 0, totals[rows - 1 : rows], totals[0:1])
        there = jnp.exp(middle - totals)
        left_prev = -unit * jnp.exp(totals - log_decay - middle)
        left_here = receptance * jnp.exp(totals - middle)
        right_insert = rate * unit * there
        right_key = key * there
        from_start = jnp.exp(middle)
        to_end = jnp.exp(final - middle)
        left = left_prev.astype(BF16)
        insert_pulls, key_pulls = [], []
        for h in range(heads):
            mask = lane_head == h
            right = jnp.concatenate(
                [jnp.where(mask, right_insert, 0.0), jnp.where(mask, right_key, 0.0)], axis=0
            ).astype(BF16)
            scores = mm_rows(left, right)
            insert_pulls.append(jnp.where(strict, scores[:, :rows], 0.0))
            key_pulls.append(jnp.where(strict, scores[:, rows:], 0.0).astype(BF16))
        value_pull = mm(jnp.concatenate(key_pulls, axis=1), of_heads(value))
        inverses = inverse_of(insert_pulls, rows)
        inverse = jnp.concatenate([item.astype(BF16) for item in inverses], axis=1)
        local_pull = mm(inverse, of_heads(value_pull)).astype(BF16)
        start_pull = mm(inverse, of_heads(left_prev * from_start)).astype(BF16)
        value = value.astype(BF16)
        parts_ref[s, 0] = left_here.astype(BF16)
        parts_ref[s, 1] = right_insert.astype(BF16)
        parts_ref[s, 2] = right_key.astype(BF16)
        parts_ref[s, 3] = value
        parts_ref[s, 4] = local_pull
        parts_ref[s, 5] = start_pull
        parts_ref[s, 6] = (left_here * from_start).astype(BF16)
        tail_insert = (right_insert * to_end).astype(BF16)
        tail_key = (right_key * to_end).astype(BF16)
        ends = mm_cols(tail_insert, local_pull) + mm_cols(tail_key, value)
        maps = mm_cols(tail_insert, start_pull)
        ends = jnp.where(same, ends, 0.0)
        maps = jnp.where(same, maps, 0.0)
        end = sum(ends[h * HEAD : (h + 1) * HEAD] for h in range(heads))
        across = sum(maps[h * HEAD : (h + 1) * HEAD] for h in range(heads))
        diagonal = ids_of((HEAD, width), 0) == ids_of((HEAD, width), 1) % HEAD
        across = across + jnp.where(diagonal, jnp.exp(final), 0.0)
        state_ref[s] = jnp.concatenate([end, across], axis=0).astype(BF16)
        return carry

    lax.fori_loop(0, strands, group, 0)


def read_kernel(direction_ref, sent_ref, kept_ref, local_ref, map_ref):
    strands, _, rows, width = sent_ref.shape
    heads = width // HEAD
    lane_head = ids_of((1, width), 1) // HEAD
    for role, parts_ref in enumerate((sent_ref, kept_ref)):
        sign = (1 - 2 * direction_ref[0]) * (1 - 2 * role)
        inclusive = (ids_of((rows, rows), 0) - ids_of((rows, rows), 1)) * sign >= 0

        def group(s, carry):
            here, insert, key, value, pull, start, read = [parts_ref[s, i] for i in range(7)]
            reads = []
            for source in (insert, key):
                scores = mm_rows(here, masked_heads(source, lane_head, heads))
                parts = [scores[:, h * rows : (h + 1) * rows] for h in range(heads)]
                reads.append(jnp.concatenate([jnp.where(inclusive, p, 0.0).astype(BF16) for p in parts], axis=1))
            pull, start, value = [
                masked_heads(item, lane_head, heads) for item in (pull, start, value)
            ]
            g = role * strands + s
            local_ref[g] = mm(reads[0], pull) + mm(reads[1], value)
            map_ref[g] = (read.astype(F32) + mm(reads[0], start)).astype(BF16)
            return carry

        lax.fori_loop(0, strands, group, 0)


def composed(later, earlier, same_head, state_only=False):
    across = later[HEAD:].astype(BF16)
    state = mm(across, spread(earlier[:HEAD].astype(BF16), same_head)) + later[:HEAD].astype(F32)
    if state_only:
        return state
    return jnp.concatenate([state, mm(across, spread(earlier[HEAD:].astype(BF16), same_head))], axis=0)


def window_of(received, same_head, state_only):
    total = received[-1].astype(F32)
    for item in reversed(received[:-1]):
        total = composed(item, total, same_head, state_only)
    return total


def pair_kernel(keep_ref, from_ref, pair_ref, state_ref):
    same_head = block_ones(keep_ref.shape[2])
    for s in range(keep_ref.shape[0]):
        pair = composed(keep_ref[s], from_ref[s], same_head).astype(BF16)
        pair_ref[s] = pair
        state_ref[s] = pair[:HEAD]


def advance_kernel(has_window, *refs):
    *ins, window_ref, current_ref, state_ref = refs
    same_head = block_ones(ins[0].shape[2])
    for s in range(ins[0].shape[0]):
        parts = [ref[s] for ref in ins]
        window = window_of(parts[1 + int(has_window) :], same_head, False)
        current = composed(parts[0], window, same_head).astype(BF16)
        current_ref[s] = current
        state_ref[s] = current[:HEAD]
        if has_window:
            window = composed(parts[1], window, same_head)
        window_ref[s] = window


def entry_kernel(has_window, *refs):
    *ins, entry_ref = refs
    same_head = block_ones(entry_ref.shape[2])
    for s in range(entry_ref.shape[0]):
        parts = [ref[s] for ref in ins]
        entry = window_of(parts[int(has_window) :], same_head, True)[:HEAD]
        if has_window:
            entry = composed(parts[0], entry, same_head, True)
        entry_ref[s] = entry.astype(BF16)


def finish_kernel(entry_ref, from_ref, other_ref, local_ref, map_ref, gain_ref, out_ref):
    strands, _, width = out_ref.shape
    same_head = block_ones(width)
    ones = same_head.astype(F32).astype(BF16)
    gain = gain_ref[...]
    for s in range(strands):
        kept = composed(from_ref[s], entry_ref[s], same_head, True).astype(BF16)
        joined = 0.0
        for role, state in enumerate((other_ref[s], kept)):
            g = role * strands + s
            wkv = local_ref[g] + mm(map_ref[g], spread(state, same_head))
            centered = wkv - head_sum(wkv, ones) * (1.0 / HEAD)
            variance = head_sum(centered * centered, ones) * (1.0 / HEAD)
            joined = joined + centered * lax.rsqrt(variance + GROUP_EPS)
        out_ref[s] = (joined * gain).astype(BF16)


def mix_kernel(index_ref, joined_ref, x_ref, w_ref, up_ref, down_ref, gain_ref, own_ref, *rest):
    *sent_refs, partial, total = rest
    strands, rows, _ = x_ref.shape
    width = own_ref.shape[1]
    gain = gain_ref[...]
    joined = jnp.concatenate([joined_ref[s] for s in range(strands)], axis=0)
    attention = mm(joined, w_ref[...])
    residuals = [x_ref[s].astype(F32) + attention[s * rows : (s + 1) * rows] for s in range(strands)]
    inner = jnp.concatenate([layer_norm(item, gain).astype(BF16) for item in residuals], axis=0)
    active = jnp.square(jnp.maximum(mm(inner, up_ref[...]), 0.0)).astype(BF16).astype(F32)
    added = sum(active[s * rows : (s + 1) * rows] for s in range(strands)).astype(BF16)
    partial[...] = mm(added, down_ref[...])
    total[...] = sum(residuals)

    def part(ref, which):
        return ref[:, pl.ds(pl.multiple_of(which * width, width), width)]

    me = index_ref[0]
    own_ref[...] = part(total, me) + part(partial, me)
    size = len(sent_refs) + 1
    for step, ref in enumerate(sent_refs):
        ref[...] = part(partial, lax.rem(me + step + 1, size)).astype(BF16)


def call(kernel, out_shape, scratch=(), mib=12, us=2, **kwargs):
    return pl.pallas_call(
        kernel,
        out_shape=out_shape,
        scratch_shapes=list(scratch),
        cost_estimate=pl.CostEstimate(flops=us * 10**9, bytes_accessed=us * 10**6, transcendentals=0),
        compiler_params=pltpu.CompilerParams(vmem_limit_bytes=mib * MIB),
        **kwargs,
    )


def shifted(value, axis, distance):
    devices = range(lax.axis_size(axis))
    return lax.ppermute(value, axis, [(i, i + distance) for i in devices if i + distance in devices])


def on_device(
    ids,
    hidden_fwd,
    hidden_rc,
    embed,
    ln1_gain,
    ln2_gain,
    mixing,
    w_receptance,
    w_key,
    w_value,
    decay_first_weight,
    decay_base,
    decay_second_weight,
    context_rate_first_weight,
    iclr_base,
    context_rate_second_weight,
    group_gain,
    w_output,
    ffn_key,
    ffn_value,
):
    rows, width = hidden_fwd.shape
    seq_count, mp_count = lax.axis_size("seq"), lax.axis_size("mp")
    strands, full = 2, ffn_key.shape[0]
    struct = jax.ShapeDtypeStruct

    mirror = [(i, seq_count - 1 - i) for i in range(seq_count)]
    rc_here = lax.ppermute(hidden_rc, "seq", mirror)
    params = (
        ln1_gain.reshape(1, full),
        mixing,
        w_receptance,
        w_key,
        w_value,
        decay_first_weight.T,
        context_rate_first_weight.T,
        decay_second_weight,
        context_rate_second_weight,
        decay_base.reshape(1, width),
        iclr_base.reshape(1, width),
    )
    strand, other = call(
        embed_kernel, (struct((rows, width), BF16), struct((rows, width), F32)), us=10
    )(ids.reshape(1, rows), hidden_fwd, embed)
    rc_here, strand, other = lax.optimization_barrier((rc_here, strand, other))
    local = call(strands_kernel, struct((strands, rows, width), BF16), us=10)(rc_here, strand, other)
    whole = lax.all_gather(local, "mp", axis=2, tiled=True)
    before = shifted(whole[:, rows - 1], "seq", 1)
    after = shifted(whole[:, 0], "seq", -1)
    w_output, _ = lax.optimization_barrier((w_output, whole))
    w_output_whole = lax.all_gather(w_output, "mp", axis=0, tiled=True)

    groups = 2 * strands
    f32_lanes, bf16_lanes = struct((groups, rows, width), F32), struct((strands, rows, width), BF16)
    parts_struct = struct((strands, 7, rows, width), BF16)
    state_struct = struct((strands, 2 * HEAD, width), BF16)
    entry_struct = struct((strands, HEAD, width), BF16)
    *lanes, edge = call(
        project_kernel,
        (f32_lanes,) * 5 + (struct((groups, full), F32),),
        scratch=[
            pltpu.VMEM((strands, rows + 16, full), F32),
            pltpu.VMEM((groups * rows, full), BF16),
        ],
    )(whole, *params)

    parity = (lax.axis_index("seq") % 2).astype(jnp.int32).reshape(1)
    sent, sent_parts, edges = call(
        functools.partial(chunk_kernel, True),
        (state_struct, parts_struct, struct((5, groups, width), F32)),
        in_specs=[SMEM_SPEC] + [VMEM_SPEC] * (8 + len(params)),
    )(parity, *lanes, before, after, edge, *params)
    partner = [(i, i ^ 1) for i in range(seq_count)]
    from_partner = lax.ppermute(sent, "seq", partner)
    kept, kept_parts = call(
        functools.partial(chunk_kernel, False),
        (state_struct, parts_struct),
        in_specs=[SMEM_SPEC] + [VMEM_SPEC] * 6,
    )(1 - parity, *lanes, edges)

    def onward(value, pairs):
        route = [(i, i + 2 * pairs if i % 2 else i - 2 * pairs) for i in range(seq_count)]
        return lax.ppermute(value, "seq", [(i, j) for i, j in route if 0 <= j < seq_count])

    current, state = call(pair_kernel, (state_struct, entry_struct))(kept, from_partner)
    window = []
    distance, count = 1, seq_count // 2
    while True:
        steps = [step for step in range(1, RADIX) if step * distance < count]
        last = distance * RADIX >= count
        received = [
            onward(state if last and step == steps[-1] else current, step * distance) for step in steps
        ]
        if last:
            break
        wide, current, state = call(
            functools.partial(advance_kernel, bool(window)),
            (struct(state_struct.shape, F32), state_struct, entry_struct),
        )(current, *window, *received)
        window = [wide]
        distance *= RADIX
    sent_parts, kept_parts, _ = lax.optimization_barrier((sent_parts, kept_parts, current))
    local_out, start_map = call(
        read_kernel,
        (f32_lanes, struct(f32_lanes.shape, BF16)),
        in_specs=[SMEM_SPEC] + [VMEM_SPEC] * 2,
    )(parity, sent_parts, kept_parts)
    received, local_out, start_map, w_output_whole = lax.optimization_barrier(
        (received, local_out, start_map, w_output_whole)
    )
    entry = call(functools.partial(entry_kernel, bool(window)), entry_struct)(*window, *received)
    other = lax.ppermute(entry, "seq", partner)
    joined = call(finish_kernel, bf16_lanes)(
        entry, from_partner, other, local_out, start_map, group_gain.reshape(1, width)
    )
    joined_whole = lax.all_gather(joined, "mp", axis=2, tiled=True)

    position = lax.axis_index("mp").astype(jnp.int32).reshape(1)
    own, *sent = call(
        mix_kernel,
        (struct((rows, width), F32),) + (struct((rows, width), BF16),) * (mp_count - 1),
        scratch=[
            pltpu.VMEM((rows, full), F32),
            pltpu.VMEM((rows, full), F32),
        ],
        mib=24,
        in_specs=[SMEM_SPEC] + [VMEM_SPEC] * 6,
    )(position, joined_whole, whole, w_output_whole, ffn_key, ffn_value, ln2_gain.reshape(1, full))
    merged = own
    for step, item in enumerate(sent):
        pairs = [(i, (i + step + 1) % mp_count) for i in range(mp_count)]
        merged = merged + lax.ppermute(item, "mp", pairs).astype(F32)
    return merged.astype(BF16)


def solution(mesh):
    in_specs = (
        P("seq"),
        P("seq", "mp"),
        P("seq", "mp"),
        P(None, "mp"),
        P(),
        P(),
        P(),
        P(None, "mp"),
        P(None, "mp"),
        P(None, "mp"),
        P(),
        P("mp"),
        P(None, "mp"),
        P(),
        P("mp"),
        P(None, "mp"),
        P("mp"),
        P("mp", None),
        P(None, "mp"),
        P("mp", None),
    )
    out_specs = P("seq", "mp")
    return jax.shard_map(
        on_device, mesh=mesh, in_specs=in_specs, out_specs=out_specs, check_vma=False
    )
```

```python
import functools

import jax
import jax.numpy as jnp
from jax import lax
from jax.experimental import pallas as pl
from jax.experimental.pallas import tpu as pltpu
from jax.sharding import PartitionSpec as P

HEAD = 64
DECAY_SCALE = 0.606531
NORM_EPS = 1e-05
GROUP_EPS = 0.00064
UNIT_EPS = 1e-06
RADIX = 4
F32 = jnp.float32
BF16 = jnp.bfloat16
MIB = 1024 * 1024
VMEM_SPEC = pl.BlockSpec(memory_space=pltpu.VMEM)
SMEM_SPEC = pl.BlockSpec(memory_space=pltpu.SMEM)


def mm(left, right):
    return jnp.dot(left, right, preferred_element_type=F32)


def mm_rows(left, right):
    return lax.dot_general(left, right, (((1,), (1,)), ((), ())), preferred_element_type=F32)


def mm_cols(left, right):
    return lax.dot_general(left, right, (((0,), (0,)), ((), ())), preferred_element_type=F32)


def halves(value):
    high = value.astype(BF16)
    return high, (value - high.astype(F32)).astype(BF16)


def head_sum(value, ones):
    high, low = halves(value)
    return mm(high, ones) + mm(low, ones)


def ids_of(shape, dim):
    return lax.broadcasted_iota(jnp.int32, shape, dim)


def block_ones(width):
    same = ids_of((width, width), 0) // HEAD == ids_of((width, width), 1) // HEAD
    return same


def spread(packed, same_head):
    tiled = jnp.concatenate([packed] * (packed.shape[1] // HEAD), axis=0)
    return jnp.where(same_head, tiled, jnp.zeros_like(tiled))


def layer_norm(values, gain):
    row_mean = jnp.mean(values, axis=-1, keepdims=True)
    centered = values - row_mean
    variance = jnp.mean(centered * centered, axis=-1, keepdims=True)
    return centered * lax.rsqrt(variance + NORM_EPS) * gain


def embed_kernel(ids_ref, fwd_ref, embed_ref, strand_ref, other_ref):
    rows = fwd_ref.shape[0]
    ids = ids_ref[...]
    letters = ids_of((embed_ref.shape[0], rows), 0)
    embed = embed_ref[...]

    def looked_up(values):
        onehot = (values == letters).astype(F32)
        return lax.dot_general(
            onehot,
            embed,
            (((0,), (0,)), ((), ())),
            precision=lax.Precision.HIGHEST,
            preferred_element_type=F32,
        )

    strand_ref[...] = (fwd_ref[...].astype(F32) + looked_up(ids)).astype(BF16)
    other_ref[...] = looked_up(3 - ids)


def strands_kernel(rc_ref, strand_ref, other_ref, out_ref):
    rows = rc_ref.shape[0]
    out_ref[0] = strand_ref[...]
    flip = (ids_of((rows, rows), 0) + ids_of((rows, rows), 1) == rows - 1).astype(F32)
    out_ref[1] = (mm(flip.astype(BF16), rc_ref[...]) + other_ref[...]).astype(BF16)


def inverse_of(pulls, rows):
    row_ids, col_ids = ids_of((rows, rows), 0), ids_of((rows, rows), 1)
    eye = (row_ids == col_ids).astype(F32)
    size = 1
    inverses = None
    while size < rows:
        within = (row_ids // (2 * size) == col_ids // (2 * size)) & (row_ids // size != col_ids // size)
        parts = [jnp.where(within, pull, 0.0) for pull in pulls]
        if size == 1:
            inverses = [eye + part for part in parts]
        else:
            lows = [inverse.astype(BF16) for inverse in inverses]
            products = [mm(part.astype(BF16), low).astype(BF16) for part, low in zip(parts, lows)]
            inverses = [inverse + mm(low, product) for inverse, low, product in zip(inverses, lows, products)]
        size *= 2
    return inverses


def project_all(mix, params):
    w_r, w_k, w_v, w_d1, w_c1, w_d2, w_c2, d_base, c_base = params
    for index, weight in enumerate((w_r, w_k, w_v)):
        yield mm(mix(index), weight[...])
    decay_low = jnp.tanh(mm_rows(mix(3), w_d1[...])).astype(BF16)
    yield -DECAY_SCALE * jax.nn.sigmoid(d_base[...] + mm(decay_low, w_d2[...]))
    rate_low = mm_rows(mix(4), w_c1[...]).astype(BF16)
    yield jax.nn.sigmoid(c_base[...] + mm(rate_low, w_c2[...]))


def project_kernel(x_ref, *refs):
    (gain_ref, mixing_ref), params = refs[:2], refs[2:11]
    outs, edge_ref, (normed, mixed) = refs[11:16], refs[16], refs[17:]
    strands, rows, _ = x_ref.shape
    width = outs[0].shape[2]
    pad = 8
    gain = gain_ref[...]
    for s in range(strands):
        values = layer_norm(x_ref[s].astype(F32), gain)
        normed[s, pad : pad + rows, :] = values
        normed[s, pad - 1 : pad, :] = jnp.zeros_like(values[:1])
        normed[s, pad + rows : pad + rows + 1, :] = jnp.zeros_like(values[:1])
        edge_ref[s : s + 1, :] = values[:1]
        edge_ref[strands + s : strands + s + 1, :] = values[rows - 1 :]

    def mix(index):
        weight = mixing_ref[index : index + 1, :]
        for s in range(strands):
            center = normed[s, pad : pad + rows, :]
            for d in range(2):
                shift = pad - 1 + 2 * d
                neighbour = normed[s, shift : shift + rows, :]
                start = (d * strands + s) * rows
                mixed[start : start + rows, :] = (center + (neighbour - center) * weight).astype(BF16)
        return mixed[...]

    shape = (2 * strands, rows, width)
    for out_ref, result in zip(outs, project_all(mix, params)):
        out_ref[...] = result.reshape(shape)


def masked_heads(value, lane_head, heads):
    return jnp.concatenate([jnp.where(lane_head == h, value, 0.0).astype(BF16) for h in range(heads)], axis=0)


def chunk_kernel(first, direction_ref, *refs):
    lanes, refs = refs[:5], refs[5:]
    if first:
        before_ref, after_ref, edge_ref, gain_ref, mixing_ref, *params, state_ref, parts_ref, edges_ref = refs
    else:
        edges_ref, state_ref, parts_ref = refs
    strands, _, rows, width = parts_ref.shape
    heads = width // HEAD
    d = direction_ref[0]
    if first:
        center = edge_ref[...]
        halo = jnp.concatenate([before_ref[...], after_ref[...]], axis=0).astype(F32)
        change = layer_norm(halo, gain_ref[...]) - center

        def mix(index):
            return (center + change * mixing_ref[index : index + 1, :]).astype(BF16)

        for index, result in enumerate(project_all(mix, params)):
            edges_ref[index] = result
    edge_row = d * (rows - 1)
    at_edge = ids_of((rows, width), 0) == edge_row
    order = (ids_of((rows, rows), 0) - ids_of((rows, rows), 1)) * (1 - 2 * d)
    strict, inclusive = order > 0, order >= 0
    same = block_ones(width)
    ones = same.astype(F32).astype(BF16)
    lane_head = ids_of((1, width), 1) // HEAD
    tri = inclusive.astype(F32).astype(BF16)

    def of_heads(value):
        return masked_heads(value, lane_head, heads)

    def prepared(s):
        g = d * strands + s

        def lane(index, ref):
            return jnp.where(at_edge, edges_ref[index, pl.ds(g, 1), :], ref[g])

        receptance, key, value, log_decay, rate = [lane(index, ref) for index, ref in enumerate(lanes)]
        unit = key * lax.rsqrt(head_sum(key * key, ones) + UNIT_EPS)
        high, low = halves(log_decay)
        totals = mm(tri, high) + mm(tri, low)
        middle = totals[rows // 2 : rows // 2 + 1]
        final = jnp.where(d == 0, totals[rows - 1 : rows], totals[0:1])
        there = jnp.exp(middle - totals)
        left_prev = -unit * jnp.exp(totals - log_decay - middle)
        left_here = receptance * jnp.exp(totals - middle)
        right_insert = rate * unit * there
        right_key = key * there
        from_start = jnp.exp(middle)
        to_end = jnp.exp(final - middle)
        left = left_prev.astype(BF16)
        insert_pulls, key_pulls = [], []
        for h in range(heads):
            mask = lane_head == h
            right = jnp.concatenate(
                [jnp.where(mask, right_insert, 0.0), jnp.where(mask, right_key, 0.0)], axis=0
            ).astype(BF16)
            scores = mm_rows(left, right)
            insert_pulls.append(jnp.where(strict, scores[:, :rows], 0.0))
            key_pulls.append(jnp.where(strict, scores[:, rows:], 0.0).astype(BF16))
        value_pull = mm(jnp.concatenate(key_pulls, axis=1), of_heads(value))
        value = value.astype(BF16)
        parts_ref[s, 0] = left_here.astype(BF16)
        parts_ref[s, 1] = right_insert.astype(BF16)
        parts_ref[s, 2] = right_key.astype(BF16)
        parts_ref[s, 3] = value
        parts_ref[s, 6] = (left_here * from_start).astype(BF16)
        tail_insert = (right_insert * to_end).astype(BF16)
        tail_key = (right_key * to_end).astype(BF16)
        solved_for = jnp.concatenate([of_heads(value_pull), of_heads(left_prev * from_start)], axis=1)
        end = mm_cols(tail_key, value)
        return insert_pulls, (solved_for, tail_insert, end, jnp.exp(final))

    prepared_all = [prepared(s) for s in range(strands)]
    inverses = inverse_of([pull for pulls, _ in prepared_all for pull in pulls], rows)
    for s, (_, (solved_for, tail_insert, end, kept)) in enumerate(prepared_all):
        own = inverses[s * heads : (s + 1) * heads]
        inverse = jnp.concatenate([item.astype(BF16) for item in own], axis=1)
        solved = mm(inverse, solved_for).astype(BF16)
        parts_ref[s, 4] = solved[:, :width]
        parts_ref[s, 5] = solved[:, width:]
        added = mm_cols(tail_insert, solved)
        ends = jnp.where(same, end + added[:, :width], 0.0)
        maps = jnp.where(same, added[:, width:], 0.0)
        end = sum(ends[h * HEAD : (h + 1) * HEAD] for h in range(heads))
        across = sum(maps[h * HEAD : (h + 1) * HEAD] for h in range(heads))
        diagonal = ids_of((HEAD, width), 0) == ids_of((HEAD, width), 1) % HEAD
        across = across + jnp.where(diagonal, kept, 0.0)
        state_ref[s] = jnp.concatenate([end, across], axis=0).astype(BF16)


def read_kernel(direction_ref, sent_ref, kept_ref, local_ref, map_ref):
    strands, _, rows, width = sent_ref.shape
    heads = width // HEAD
    lane_head = ids_of((1, width), 1) // HEAD
    for role, parts_ref in enumerate((sent_ref, kept_ref)):
        sign = (1 - 2 * direction_ref[0]) * (1 - 2 * role)
        inclusive = (ids_of((rows, rows), 0) - ids_of((rows, rows), 1)) * sign >= 0

        def group(s, carry):
            here, insert, key, value, pull, start, read = [parts_ref[s, i] for i in range(7)]
            reads = []
            for source in (insert, key):
                scores = mm_rows(here, masked_heads(source, lane_head, heads))
                parts = [scores[:, h * rows : (h + 1) * rows] for h in range(heads)]
                reads.append(jnp.concatenate([jnp.where(inclusive, p, 0.0).astype(BF16) for p in parts], axis=1))
            pull, start, value = [
                masked_heads(item, lane_head, heads) for item in (pull, start, value)
            ]
            g = role * strands + s
            local_ref[g] = mm(reads[0], pull) + mm(reads[1], value)
            map_ref[g] = (read.astype(F32) + mm(reads[0], start)).astype(BF16)
            return carry

        lax.fori_loop(0, strands, group, 0)


def composed(later, earlier, same_head, state_only=False):
    across = later[HEAD:].astype(BF16)
    state = mm(across, spread(earlier[:HEAD].astype(BF16), same_head)) + later[:HEAD].astype(F32)
    if state_only:
        return state
    return jnp.concatenate([state, mm(across, spread(earlier[HEAD:].astype(BF16), same_head))], axis=0)


def window_of(received, same_head, state_only):
    total = received[-1].astype(F32)
    for item in reversed(received[:-1]):
        total = composed(item, total, same_head, state_only)
    return total


def pair_kernel(keep_ref, from_ref, pair_ref, state_ref):
    same_head = block_ones(keep_ref.shape[2])
    for s in range(keep_ref.shape[0]):
        pair = composed(keep_ref[s], from_ref[s], same_head).astype(BF16)
        pair_ref[s] = pair
        state_ref[s] = pair[:HEAD]


def advance_kernel(has_window, *refs):
    *ins, window_ref, current_ref, state_ref = refs
    same_head = block_ones(ins[0].shape[2])
    for s in range(ins[0].shape[0]):
        parts = [ref[s] for ref in ins]
        window = window_of(parts[1 + int(has_window) :], same_head, False)
        current = composed(parts[0], window, same_head).astype(BF16)
        current_ref[s] = current
        state_ref[s] = current[:HEAD]
        if has_window:
            window = composed(parts[1], window, same_head)
        window_ref[s] = window


def entry_kernel(has_window, *refs):
    *ins, entry_ref = refs
    same_head = block_ones(entry_ref.shape[2])
    for s in range(entry_ref.shape[0]):
        parts = [ref[s] for ref in ins]
        entry = window_of(parts[int(has_window) :], same_head, True)[:HEAD]
        if has_window:
            entry = composed(parts[0], entry, same_head, True)
        entry_ref[s] = entry.astype(BF16)


def finish_kernel(entry_ref, from_ref, other_ref, local_ref, map_ref, gain_ref, out_ref):
    strands, _, width = out_ref.shape
    same_head = block_ones(width)
    ones = same_head.astype(F32).astype(BF16)
    gain = gain_ref[...]
    for s in range(strands):
        kept = composed(from_ref[s], entry_ref[s], same_head, True).astype(BF16)
        joined = 0.0
        for role, state in enumerate((other_ref[s], kept)):
            g = role * strands + s
            wkv = local_ref[g] + mm(map_ref[g], spread(state, same_head))
            centered = wkv - head_sum(wkv, ones) * (1.0 / HEAD)
            variance = head_sum(centered * centered, ones) * (1.0 / HEAD)
            joined = joined + centered * lax.rsqrt(variance + GROUP_EPS)
        out_ref[s] = (joined * gain).astype(BF16)


def mix_kernel(index_ref, joined_ref, x_ref, w_ref, up_ref, down_ref, gain_ref, own_ref, *rest):
    *sent_refs, partial, total = rest
    strands, rows, _ = x_ref.shape
    width = own_ref.shape[1]
    gain = gain_ref[...]
    joined = jnp.concatenate([joined_ref[s] for s in range(strands)], axis=0)
    attention = mm(joined, w_ref[...])
    residuals = [x_ref[s].astype(F32) + attention[s * rows : (s + 1) * rows] for s in range(strands)]
    inner = jnp.concatenate([layer_norm(item, gain).astype(BF16) for item in residuals], axis=0)
    active = jnp.square(jnp.maximum(mm(inner, up_ref[...]), 0.0)).astype(BF16).astype(F32)
    added = sum(active[s * rows : (s + 1) * rows] for s in range(strands)).astype(BF16)
    partial[...] = mm(added, down_ref[...])
    total[...] = sum(residuals)

    def part(ref, which):
        return ref[:, pl.ds(pl.multiple_of(which * width, width), width)]

    me = index_ref[0]
    own_ref[...] = part(total, me) + part(partial, me)
    size = len(sent_refs) + 1
    for step, ref in enumerate(sent_refs):
        ref[...] = part(partial, lax.rem(me + step + 1, size)).astype(BF16)


def call(kernel, out_shape, scratch=(), mib=12, us=2, **kwargs):
    return pl.pallas_call(
        kernel,
        out_shape=out_shape,
        scratch_shapes=list(scratch),
        cost_estimate=pl.CostEstimate(flops=us * 10**9, bytes_accessed=us * 10**6, transcendentals=0),
        compiler_params=pltpu.CompilerParams(vmem_limit_bytes=mib * MIB),
        **kwargs,
    )


def shifted(value, axis, distance):
    devices = range(lax.axis_size(axis))
    return lax.ppermute(value, axis, [(i, i + distance) for i in devices if i + distance in devices])


def on_device(
    ids,
    hidden_fwd,
    hidden_rc,
    embed,
    ln1_gain,
    ln2_gain,
    mixing,
    w_receptance,
    w_key,
    w_value,
    decay_first_weight,
    decay_base,
    decay_second_weight,
    context_rate_first_weight,
    iclr_base,
    context_rate_second_weight,
    group_gain,
    w_output,
    ffn_key,
    ffn_value,
):
    rows, width = hidden_fwd.shape
    seq_count, mp_count = lax.axis_size("seq"), lax.axis_size("mp")
    strands, full = 2, ffn_key.shape[0]
    struct = jax.ShapeDtypeStruct

    mirror = [(i, seq_count - 1 - i) for i in range(seq_count)]
    rc_here = lax.ppermute(hidden_rc, "seq", mirror)
    params = (
        ln1_gain.reshape(1, full),
        mixing,
        w_receptance,
        w_key,
        w_value,
        decay_first_weight.T,
        context_rate_first_weight.T,
        decay_second_weight,
        context_rate_second_weight,
        decay_base.reshape(1, width),
        iclr_base.reshape(1, width),
    )
    strand, other = call(
        embed_kernel, (struct((rows, width), BF16), struct((rows, width), F32)), us=10
    )(ids.reshape(1, rows), hidden_fwd, embed)
    rc_here, strand, other = lax.optimization_barrier((rc_here, strand, other))
    local = call(strands_kernel, struct((strands, rows, width), BF16), us=10)(rc_here, strand, other)
    whole = lax.all_gather(local, "mp", axis=2, tiled=True)
    before = shifted(whole[:, rows - 1], "seq", 1)
    after = shifted(whole[:, 0], "seq", -1)
    w_output, _ = lax.optimization_barrier((w_output, whole))
    w_output_whole = lax.all_gather(w_output, "mp", axis=0, tiled=True)

    groups = 2 * strands
    f32_lanes, bf16_lanes = struct((groups, rows, width), F32), struct((strands, rows, width), BF16)
    parts_struct = struct((strands, 7, rows, width), BF16)
    state_struct = struct((strands, 2 * HEAD, width), BF16)
    entry_struct = struct((strands, HEAD, width), BF16)
    *lanes, edge = call(
        project_kernel,
        (f32_lanes,) * 5 + (struct((groups, full), F32),),
        scratch=[
            pltpu.VMEM((strands, rows + 16, full), F32),
            pltpu.VMEM((groups * rows, full), BF16),
        ],
    )(whole, *params)

    parity = (lax.axis_index("seq") % 2).astype(jnp.int32).reshape(1)
    sent, sent_parts, edges = call(
        functools.partial(chunk_kernel, True),
        (state_struct, parts_struct, struct((5, groups, width), F32)),
        in_specs=[SMEM_SPEC] + [VMEM_SPEC] * (8 + len(params)),
    )(parity, *lanes, before, after, edge, *params)
    partner = [(i, i ^ 1) for i in range(seq_count)]
    from_partner = lax.ppermute(sent, "seq", partner)
    kept, kept_parts = call(
        functools.partial(chunk_kernel, False),
        (state_struct, parts_struct),
        in_specs=[SMEM_SPEC] + [VMEM_SPEC] * 6,
    )(1 - parity, *lanes, edges)

    def onward(value, pairs):
        route = [(i, i + 2 * pairs if i % 2 else i - 2 * pairs) for i in range(seq_count)]
        return lax.ppermute(value, "seq", [(i, j) for i, j in route if 0 <= j < seq_count])

    current, state = call(pair_kernel, (state_struct, entry_struct))(kept, from_partner)
    window = []
    distance, count = 1, seq_count // 2
    while True:
        steps = [step for step in range(1, RADIX) if step * distance < count]
        last = distance * RADIX >= count
        received = [
            onward(state if last and step == steps[-1] else current, step * distance) for step in steps
        ]
        if last:
            break
        wide, current, state = call(
            functools.partial(advance_kernel, bool(window)),
            (struct(state_struct.shape, F32), state_struct, entry_struct),
        )(current, *window, *received)
        window = [wide]
        distance *= RADIX
    sent_parts, kept_parts, _ = lax.optimization_barrier((sent_parts, kept_parts, current))
    local_out, start_map = call(
        read_kernel,
        (f32_lanes, struct(f32_lanes.shape, BF16)),
        in_specs=[SMEM_SPEC] + [VMEM_SPEC] * 2,
    )(parity, sent_parts, kept_parts)
    received, local_out, start_map, w_output_whole = lax.optimization_barrier(
        (received, local_out, start_map, w_output_whole)
    )
    entry = call(functools.partial(entry_kernel, bool(window)), entry_struct)(*window, *received)
    other = lax.ppermute(entry, "seq", partner)
    joined = call(finish_kernel, bf16_lanes)(
        entry, from_partner, other, local_out, start_map, group_gain.reshape(1, width)
    )
    joined_whole = lax.all_gather(joined, "mp", axis=2, tiled=True)

    position = lax.axis_index("mp").astype(jnp.int32).reshape(1)
    own, *sent = call(
        mix_kernel,
        (struct((rows, width), F32),) + (struct((rows, width), BF16),) * (mp_count - 1),
        scratch=[
            pltpu.VMEM((rows, full), F32),
            pltpu.VMEM((rows, full), F32),
        ],
        mib=24,
        in_specs=[SMEM_SPEC] + [VMEM_SPEC] * 6,
    )(position, joined_whole, whole, w_output_whole, ffn_key, ffn_value, ln2_gain.reshape(1, full))
    merged = own
    for step, item in enumerate(sent):
        pairs = [(i, (i + step + 1) % mp_count) for i in range(mp_count)]
        merged = merged + lax.ppermute(item, "mp", pairs).astype(F32)
    return merged.astype(BF16)


def solution(mesh):
    in_specs = (
        P("seq"),
        P("seq", "mp"),
        P("seq", "mp"),
        P(None, "mp"),
        P(),
        P(),
        P(),
        P(None, "mp"),
        P(None, "mp"),
        P(None, "mp"),
        P(),
        P("mp"),
        P(None, "mp"),
        P(),
        P("mp"),
        P(None, "mp"),
        P("mp"),
        P("mp", None),
        P(None, "mp"),
        P("mp", None),
    )
    out_specs = P("seq", "mp")
    return jax.shard_map(
        on_device, mesh=mesh, in_specs=in_specs, out_specs=out_specs, check_vma=False
    )
```

```python
import functools

import jax
import jax.numpy as jnp
from jax import lax
from jax.experimental import pallas as pl
from jax.experimental.pallas import tpu as pltpu
from jax.sharding import PartitionSpec as P

HEAD = 64
DECAY_SCALE = 0.606531
NORM_EPS = 1e-05
GROUP_EPS = 0.00064
UNIT_EPS = 1e-06
F32 = jnp.float32
BF16 = jnp.bfloat16
MIB = 1024 * 1024
VMEM_SPEC = pl.BlockSpec(memory_space=pltpu.VMEM)
SMEM_SPEC = pl.BlockSpec(memory_space=pltpu.SMEM)


def mm(left, right):
    return jnp.dot(left, right, preferred_element_type=F32)


def mm_rows(left, right):
    return lax.dot_general(left, right, (((1,), (1,)), ((), ())), preferred_element_type=F32)


def mm_cols(left, right):
    return lax.dot_general(left, right, (((0,), (0,)), ((), ())), preferred_element_type=F32)


def halves(value):
    high = value.astype(BF16)
    return high, (value - high.astype(F32)).astype(BF16)


def head_sum(value, ones):
    high, low = halves(value)
    return mm(high, ones) + mm(low, ones)


def ids_of(shape, dim):
    return lax.broadcasted_iota(jnp.int32, shape, dim)


def block_ones(width):
    same = ids_of((width, width), 0) // HEAD == ids_of((width, width), 1) // HEAD
    return same


def spread(packed, same_head):
    tiled = jnp.concatenate([packed] * (packed.shape[1] // HEAD), axis=0)
    return jnp.where(same_head, tiled, jnp.zeros_like(tiled))


def layer_norm(values, gain):
    row_mean = jnp.mean(values, axis=-1, keepdims=True)
    centered = values - row_mean
    variance = jnp.mean(centered * centered, axis=-1, keepdims=True)
    return centered * lax.rsqrt(variance + NORM_EPS) * gain


def embed_kernel(ids_ref, fwd_ref, embed_ref, strand_ref, other_ref):
    rows = fwd_ref.shape[0]
    ids = ids_ref[...]
    letters = ids_of((embed_ref.shape[0], rows), 0)
    embed = embed_ref[...]

    def looked_up(values):
        onehot = (values == letters).astype(F32)
        return lax.dot_general(
            onehot,
            embed,
            (((0,), (0,)), ((), ())),
            precision=lax.Precision.HIGHEST,
            preferred_element_type=F32,
        )

    strand_ref[...] = (fwd_ref[...].astype(F32) + looked_up(ids)).astype(BF16)
    other_ref[...] = looked_up(3 - ids)


def strands_kernel(rc_ref, strand_ref, other_ref, out_ref):
    rows = rc_ref.shape[0]
    out_ref[0] = strand_ref[...]
    flip = (ids_of((rows, rows), 0) + ids_of((rows, rows), 1) == rows - 1).astype(F32)
    out_ref[1] = (mm(flip.astype(BF16), rc_ref[...]) + other_ref[...]).astype(BF16)


def inverse_of(pulls, rows):
    row_ids, col_ids = ids_of((rows, rows), 0), ids_of((rows, rows), 1)
    eye = (row_ids == col_ids).astype(F32)
    size = 1
    inverses = None
    while size < rows:
        within = (row_ids // (2 * size) == col_ids // (2 * size)) & (row_ids // size != col_ids // size)
        parts = [jnp.where(within, pull, 0.0) for pull in pulls]
        if size == 1:
            inverses = [eye + part for part in parts]
        else:
            lows = [inverse.astype(BF16) for inverse in inverses]
            products = [mm(part.astype(BF16), low).astype(BF16) for part, low in zip(parts, lows)]
            inverses = [inverse + mm(low, product) for inverse, low, product in zip(inverses, lows, products)]
        size *= 2
    return inverses


def project_all(mix, params):
    w_r, w_k, w_v, w_d1, w_c1, w_d2, w_c2, d_base, c_base = params
    for index, weight in enumerate((w_r, w_k, w_v)):
        yield mm(mix(index), weight[...])
    decay_low = jnp.tanh(mm_rows(mix(3), w_d1[...])).astype(BF16)
    yield -DECAY_SCALE * jax.nn.sigmoid(d_base[...] + mm(decay_low, w_d2[...]))
    rate_low = mm_rows(mix(4), w_c1[...]).astype(BF16)
    yield jax.nn.sigmoid(c_base[...] + mm(rate_low, w_c2[...]))


def project_kernel(x_ref, *refs):
    (gain_ref, mixing_ref), params = refs[:2], refs[2:11]
    outs, edge_ref, (normed, mixed) = refs[11:16], refs[16], refs[17:]
    strands, rows, _ = x_ref.shape
    width = outs[0].shape[2]
    pad = 8
    gain = gain_ref[...]
    for s in range(strands):
        values = layer_norm(x_ref[s].astype(F32), gain)
        normed[s, pad : pad + rows, :] = values
        normed[s, pad - 1 : pad, :] = jnp.zeros_like(values[:1])
        normed[s, pad + rows : pad + rows + 1, :] = jnp.zeros_like(values[:1])
        edge_ref[s : s + 1, :] = values[:1]
        edge_ref[strands + s : strands + s + 1, :] = values[rows - 1 :]

    def mix(index):
        weight = mixing_ref[index : index + 1, :]
        for s in range(strands):
            center = normed[s, pad : pad + rows, :]
            for d in range(2):
                shift = pad - 1 + 2 * d
                neighbour = normed[s, shift : shift + rows, :]
                start = (d * strands + s) * rows
                mixed[start : start + rows, :] = (center + (neighbour - center) * weight).astype(BF16)
        return mixed[...]

    shape = (2 * strands, rows, width)
    for out_ref, result in zip(outs, project_all(mix, params)):
        out_ref[...] = result.reshape(shape)


def masked_heads(value, lane_head, heads):
    return jnp.concatenate([jnp.where(lane_head == h, value, 0.0).astype(BF16) for h in range(heads)], axis=0)


def chunk_kernel(first, direction_ref, *refs):
    lanes, refs = refs[:5], refs[5:]
    if first:
        partner_ref, beyond_ref, edge_ref, gain_ref, mixing_ref, *params, state_ref, parts_ref, edges_ref = refs
    else:
        edges_ref, state_ref, parts_ref = refs
    strands, _, rows, width = parts_ref.shape
    heads = width // HEAD
    d = direction_ref[0]
    if first:
        center = edge_ref[...]
        near, far = partner_ref[...].astype(F32), beyond_ref[...].astype(F32)
        odd = d == 1
        halo = jnp.concatenate([jnp.where(odd, near, far), jnp.where(odd, far, near)], axis=0)
        change = layer_norm(halo, gain_ref[...]) - center

        def mix(index):
            return (center + change * mixing_ref[index : index + 1, :]).astype(BF16)

        for index, result in enumerate(project_all(mix, params)):
            edges_ref[index] = result
    edge_row = d * (rows - 1)
    at_edge = ids_of((rows, width), 0) == edge_row
    order = (ids_of((rows, rows), 0) - ids_of((rows, rows), 1)) * (1 - 2 * d)
    strict, inclusive = order > 0, order >= 0
    same = block_ones(width)
    ones = same.astype(F32).astype(BF16)
    lane_head = ids_of((1, width), 1) // HEAD
    tri = inclusive.astype(F32).astype(BF16)

    def of_heads(value):
        return masked_heads(value, lane_head, heads)

    def prepared(s):
        g = d * strands + s

        def lane(index, ref):
            return jnp.where(at_edge, edges_ref[index, pl.ds(g, 1), :], ref[g])

        receptance, key, value, log_decay, rate = [lane(index, ref) for index, ref in enumerate(lanes)]
        unit = key * lax.rsqrt(head_sum(key * key, ones) + UNIT_EPS)
        high, low = halves(log_decay)
        totals = mm(tri, high) + mm(tri, low)
        middle = totals[rows // 2 : rows // 2 + 1]
        final = jnp.where(d == 0, totals[rows - 1 : rows], totals[0:1])
        there = jnp.exp(middle - totals)
        left_prev = -unit * jnp.exp(totals - log_decay - middle)
        left_here = receptance * jnp.exp(totals - middle)
        right_insert = rate * unit * there
        right_key = key * there
        from_start = jnp.exp(middle)
        to_end = jnp.exp(final - middle)
        left = left_prev.astype(BF16)
        insert_pulls, key_pulls = [], []
        for h in range(heads):
            mask = lane_head == h
            right = jnp.concatenate(
                [jnp.where(mask, right_insert, 0.0), jnp.where(mask, right_key, 0.0)], axis=0
            ).astype(BF16)
            scores = mm_rows(left, right)
            insert_pulls.append(jnp.where(strict, scores[:, :rows], 0.0))
            key_pulls.append(jnp.where(strict, scores[:, rows:], 0.0).astype(BF16))
        value_pull = mm(jnp.concatenate(key_pulls, axis=1), of_heads(value))
        value = value.astype(BF16)
        parts_ref[s, 0] = left_here.astype(BF16)
        parts_ref[s, 1] = right_insert.astype(BF16)
        parts_ref[s, 2] = right_key.astype(BF16)
        parts_ref[s, 3] = value
        parts_ref[s, 6] = (left_here * from_start).astype(BF16)
        tail_insert = (right_insert * to_end).astype(BF16)
        tail_key = (right_key * to_end).astype(BF16)
        solved_for = jnp.concatenate([of_heads(value_pull), of_heads(left_prev * from_start)], axis=1)
        end = mm_cols(tail_key, value)
        return insert_pulls, (solved_for, tail_insert, end, jnp.exp(final))

    prepared_all = [prepared(s) for s in range(strands)]
    inverses = inverse_of([pull for pulls, _ in prepared_all for pull in pulls], rows)
    for s, (_, (solved_for, tail_insert, end, kept)) in enumerate(prepared_all):
        own = inverses[s * heads : (s + 1) * heads]
        inverse = jnp.concatenate([item.astype(BF16) for item in own], axis=1)
        solved = mm(inverse, solved_for).astype(BF16)
        parts_ref[s, 4] = solved[:, :width]
        parts_ref[s, 5] = solved[:, width:]
        added = mm_cols(tail_insert, solved)
        ends = jnp.where(same, end + added[:, :width], 0.0)
        maps = jnp.where(same, added[:, width:], 0.0)
        end = sum(ends[h * HEAD : (h + 1) * HEAD] for h in range(heads))
        across = sum(maps[h * HEAD : (h + 1) * HEAD] for h in range(heads))
        diagonal = ids_of((HEAD, width), 0) == ids_of((HEAD, width), 1) % HEAD
        across = across + jnp.where(diagonal, kept, 0.0)
        state_ref[s] = jnp.concatenate([end, across], axis=0).astype(BF16)


def read_kernel(direction_ref, sent_ref, kept_ref, local_ref, map_ref):
    strands, _, rows, width = sent_ref.shape
    heads = width // HEAD
    lane_head = ids_of((1, width), 1) // HEAD
    for role, parts_ref in enumerate((sent_ref, kept_ref)):
        sign = (1 - 2 * direction_ref[0]) * (1 - 2 * role)
        inclusive = (ids_of((rows, rows), 0) - ids_of((rows, rows), 1)) * sign >= 0

        def group(s, carry):
            here, insert, key, value, pull, start, read = [parts_ref[s, i] for i in range(7)]
            reads = []
            for source in (insert, key):
                scores = mm_rows(here, masked_heads(source, lane_head, heads))
                parts = [scores[:, h * rows : (h + 1) * rows] for h in range(heads)]
                reads.append(jnp.concatenate([jnp.where(inclusive, p, 0.0).astype(BF16) for p in parts], axis=1))
            pull, start, value = [
                masked_heads(item, lane_head, heads) for item in (pull, start, value)
            ]
            g = role * strands + s
            local_ref[g] = mm(reads[0], pull) + mm(reads[1], value)
            map_ref[g] = (read.astype(F32) + mm(reads[0], start)).astype(BF16)
            return carry

        lax.fori_loop(0, strands, group, 0)


def composed(later, earlier, same_head, state_only=False):
    across = later[HEAD:].astype(BF16)
    state = mm(across, spread(earlier[:HEAD].astype(BF16), same_head)) + later[:HEAD].astype(F32)
    if state_only:
        return state
    return jnp.concatenate([state, mm(across, spread(earlier[HEAD:].astype(BF16), same_head))], axis=0)


def pair_kernel(keep_ref, from_ref, pair_ref, state_ref):
    same_head = block_ones(keep_ref.shape[2])
    for s in range(keep_ref.shape[0]):
        pair = composed(keep_ref[s], from_ref[s], same_head).astype(BF16)
        pair_ref[s] = pair
        state_ref[s] = pair[:HEAD]


def advance_kernel(has_prefix, later_ref, total_ref, from_ref, *refs):
    *prefix_ref, wide_ref, next_ref, state_ref = refs
    same_head = block_ones(total_ref.shape[2])
    later = later_ref[0] == 1
    shape = total_ref.shape[1:]
    within = (ids_of(shape, 0) - HEAD) == ids_of(shape, 1) % HEAD
    for s in range(total_ref.shape[0]):
        own, other = total_ref[s], from_ref[s]
        total = composed(jnp.where(later, own, other), jnp.where(later, other, own), same_head).astype(BF16)
        next_ref[s] = total
        state_ref[s] = total[:HEAD]
        ahead = jnp.where(later, other.astype(F32), within.astype(F32))
        if has_prefix:
            ahead = composed(prefix_ref[0][s], ahead, same_head)
        wide_ref[s] = ahead


def entry_kernel(has_prefix, later_ref, from_ref, *refs):
    *prefix_ref, entry_ref = refs
    same_head = block_ones(entry_ref.shape[2])
    for s in range(entry_ref.shape[0]):
        other = from_ref[s]
        ahead = jnp.where(later_ref[0] == 1, other, jnp.zeros_like(other))
        if has_prefix:
            ahead = composed(prefix_ref[0][s], ahead, same_head, True)
        entry_ref[s] = ahead.astype(BF16)


def finish_kernel(entry_ref, from_ref, other_ref, local_ref, map_ref, gain_ref, out_ref):
    strands, _, width = out_ref.shape
    same_head = block_ones(width)
    ones = same_head.astype(F32).astype(BF16)
    gain = gain_ref[...]
    for s in range(strands):
        kept = composed(from_ref[s], entry_ref[s], same_head, True).astype(BF16)
        joined = 0.0
        for role, state in enumerate((other_ref[s], kept)):
            g = role * strands + s
            wkv = local_ref[g] + mm(map_ref[g], spread(state, same_head))
            centered = wkv - head_sum(wkv, ones) * (1.0 / HEAD)
            variance = head_sum(centered * centered, ones) * (1.0 / HEAD)
            joined = joined + centered * lax.rsqrt(variance + GROUP_EPS)
        out_ref[s] = (joined * gain).astype(BF16)


def mix_kernel(blocks, index_ref, joined_ref, x_ref, *refs):
    w_refs, (up_ref, down_ref, gain_ref, own_ref) = refs[:blocks], refs[blocks : blocks + 4]
    *sent_refs, partial, total = refs[blocks + 4 :]
    strands, rows, _ = x_ref.shape
    width = own_ref.shape[1]
    gain = gain_ref[...]
    me = index_ref[0]
    attention = 0.0
    for step, w_ref in enumerate(w_refs):
        start = pl.multiple_of((me ^ step) * width, width)
        joined = jnp.concatenate([joined_ref[s, :, pl.ds(start, width)] for s in range(strands)], axis=0)
        attention = attention + mm(joined, w_ref[...])
    residuals = [x_ref[s].astype(F32) + attention[s * rows : (s + 1) * rows] for s in range(strands)]
    inner = jnp.concatenate([layer_norm(item, gain).astype(BF16) for item in residuals], axis=0)
    active = jnp.square(jnp.maximum(mm(inner, up_ref[...]), 0.0)).astype(BF16).astype(F32)
    added = sum(active[s * rows : (s + 1) * rows] for s in range(strands)).astype(BF16)
    partial[...] = mm(added, down_ref[...])
    total[...] = sum(residuals)

    def part(ref, which):
        return ref[:, pl.ds(pl.multiple_of(which * width, width), width)]

    own_ref[...] = part(total, me) + part(partial, me)
    for step, ref in enumerate(sent_refs):
        ref[...] = part(partial, me ^ (step + 1)).astype(BF16)


def call(kernel, out_shape, scratch=(), mib=12, us=2, **kwargs):
    return pl.pallas_call(
        kernel,
        out_shape=out_shape,
        scratch_shapes=list(scratch),
        cost_estimate=pl.CostEstimate(flops=us * 10**9, bytes_accessed=us * 10**6, transcendentals=0),
        compiler_params=pltpu.CompilerParams(vmem_limit_bytes=mib * MIB),
        **kwargs,
    )


def swapped(value, axis, mask):
    return lax.ppermute(value, axis, [(i, i ^ mask) for i in range(lax.axis_size(axis))])


def on_device(
    ids,
    hidden_fwd,
    hidden_rc,
    embed,
    ln1_gain,
    ln2_gain,
    mixing,
    w_receptance,
    w_key,
    w_value,
    decay_first_weight,
    decay_base,
    decay_second_weight,
    context_rate_first_weight,
    iclr_base,
    context_rate_second_weight,
    group_gain,
    w_output,
    ffn_key,
    ffn_value,
):
    rows, width = hidden_fwd.shape
    seq_count, mp_count = lax.axis_size("seq"), lax.axis_size("mp")
    strands, full = 2, ffn_key.shape[0]
    struct = jax.ShapeDtypeStruct

    mirror = [(i, seq_count - 1 - i) for i in range(seq_count)]
    rc_here = lax.ppermute(hidden_rc, "seq", mirror)
    params = (
        ln1_gain.reshape(1, full),
        mixing,
        w_receptance,
        w_key,
        w_value,
        decay_first_weight.T,
        context_rate_first_weight.T,
        decay_second_weight,
        context_rate_second_weight,
        decay_base.reshape(1, width),
        iclr_base.reshape(1, width),
    )
    strand, other = call(
        embed_kernel, (struct((rows, width), BF16), struct((rows, width), F32)), us=10
    )(ids.reshape(1, rows), hidden_fwd, embed)
    rc_here, strand, other = lax.optimization_barrier((rc_here, strand, other))
    local = call(strands_kernel, struct((strands, rows, width), BF16), us=10)(rc_here, strand, other)
    whole = lax.all_gather(local, "mp", axis=2, tiled=True)
    place = lax.axis_index("seq").astype(jnp.int32)
    parity = place % 2
    first, last = whole[:, 0], whole[:, rows - 1]
    near = lax.ppermute(jnp.where(parity == 1, first, last), "seq", [(i, i ^ 1) for i in range(seq_count)])
    bridges = [(i, i + 1) for i in range(1, seq_count - 1, 2)]
    bridges += [(j, i) for i, j in bridges]
    far = lax.ppermute(jnp.where(parity == 1, last, first), "seq", bridges)
    parity = parity.reshape(1)
    w_output_held, _ = lax.optimization_barrier((w_output, whole))
    w_across = swapped(w_output_held, "mp", 2)
    w_beside = swapped(w_output_held, "mp", 1)

    groups = 2 * strands
    f32_lanes, bf16_lanes = struct((groups, rows, width), F32), struct((strands, rows, width), BF16)
    parts_struct = struct((strands, 7, rows, width), BF16)
    state_struct = struct((strands, 2 * HEAD, width), BF16)
    entry_struct = struct((strands, HEAD, width), BF16)
    *lanes, edge = call(
        project_kernel,
        (f32_lanes,) * 5 + (struct((groups, full), F32),),
        scratch=[
            pltpu.VMEM((strands, rows + 16, full), F32),
            pltpu.VMEM((groups * rows, full), BF16),
        ],
    )(whole, *params)

    sent, sent_parts, edges = call(
        functools.partial(chunk_kernel, True),
        (state_struct, parts_struct, struct((5, groups, width), F32)),
        in_specs=[SMEM_SPEC] + [VMEM_SPEC] * (8 + len(params)),
    )(parity, *lanes, near, far, edge, *params)
    from_partner = swapped(sent, "seq", 1)
    kept, kept_parts = call(
        functools.partial(chunk_kernel, False),
        (state_struct, parts_struct),
        in_specs=[SMEM_SPEC] + [VMEM_SPEC] * 6,
    )(1 - parity, *lanes, edges)

    total, state = call(pair_kernel, (state_struct, entry_struct))(kept, from_partner)
    paired = total
    w_across, _ = lax.optimization_barrier((w_across, total))
    w_opposite = swapped(w_across, "mp", 1)
    prefix = []
    bits = range(1, seq_count.bit_length() - 1)
    for bit in bits:
        later = ((place >> bit) % 2 == place % 2).astype(jnp.int32).reshape(1)
        if bit == bits[-1]:
            received = swapped(state, "seq", 1 << bit)
            break
        arriving = swapped(total, "seq", 1 << bit)
        wide, total, state = call(
            functools.partial(advance_kernel, bool(prefix)),
            (struct(state_struct.shape, F32), state_struct, entry_struct),
            in_specs=[SMEM_SPEC] + [VMEM_SPEC] * (2 + len(prefix)),
        )(later, total, arriving, *prefix)
        prefix = [wide]
    sent_parts, kept_parts, _ = lax.optimization_barrier((sent_parts, kept_parts, paired))
    local_out, start_map = call(
        read_kernel,
        (f32_lanes, struct(f32_lanes.shape, BF16)),
        in_specs=[SMEM_SPEC] + [VMEM_SPEC] * 2,
    )(parity, sent_parts, kept_parts)
    received, local_out, start_map, w_opposite = lax.optimization_barrier(
        (received, local_out, start_map, w_opposite)
    )
    entry = call(
        functools.partial(entry_kernel, bool(prefix)),
        entry_struct,
        in_specs=[SMEM_SPEC] + [VMEM_SPEC] * (1 + len(prefix)),
    )(later, received, *prefix)
    other = swapped(entry, "seq", 1)
    joined = call(finish_kernel, bf16_lanes)(
        entry, from_partner, other, local_out, start_map, group_gain.reshape(1, width)
    )
    joined_whole = lax.all_gather(joined, "mp", axis=2, tiled=True)

    w_blocks = (w_output, w_beside, w_across, w_opposite)
    position = lax.axis_index("mp").astype(jnp.int32).reshape(1)
    own, *sent = call(
        functools.partial(mix_kernel, mp_count),
        (struct((rows, width), F32),) + (struct((rows, width), BF16),) * (mp_count - 1),
        scratch=[
            pltpu.VMEM((rows, full), F32),
            pltpu.VMEM((rows, full), F32),
        ],
        mib=24,
        in_specs=[SMEM_SPEC] + [VMEM_SPEC] * (5 + mp_count),
    )(position, joined_whole, whole, *w_blocks, ffn_key, ffn_value, ln2_gain.reshape(1, full))
    merged = own
    for step, item in enumerate(sent):
        merged = merged + swapped(item, "mp", step + 1).astype(F32)
    return merged.astype(BF16)


def solution(mesh):
    in_specs = (
        P("seq"),
        P("seq", "mp"),
        P("seq", "mp"),
        P(None, "mp"),
        P(),
        P(),
        P(),
        P(None, "mp"),
        P(None, "mp"),
        P(None, "mp"),
        P(),
        P("mp"),
        P(None, "mp"),
        P(),
        P("mp"),
        P(None, "mp"),
        P("mp"),
        P("mp", None),
        P(None, "mp"),
        P("mp", None),
    )
    out_specs = P("seq", "mp")
    return jax.shard_map(
        on_device, mesh=mesh, in_specs=in_specs, out_specs=out_specs, check_vma=False
    )
```

```python
import functools

import jax
import jax.numpy as jnp
from jax import lax
from jax.experimental import pallas as pl
from jax.experimental.pallas import tpu as pltpu
from jax.sharding import PartitionSpec as P

HEAD = 64
DECAY_SCALE = 0.606531
NORM_EPS = 1e-05
GROUP_EPS = 0.00064
UNIT_EPS = 1e-06
F32 = jnp.float32
BF16 = jnp.bfloat16
MIB = 1024 * 1024
VMEM_SPEC = pl.BlockSpec(memory_space=pltpu.VMEM)
SMEM_SPEC = pl.BlockSpec(memory_space=pltpu.SMEM)


def mm(left, right):
    return jnp.dot(left, right, preferred_element_type=F32)


def mm_rows(left, right):
    return lax.dot_general(left, right, (((1,), (1,)), ((), ())), preferred_element_type=F32)


def mm_cols(left, right):
    return lax.dot_general(left, right, (((0,), (0,)), ((), ())), preferred_element_type=F32)


def halves(value):
    high = value.astype(BF16)
    return high, (value - high.astype(F32)).astype(BF16)


def head_sum(value, ones):
    high, low = halves(value)
    return mm(high, ones) + mm(low, ones)


def ids_of(shape, dim):
    return lax.broadcasted_iota(jnp.int32, shape, dim)


def block_ones(width):
    same = ids_of((width, width), 0) // HEAD == ids_of((width, width), 1) // HEAD
    return same


def spread(packed, same_head):
    tiled = jnp.concatenate([packed] * (packed.shape[1] // HEAD), axis=0)
    return jnp.where(same_head, tiled, jnp.zeros_like(tiled))


def layer_norm(values, gain):
    row_mean = jnp.mean(values, axis=-1, keepdims=True)
    centered = values - row_mean
    variance = jnp.mean(centered * centered, axis=-1, keepdims=True)
    return centered * lax.rsqrt(variance + NORM_EPS) * gain


def embed_kernel(ids_ref, fwd_ref, embed_ref, strand_ref, other_ref):
    rows = fwd_ref.shape[0]
    ids = ids_ref[...]
    letters = ids_of((embed_ref.shape[0], rows), 0)
    embed = embed_ref[...]

    def looked_up(values):
        onehot = (values == letters).astype(F32)
        return lax.dot_general(
            onehot,
            embed,
            (((0,), (0,)), ((), ())),
            precision=lax.Precision.HIGHEST,
            preferred_element_type=F32,
        )

    strand_ref[...] = (fwd_ref[...].astype(F32) + looked_up(ids)).astype(BF16)
    other_ref[...] = looked_up(3 - ids)


def strands_kernel(rc_ref, strand_ref, other_ref, out_ref):
    rows = rc_ref.shape[0]
    out_ref[0] = strand_ref[...]
    flip = (ids_of((rows, rows), 0) + ids_of((rows, rows), 1) == rows - 1).astype(F32)
    out_ref[1] = (mm(flip.astype(BF16), rc_ref[...]) + other_ref[...]).astype(BF16)


def inverse_of(pulls, rows):
    row_ids, col_ids = ids_of((rows, rows), 0), ids_of((rows, rows), 1)
    eye = (row_ids == col_ids).astype(F32)
    size = 1
    inverses = None
    while size < rows:
        within = (row_ids // (2 * size) == col_ids // (2 * size)) & (row_ids // size != col_ids // size)
        parts = [jnp.where(within, pull, 0.0) for pull in pulls]
        if size == 1:
            inverses = [eye + part for part in parts]
        else:
            lows = [inverse.astype(BF16) for inverse in inverses]
            products = [mm(part.astype(BF16), low).astype(BF16) for part, low in zip(parts, lows)]
            inverses = [inverse + mm(low, product) for inverse, low, product in zip(inverses, lows, products)]
        size *= 2
    return inverses


def project_all(mix, params):
    w_r, w_k, w_v, w_d1, w_c1, w_d2, w_c2, d_base, c_base = params
    for index, weight in enumerate((w_r, w_k, w_v)):
        yield mm(mix(index), weight[...])
    decay_low = jnp.tanh(mm_rows(mix(3), w_d1[...])).astype(BF16)
    yield -DECAY_SCALE * jax.nn.sigmoid(d_base[...] + mm(decay_low, w_d2[...]))
    rate_low = mm_rows(mix(4), w_c1[...]).astype(BF16)
    yield jax.nn.sigmoid(c_base[...] + mm(rate_low, w_c2[...]))


def project_kernel(x_ref, *refs):
    (gain_ref, mixing_ref), params = refs[:2], refs[2:11]
    outs, edge_ref, (normed, mixed) = refs[11:16], refs[16], refs[17:]
    strands, rows, _ = x_ref.shape
    width = outs[0].shape[2]
    pad = 8
    gain = gain_ref[...]
    for s in range(strands):
        values = layer_norm(x_ref[s].astype(F32), gain)
        normed[s, pad : pad + rows, :] = values
        normed[s, pad - 1 : pad, :] = jnp.zeros_like(values[:1])
        normed[s, pad + rows : pad + rows + 1, :] = jnp.zeros_like(values[:1])
        edge_ref[s : s + 1, :] = values[:1]
        edge_ref[strands + s : strands + s + 1, :] = values[rows - 1 :]

    step = 16
    for s in range(strands):
        for start in range(0, rows, step):
            center = normed[s, pad + start : pad + start + step, :]
            for d in range(2):
                shift = pad + start - 1 + 2 * d
                change = normed[s, shift : shift + step, :] - center
                place = (d * strands + s) * rows + start
                for index in range(mixed.shape[0]):
                    weight = mixing_ref[index : index + 1, :]
                    mixed[index, place : place + step, :] = (center + change * weight).astype(BF16)

    def mix(index):
        return mixed[index]

    shape = (2 * strands, rows, width)
    for out_ref, result in zip(outs, project_all(mix, params)):
        out_ref[...] = result.reshape(shape)


def masked_heads(value, lane_head, heads):
    return jnp.concatenate([jnp.where(lane_head == h, value, 0.0).astype(BF16) for h in range(heads)], axis=0)


def chunk_kernel(first, direction_ref, *refs):
    lanes, refs = refs[:5], refs[5:]
    if first:
        partner_ref, beyond_ref, edge_ref, gain_ref, mixing_ref, *params, state_ref, parts_ref, edges_ref = refs
    else:
        edges_ref, state_ref, parts_ref = refs
    strands, _, rows, width = parts_ref.shape
    heads = width // HEAD
    d = direction_ref[0]
    if first:
        center = edge_ref[...]
        near, far = partner_ref[...].astype(F32), beyond_ref[...].astype(F32)
        odd = d == 1
        halo = jnp.concatenate([jnp.where(odd, near, far), jnp.where(odd, far, near)], axis=0)
        change = layer_norm(halo, gain_ref[...]) - center

        def mix(index):
            return (center + change * mixing_ref[index : index + 1, :]).astype(BF16)

        for index, result in enumerate(project_all(mix, params)):
            edges_ref[index] = result
    edge_row = d * (rows - 1)
    at_edge = ids_of((rows, width), 0) == edge_row
    order = (ids_of((rows, rows), 0) - ids_of((rows, rows), 1)) * (1 - 2 * d)
    strict, inclusive = order > 0, order >= 0
    same = block_ones(width)
    ones = same.astype(F32).astype(BF16)
    lane_head = ids_of((1, width), 1) // HEAD
    tri = inclusive.astype(F32).astype(BF16)

    def of_heads(value):
        return masked_heads(value, lane_head, heads)

    def prepared(s):
        g = d * strands + s

        def lane(index, ref):
            return jnp.where(at_edge, edges_ref[index, pl.ds(g, 1), :], ref[g])

        receptance, key, value, log_decay, rate = [lane(index, ref) for index, ref in enumerate(lanes)]
        unit = key * lax.rsqrt(head_sum(key * key, ones) + UNIT_EPS)
        high, low = halves(log_decay)
        totals = mm(tri, high) + mm(tri, low)
        middle = totals[rows // 2 : rows // 2 + 1]
        final = jnp.where(d == 0, totals[rows - 1 : rows], totals[0:1])
        there = jnp.exp(middle - totals)
        left_prev = -unit * jnp.exp(totals - log_decay - middle)
        left_here = receptance * jnp.exp(totals - middle)
        right_insert = rate * unit * there
        right_key = key * there
        from_start = jnp.exp(middle)
        to_end = jnp.exp(final - middle)
        left = left_prev.astype(BF16)
        insert_pulls, key_pulls = [], []
        for h in range(heads):
            mask = lane_head == h
            right = jnp.concatenate(
                [jnp.where(mask, right_insert, 0.0), jnp.where(mask, right_key, 0.0)], axis=0
            ).astype(BF16)
            scores = mm_rows(left, right)
            insert_pulls.append(jnp.where(strict, scores[:, :rows], 0.0))
            key_pulls.append(jnp.where(strict, scores[:, rows:], 0.0).astype(BF16))
        value_pull = mm(jnp.concatenate(key_pulls, axis=1), of_heads(value))
        value = value.astype(BF16)
        parts_ref[s, 0] = left_here.astype(BF16)
        parts_ref[s, 1] = right_insert.astype(BF16)
        parts_ref[s, 2] = right_key.astype(BF16)
        parts_ref[s, 3] = value
        parts_ref[s, 6] = (left_here * from_start).astype(BF16)
        tail_insert = (right_insert * to_end).astype(BF16)
        tail_key = (right_key * to_end).astype(BF16)
        solved_for = jnp.concatenate([of_heads(value_pull), of_heads(left_prev * from_start)], axis=1)
        end = mm_cols(tail_key, value)
        return insert_pulls, (solved_for, tail_insert, end, jnp.exp(final))

    prepared_all = [prepared(s) for s in range(strands)]
    inverses = inverse_of([pull for pulls, _ in prepared_all for pull in pulls], rows)
    for s, (_, (solved_for, tail_insert, end, kept)) in enumerate(prepared_all):
        own = inverses[s * heads : (s + 1) * heads]
        inverse = jnp.concatenate([item.astype(BF16) for item in own], axis=1)
        solved = mm(inverse, solved_for).astype(BF16)
        parts_ref[s, 4] = solved[:, :width]
        parts_ref[s, 5] = solved[:, width:]
        added = mm_cols(tail_insert, solved)
        ends = jnp.where(same, end + added[:, :width], 0.0)
        maps = jnp.where(same, added[:, width:], 0.0)
        end = sum(ends[h * HEAD : (h + 1) * HEAD] for h in range(heads))
        across = sum(maps[h * HEAD : (h + 1) * HEAD] for h in range(heads))
        diagonal = ids_of((HEAD, width), 0) == ids_of((HEAD, width), 1) % HEAD
        across = across + jnp.where(diagonal, kept, 0.0)
        state_ref[s] = jnp.concatenate([end, across], axis=0).astype(BF16)


def read_kernel(direction_ref, sent_ref, kept_ref, local_ref, map_ref):
    strands, _, rows, width = sent_ref.shape
    heads = width // HEAD
    lane_head = ids_of((1, width), 1) // HEAD
    for role, parts_ref in enumerate((sent_ref, kept_ref)):
        sign = (1 - 2 * direction_ref[0]) * (1 - 2 * role)
        inclusive = (ids_of((rows, rows), 0) - ids_of((rows, rows), 1)) * sign >= 0

        def group(s, carry):
            here, insert, key, value, pull, start, read = [parts_ref[s, i] for i in range(7)]
            reads = []
            for source in (insert, key):
                scores = mm_rows(here, masked_heads(source, lane_head, heads))
                parts = [scores[:, h * rows : (h + 1) * rows] for h in range(heads)]
                reads.append(jnp.concatenate([jnp.where(inclusive, p, 0.0).astype(BF16) for p in parts], axis=1))
            pull, start, value = [
                masked_heads(item, lane_head, heads) for item in (pull, start, value)
            ]
            g = role * strands + s
            local_ref[g] = mm(reads[0], pull) + mm(reads[1], value)
            map_ref[g] = (read.astype(F32) + mm(reads[0], start)).astype(BF16)
            return carry

        lax.fori_loop(0, strands, group, 0)


def composed(later, earlier, same_head, state_only=False):
    across = later[HEAD:].astype(BF16)
    state = mm(across, spread(earlier[:HEAD].astype(BF16), same_head)) + later[:HEAD].astype(F32)
    if state_only:
        return state
    return jnp.concatenate([state, mm(across, spread(earlier[HEAD:].astype(BF16), same_head))], axis=0)


def pair_kernel(keep_ref, from_ref, pair_ref):
    same_head = block_ones(keep_ref.shape[2])
    for s in range(keep_ref.shape[0]):
        pair_ref[s] = composed(keep_ref[s], from_ref[s], same_head).astype(BF16)


def advance_kernel(has_prefix, later_ref, total_ref, from_ref, *refs):
    *prefix_ref, wide_ref, next_ref = refs
    state_only = next_ref.shape[1] == HEAD
    same_head = block_ones(total_ref.shape[2])
    later = later_ref[0] == 1
    shape = total_ref.shape[1:]
    within = (ids_of(shape, 0) - HEAD) == ids_of(shape, 1) % HEAD
    for s in range(total_ref.shape[0]):
        own, other = total_ref[s], from_ref[s]
        total = composed(jnp.where(later, own, other), jnp.where(later, other, own), same_head, state_only)
        next_ref[s] = total.astype(BF16)
        ahead = jnp.where(later, other.astype(F32), within.astype(F32))
        if has_prefix:
            ahead = composed(prefix_ref[0][s], ahead, same_head)
        wide_ref[s] = ahead


def entry_kernel(has_prefix, later_ref, from_ref, *refs):
    *prefix_ref, entry_ref = refs
    same_head = block_ones(entry_ref.shape[2])
    for s in range(entry_ref.shape[0]):
        other = from_ref[s]
        ahead = jnp.where(later_ref[0] == 1, other, jnp.zeros_like(other))
        if has_prefix:
            ahead = composed(prefix_ref[0][s], ahead, same_head, True)
        entry_ref[s] = ahead.astype(BF16)


def finish_kernel(entry_ref, from_ref, other_ref, local_ref, map_ref, gain_ref, out_ref):
    strands, _, width = out_ref.shape
    same_head = block_ones(width)
    ones = same_head.astype(F32).astype(BF16)
    gain = gain_ref[...]
    for s in range(strands):
        kept = composed(from_ref[s], entry_ref[s], same_head, True).astype(BF16)
        joined = 0.0
        for role, state in enumerate((other_ref[s], kept)):
            g = role * strands + s
            wkv = local_ref[g] + mm(map_ref[g], spread(state, same_head))
            centered = wkv - head_sum(wkv, ones) * (1.0 / HEAD)
            variance = head_sum(centered * centered, ones) * (1.0 / HEAD)
            joined = joined + centered * lax.rsqrt(variance + GROUP_EPS)
        out_ref[s] = (joined * gain).astype(BF16)


def mix_kernel(blocks, index_ref, joined_ref, x_ref, *refs):
    w_refs, (up_ref, down_ref, gain_ref, own_ref) = refs[:blocks], refs[blocks : blocks + 4]
    *sent_refs, partial, total = refs[blocks + 4 :]
    strands, rows, _ = x_ref.shape
    width = own_ref.shape[1]
    gain = gain_ref[...]
    me = index_ref[0]
    attention = 0.0
    for step, w_ref in enumerate(w_refs):
        start = pl.multiple_of((me ^ step) * width, width)
        joined = jnp.concatenate([joined_ref[s, :, pl.ds(start, width)] for s in range(strands)], axis=0)
        attention = attention + mm(joined, w_ref[...])
    residuals = [x_ref[s].astype(F32) + attention[s * rows : (s + 1) * rows] for s in range(strands)]
    inner = jnp.concatenate([layer_norm(item, gain).astype(BF16) for item in residuals], axis=0)
    active = jnp.square(jnp.maximum(mm(inner, up_ref[...]), 0.0)).astype(BF16).astype(F32)
    added = sum(active[s * rows : (s + 1) * rows] for s in range(strands)).astype(BF16)
    partial[...] = mm(added, down_ref[...])
    total[...] = sum(residuals)

    def part(ref, which):
        return ref[:, pl.ds(pl.multiple_of(which * width, width), width)]

    own_ref[...] = part(total, me) + part(partial, me)
    for step, ref in enumerate(sent_refs):
        ref[...] = part(partial, me ^ (step + 1)).astype(BF16)


def call(kernel, out_shape, scratch=(), mib=12, us=10, **kwargs):
    return pl.pallas_call(
        kernel,
        out_shape=out_shape,
        scratch_shapes=list(scratch),
        cost_estimate=pl.CostEstimate(flops=us * 10**9, bytes_accessed=us * 10**6, transcendentals=0),
        compiler_params=pltpu.CompilerParams(vmem_limit_bytes=mib * MIB),
        **kwargs,
    )


def swapped(value, axis, mask):
    return lax.ppermute(value, axis, [(i, i ^ mask) for i in range(lax.axis_size(axis))])


def on_device(
    ids,
    hidden_fwd,
    hidden_rc,
    embed,
    ln1_gain,
    ln2_gain,
    mixing,
    w_receptance,
    w_key,
    w_value,
    decay_first_weight,
    decay_base,
    decay_second_weight,
    context_rate_first_weight,
    iclr_base,
    context_rate_second_weight,
    group_gain,
    w_output,
    ffn_key,
    ffn_value,
):
    rows, width = hidden_fwd.shape
    seq_count, mp_count = lax.axis_size("seq"), lax.axis_size("mp")
    strands, full = 2, ffn_key.shape[0]
    struct = jax.ShapeDtypeStruct

    mirror = [(i, seq_count - 1 - i) for i in range(seq_count)]
    rc_here = lax.ppermute(hidden_rc, "seq", mirror)
    params = (
        ln1_gain.reshape(1, full),
        mixing,
        w_receptance,
        w_key,
        w_value,
        decay_first_weight.T,
        context_rate_first_weight.T,
        decay_second_weight,
        context_rate_second_weight,
        decay_base.reshape(1, width),
        iclr_base.reshape(1, width),
    )
    strand, other = call(
        embed_kernel, (struct((rows, width), BF16), struct((rows, width), F32)), us=10, mib=4
    )(ids.reshape(1, rows), hidden_fwd, embed)
    rc_here, strand, other = lax.optimization_barrier((rc_here, strand, other))
    local = call(strands_kernel, struct((strands, rows, width), BF16), us=10, mib=4)(rc_here, strand, other)
    whole = lax.all_gather(local, "mp", axis=2, tiled=True)
    place = lax.axis_index("seq").astype(jnp.int32)
    parity = place % 2
    first, last = whole[:, 0], whole[:, rows - 1]
    near = lax.ppermute(jnp.where(parity == 1, first, last), "seq", [(i, i ^ 1) for i in range(seq_count)])
    bridges = [(i, i + 1) for i in range(1, seq_count - 1, 2)]
    bridges += [(j, i) for i, j in bridges]
    far = lax.ppermute(jnp.where(parity == 1, last, first), "seq", bridges)
    parity = parity.reshape(1)

    groups = 2 * strands
    f32_lanes, bf16_lanes = struct((groups, rows, width), F32), struct((strands, rows, width), BF16)
    parts_struct = struct((strands, 7, rows, width), BF16)
    state_struct = struct((strands, 2 * HEAD, width), BF16)
    entry_struct = struct((strands, HEAD, width), BF16)
    *lanes, edge = call(
        project_kernel,
        (f32_lanes,) * 5 + (struct((groups, full), F32),),
        scratch=[
            pltpu.VMEM((strands, rows + 16, full), F32),
            pltpu.VMEM((mixing.shape[0], groups * rows, full), BF16),
        ],
    )(whole, *params)

    sent, sent_parts, edges = call(
        functools.partial(chunk_kernel, True),
        (state_struct, parts_struct, struct((5, groups, width), F32)),
        in_specs=[SMEM_SPEC] + [VMEM_SPEC] * (8 + len(params)),
    )(parity, *lanes, near, far, edge, *params)
    from_partner = swapped(sent, "seq", 1)
    kept, kept_parts = call(
        functools.partial(chunk_kernel, False),
        (state_struct, parts_struct),
        in_specs=[SMEM_SPEC] + [VMEM_SPEC] * 6,
    )(1 - parity, *lanes, edges)

    total = call(pair_kernel, state_struct, mib=4, us=1)(kept, from_partner)
    w_held, _ = lax.optimization_barrier((w_output, total))
    w_across = swapped(w_held, "mp", 2)
    sent_parts, kept_parts, _ = lax.optimization_barrier((sent_parts, kept_parts, total))
    reads = call(
        read_kernel,
        (f32_lanes, struct(f32_lanes.shape, BF16)),
        mib=6,
        in_specs=[SMEM_SPEC] + [VMEM_SPEC] * 2,
    )(parity, sent_parts, kept_parts)
    prefix = []
    bits = range(1, seq_count.bit_length() - 1)
    for bit in bits:
        later = ((place >> bit) % 2 == place % 2).astype(jnp.int32).reshape(1)
        received = swapped(total, "seq", 1 << bit)
        if bit == bits[0]:
            received, reads = lax.optimization_barrier((received, reads))
        if bit == bits[-1]:
            break
        wide, total = call(
            functools.partial(advance_kernel, bool(prefix)),
            (struct(state_struct.shape, F32), entry_struct if bit + 1 == bits[-1] else state_struct),
            mib=4,
            us=1,
            in_specs=[SMEM_SPEC] + [VMEM_SPEC] * (2 + len(prefix)),
        )(later, total, received, *prefix)
        prefix = [wide]
    w_held, _ = lax.optimization_barrier((w_output, total))
    w_beside = swapped(w_held, "mp", 1)
    entry = call(
        functools.partial(entry_kernel, bool(prefix)),
        entry_struct,
        mib=4,
        us=1,
        in_specs=[SMEM_SPEC] + [VMEM_SPEC] * (1 + len(prefix)),
    )(later, received, *prefix)
    other = swapped(entry, "seq", 1)
    w_across, other = lax.optimization_barrier((w_across, other))
    w_opposite = swapped(w_across, "mp", 1)
    joined = call(finish_kernel, bf16_lanes, mib=6)(
        entry, from_partner, other, *reads, group_gain.reshape(1, width)
    )
    joined_whole = lax.all_gather(joined, "mp", axis=2, tiled=True)

    w_blocks = (w_output, w_beside, w_across, w_opposite)
    position = lax.axis_index("mp").astype(jnp.int32).reshape(1)
    own, *sent = call(
        functools.partial(mix_kernel, mp_count),
        (struct((rows, width), F32),) + (struct((rows, width), BF16),) * (mp_count - 1),
        scratch=[
            pltpu.VMEM((rows, full), F32),
            pltpu.VMEM((rows, full), F32),
        ],
        mib=16,
        in_specs=[SMEM_SPEC] + [VMEM_SPEC] * (5 + mp_count),
    )(position, joined_whole, whole, *w_blocks, ffn_key, ffn_value, ln2_gain.reshape(1, full))
    merged = own
    for step, item in enumerate(sent):
        merged = merged + swapped(item, "mp", step + 1).astype(F32)
    return merged.astype(BF16)


def solution(mesh):
    in_specs = (
        P("seq"),
        P("seq", "mp"),
        P("seq", "mp"),
        P(None, "mp"),
        P(),
        P(),
        P(),
        P(None, "mp"),
        P(None, "mp"),
        P(None, "mp"),
        P(),
        P("mp"),
        P(None, "mp"),
        P(),
        P("mp"),
        P(None, "mp"),
        P("mp"),
        P("mp", None),
        P(None, "mp"),
        P("mp", None),
    )
    out_specs = P("seq", "mp")
    return jax.shard_map(
        on_device, mesh=mesh, in_specs=in_specs, out_specs=out_specs, check_vma=False
    )
```

```python
import functools

import jax
import jax.numpy as jnp
from jax import lax
from jax.experimental import pallas as pl
from jax.experimental.pallas import tpu as pltpu
from jax.sharding import PartitionSpec as P

HEAD = 64
DECAY_SCALE = 0.606531
NORM_EPS = 1e-05
GROUP_EPS = 0.00064
UNIT_EPS = 1e-06
F32 = jnp.float32
BF16 = jnp.bfloat16
MIB = 1024 * 1024
VMEM_SPEC = pl.BlockSpec(memory_space=pltpu.VMEM)
SMEM_SPEC = pl.BlockSpec(memory_space=pltpu.SMEM)


def mm(left, right):
    return jnp.dot(left, right, preferred_element_type=F32)


def mm_rows(left, right):
    return lax.dot_general(left, right, (((1,), (1,)), ((), ())), preferred_element_type=F32)


def mm_cols(left, right):
    return lax.dot_general(left, right, (((0,), (0,)), ((), ())), preferred_element_type=F32)


def halves(value):
    high = value.astype(BF16)
    return high, (value - high.astype(F32)).astype(BF16)


def head_sum(value, ones):
    high, low = halves(value)
    return mm(high, ones) + mm(low, ones)


def ids_of(shape, dim):
    return lax.broadcasted_iota(jnp.int32, shape, dim)


def block_ones(width):
    same = ids_of((width, width), 0) // HEAD == ids_of((width, width), 1) // HEAD
    return same


def spread(packed, same_head):
    tiled = jnp.concatenate([packed] * (packed.shape[1] // HEAD), axis=0)
    return jnp.where(same_head, tiled, jnp.zeros_like(tiled))


def layer_norm(values, gain):
    row_mean = jnp.mean(values, axis=-1, keepdims=True)
    centered = values - row_mean
    variance = jnp.mean(centered * centered, axis=-1, keepdims=True)
    return centered * lax.rsqrt(variance + NORM_EPS) * gain


def embed_kernel(ids_ref, fwd_ref, embed_ref, strand_ref, other_ref):
    rows = fwd_ref.shape[0]
    ids = ids_ref[...]
    letters = ids_of((embed_ref.shape[0], rows), 0)
    embed = embed_ref[...]

    def looked_up(values):
        onehot = (values == letters).astype(F32)
        return lax.dot_general(
            onehot,
            embed,
            (((0,), (0,)), ((), ())),
            precision=lax.Precision.HIGHEST,
            preferred_element_type=F32,
        )

    strand_ref[...] = (fwd_ref[...].astype(F32) + looked_up(ids)).astype(BF16)
    other_ref[...] = looked_up(3 - ids)


def strands_kernel(rc_ref, strand_ref, other_ref, out_ref):
    rows = rc_ref.shape[0]
    out_ref[0] = strand_ref[...]
    flip = (ids_of((rows, rows), 0) + ids_of((rows, rows), 1) == rows - 1).astype(F32)
    out_ref[1] = (mm(flip.astype(BF16), rc_ref[...]) + other_ref[...]).astype(BF16)


def inverse_of(pulls, rows):
    row_ids, col_ids = ids_of((rows, rows), 0), ids_of((rows, rows), 1)
    eye = (row_ids == col_ids).astype(F32)
    size = 1
    inverses = None
    while size < rows:
        within = (row_ids // (2 * size) == col_ids // (2 * size)) & (row_ids // size != col_ids // size)
        parts = [jnp.where(within, pull, 0.0) for pull in pulls]
        if size == 1:
            inverses = [eye + part for part in parts]
        else:
            lows = [inverse.astype(BF16) for inverse in inverses]
            products = [mm(part.astype(BF16), low).astype(BF16) for part, low in zip(parts, lows)]
            inverses = [inverse + mm(low, product) for inverse, low, product in zip(inverses, lows, products)]
        size *= 2
    return inverses


def gates(low, w_d2, w_c2, d_base, c_base):
    rank, width = w_d2.shape
    low = jnp.where(ids_of(low.shape, 1) < rank, jnp.tanh(low), low).astype(BF16)
    zero = jnp.zeros((rank, width), BF16)
    both = jnp.concatenate(
        [jnp.concatenate([w_d2, zero], axis=1), jnp.concatenate([zero, w_c2], axis=1)], axis=0
    )
    result = mm(low, both)
    log_decay = -DECAY_SCALE * jax.nn.sigmoid(d_base + result[:, :width])
    return log_decay, jax.nn.sigmoid(c_base + result[:, width:])


def project_kernel(x_ref, gain_ref, mixing_ref, w_k, w_v, w_d1, w_c1, w_d2, w_c2, d_base, c_base, *refs):
    outs, (normed, low_ref, edge_ref, mixed, shifts) = refs[:4], refs[4:]
    strands, rows, _ = x_ref.shape
    shape = outs[0].shape
    pad = 8
    gain = gain_ref[...]
    lows = [(w_d1[...].astype(F32), mixing_ref[3:4]), (w_c1[...].astype(F32), mixing_ref[4:5])]
    parts = [weight * (1.0 - share) for weight, share in lows] + [weight * share for weight, share in lows]
    low_ref[...] = jnp.concatenate(parts, axis=0).astype(BF16)
    half = low_ref.shape[0] // 2
    for s in range(strands):
        values = layer_norm(x_ref[s].astype(F32), gain)
        zero = jnp.zeros_like(values[:1])
        normed[s, pad : pad + rows, :] = values
        normed[s, pad - 1 : pad, :] = zero
        normed[s, pad + rows : pad + rows + 1, :] = zero
        edge_ref[s : s + 1, :] = values[:1]
        edge_ref[strands + s : strands + s + 1, :] = values[rows - 1 :]
        low = mm_rows(values.astype(BF16), low_ref[...])
        shifts[s, pad : pad + rows, :] = low[:, half:]
        shifts[s, pad - 1 : pad, :] = zero[:, :half]
        shifts[s, pad + rows : pad + rows + 1, :] = zero[:, :half]
        for d in range(2):
            shift = pad - 1 + 2 * d
            g = d * strands + s
            log_decay, rate = gates(
                low[:, :half] + shifts[s, shift : shift + rows, :], w_d2[...], w_c2[...], d_base[...], c_base[...]
            )
            outs[2][g] = log_decay
            outs[3][g] = rate
    blend(normed, mixing_ref, (1, 2), rows, mixed)
    outs[0][...] = mm(mixed[0], w_k[...]).reshape(shape)
    outs[1][...] = mm(mixed[1], w_v[...]).reshape(shape)


def blend(normed, mixing_ref, indices, rows, mixed):
    strands = normed.shape[0]
    step, pad = 16, 8
    for s in range(strands):
        for start in range(0, rows, step):
            center = normed[s, pad + start : pad + start + step, :]
            for d in range(2):
                shift = pad + start - 1 + 2 * d
                change = normed[s, shift : shift + step, :] - center
                place = (d * strands + s) * rows + start
                for slot, index in enumerate(indices):
                    weight = mixing_ref[index : index + 1, :]
                    mixed[slot, place : place + step, :] = (center + change * weight).astype(BF16)


def receptance_kernel(normed, mixing_ref, edge_ref, w_r, out_ref, mixed):
    groups, rows, _ = out_ref.shape
    blend(normed, mixing_ref, (0,), rows, mixed)
    out_ref[...] = mm(mixed[0], w_r[...]).reshape(out_ref.shape)
    edges = mm(edge_ref[...].astype(BF16), w_r[...])
    for g in range(groups):
        row = 0 if g < groups // 2 else rows - 1
        out_ref[g, row : row + 1] = edges[g : g + 1]


def masked_heads(value, lane_head, heads):
    return jnp.concatenate([jnp.where(lane_head == h, value, 0.0).astype(BF16) for h in range(heads)], axis=0)


def chunk_kernel(first, direction_ref, *refs):
    lanes, refs = refs[:4], refs[4:]
    if first:
        partner_ref, beyond_ref, edge_ref, low_ref, gain_ref, mixing_ref, w_k, w_v, *gate_refs = refs[:12]
        state_ref, parts_ref, here_ref, edges_ref, read_edge_ref = refs[12:]
    else:
        edges_ref, state_ref, parts_ref, here_ref = refs
    strands, _, rows, width = parts_ref.shape
    heads = width // HEAD
    d = direction_ref[0]
    if first:
        center = edge_ref[...]
        near, far = partner_ref[...].astype(F32), beyond_ref[...].astype(F32)
        odd = d == 1
        halo = jnp.concatenate([jnp.where(odd, near, far), jnp.where(odd, far, near)], axis=0)
        halo = layer_norm(halo, gain_ref[...])
        change = halo - center

        def mix(index):
            return (center + change * mixing_ref[index : index + 1, :]).astype(BF16)

        edges_ref[0] = mm(mix(1), w_k[...])
        edges_ref[1] = mm(mix(2), w_v[...])
        low = mm_rows(jnp.concatenate([center, halo], axis=0).astype(BF16), low_ref[...])
        half, count = low.shape[1] // 2, center.shape[0]
        low = low[:count, :half] + low[count:, half:]
        edges_ref[2], edges_ref[3] = gates(low, *[ref[...] for ref in gate_refs])
        read_edge_ref[...] = center + change * mixing_ref[0:1, :]
    edge_row = d * (rows - 1)
    at_edge = ids_of((rows, width), 0) == edge_row
    order = (ids_of((rows, rows), 0) - ids_of((rows, rows), 1)) * (1 - 2 * d)
    strict, inclusive = order > 0, order >= 0
    same = block_ones(width)
    ones = same.astype(F32).astype(BF16)
    lane_head = ids_of((1, width), 1) // HEAD
    tri = inclusive.astype(F32).astype(BF16)

    def of_heads(value):
        return masked_heads(value, lane_head, heads)

    def prepared(s):
        g = d * strands + s

        def lane(index, ref):
            return jnp.where(at_edge, edges_ref[index, pl.ds(g, 1), :], ref[g])

        key, value, log_decay, rate = [lane(index, ref) for index, ref in enumerate(lanes)]
        unit = key * lax.rsqrt(head_sum(key * key, ones) + UNIT_EPS)
        high, low = halves(log_decay)
        totals = mm(tri, high) + mm(tri, low)
        middle = totals[rows // 2 : rows // 2 + 1]
        final = jnp.where(d == 0, totals[rows - 1 : rows], totals[0:1])
        there = jnp.exp(middle - totals)
        left_prev = -unit * jnp.exp(totals - log_decay - middle)
        right_insert = rate * unit * there
        right_key = key * there
        from_start = jnp.exp(middle)
        to_end = jnp.exp(final - middle)
        left = left_prev.astype(BF16)
        insert_pulls, key_pulls = [], []
        for h in range(heads):
            mask = lane_head == h
            right = jnp.concatenate(
                [jnp.where(mask, right_insert, 0.0), jnp.where(mask, right_key, 0.0)], axis=0
            ).astype(BF16)
            scores = mm_rows(left, right)
            insert_pulls.append(jnp.where(strict, scores[:, :rows], 0.0))
            key_pulls.append(jnp.where(strict, scores[:, rows:], 0.0).astype(BF16))
        value_pull = mm(jnp.concatenate(key_pulls, axis=1), of_heads(value))
        value = value.astype(BF16)
        here_ref[s, :rows] = jnp.exp(totals - middle)
        here_ref[s, rows:] = jnp.broadcast_to(from_start, (here_ref.shape[1] - rows, width))
        parts_ref[s, 0] = right_insert.astype(BF16)
        parts_ref[s, 1] = right_key.astype(BF16)
        parts_ref[s, 2] = value
        tail_insert = (right_insert * to_end).astype(BF16)
        tail_key = (right_key * to_end).astype(BF16)
        solved_for = jnp.concatenate([of_heads(value_pull), of_heads(left_prev * from_start)], axis=1)
        end = mm_cols(tail_key, value)
        return insert_pulls, (solved_for, tail_insert, end, jnp.exp(final))

    prepared_all = [prepared(s) for s in range(strands)]
    inverses = inverse_of([pull for pulls, _ in prepared_all for pull in pulls], rows)
    for s, (_, (solved_for, tail_insert, end, kept)) in enumerate(prepared_all):
        own = inverses[s * heads : (s + 1) * heads]
        inverse = jnp.concatenate([item.astype(BF16) for item in own], axis=1)
        solved = mm(inverse, solved_for).astype(BF16)
        parts_ref[s, 3] = solved[:, :width]
        parts_ref[s, 4] = solved[:, width:]
        added = mm_cols(tail_insert, solved)
        ends = jnp.where(same, end + added[:, :width], 0.0)
        maps = jnp.where(same, added[:, width:], 0.0)
        end = sum(ends[h * HEAD : (h + 1) * HEAD] for h in range(heads))
        across = sum(maps[h * HEAD : (h + 1) * HEAD] for h in range(heads))
        diagonal = ids_of((HEAD, width), 0) == ids_of((HEAD, width), 1) % HEAD
        across = across + jnp.where(diagonal, kept, 0.0)
        state_ref[s] = jnp.concatenate([end, across], axis=0).astype(BF16)


def read_kernel(
    direction_ref, receptances, sent_ref, kept_ref, sent_here_ref, kept_here_ref, local_ref, map_ref
):
    strands, _, rows, width = sent_ref.shape
    heads = width // HEAD
    lane_head = ids_of((1, width), 1) // HEAD
    for role, (parts_ref, here_ref) in enumerate(((sent_ref, sent_here_ref), (kept_ref, kept_here_ref))):
        d = (direction_ref[0] + role) % 2
        inclusive = (ids_of((rows, rows), 0) - ids_of((rows, rows), 1)) * (1 - 2 * d) >= 0

        def group(s, carry):
            insert, key, value, pull, start = [parts_ref[s, i] for i in range(5)]
            left = receptances[d * strands + s] * here_ref[s, :rows]
            here = left.astype(BF16)
            reads = []
            for source in (insert, key):
                scores = mm_rows(here, masked_heads(source, lane_head, heads))
                parts = [scores[:, h * rows : (h + 1) * rows] for h in range(heads)]
                reads.append(jnp.concatenate([jnp.where(inclusive, p, 0.0).astype(BF16) for p in parts], axis=1))
            pull, start, value = [
                masked_heads(item, lane_head, heads) for item in (pull, start, value)
            ]
            g = role * strands + s
            local_ref[g] = mm(reads[0], pull) + mm(reads[1], value)
            map_ref[g] = (left * here_ref[s, rows : rows + 1] + mm(reads[0], start)).astype(BF16)
            return carry

        lax.fori_loop(0, strands, group, 0)


def composed(later, earlier, same_head, state_only=False):
    across = later[HEAD:].astype(BF16)
    state = mm(across, spread(earlier[:HEAD].astype(BF16), same_head)) + later[:HEAD].astype(F32)
    if state_only:
        return state
    return jnp.concatenate([state, mm(across, spread(earlier[HEAD:].astype(BF16), same_head))], axis=0)


def pair_kernel(keep_ref, from_ref, pair_ref):
    same_head = block_ones(keep_ref.shape[2])
    for s in range(keep_ref.shape[0]):
        pair_ref[s] = composed(keep_ref[s], from_ref[s], same_head).astype(BF16)


def advance_kernel(has_prefix, later_ref, total_ref, from_ref, *refs):
    *prefix_ref, wide_ref, next_ref = refs
    state_only = next_ref.shape[1] == HEAD
    same_head = block_ones(total_ref.shape[2])
    later = later_ref[0] == 1
    shape = total_ref.shape[1:]
    within = (ids_of(shape, 0) - HEAD) == ids_of(shape, 1) % HEAD
    for s in range(total_ref.shape[0]):
        own, other = total_ref[s], from_ref[s]
        total = composed(jnp.where(later, own, other), jnp.where(later, other, own), same_head, state_only)
        next_ref[s] = total.astype(BF16)
        ahead = jnp.where(later, other.astype(F32), within.astype(F32))
        if has_prefix:
            ahead = composed(prefix_ref[0][s], ahead, same_head)
        wide_ref[s] = ahead


def entry_kernel(has_prefix, later_ref, from_ref, *refs):
    *prefix_ref, entry_ref = refs
    same_head = block_ones(entry_ref.shape[2])
    for s in range(entry_ref.shape[0]):
        other = from_ref[s]
        ahead = jnp.where(later_ref[0] == 1, other, jnp.zeros_like(other))
        if has_prefix:
            ahead = composed(prefix_ref[0][s], ahead, same_head, True)
        entry_ref[s] = ahead.astype(BF16)


def normed_heads(role, states, local_ref, map_ref):
    strands, width = len(states), local_ref.shape[2]
    same_head = block_ones(width)
    ones = same_head.astype(F32).astype(BF16)
    for s, state in enumerate(states):
        g = role * strands + s
        wkv = local_ref[g] + mm(map_ref[g], spread(state, same_head))
        centered = wkv - head_sum(wkv, ones) * (1.0 / HEAD)
        variance = head_sum(centered * centered, ones) * (1.0 / HEAD)
        yield centered * lax.rsqrt(variance + GROUP_EPS)


def kept_kernel(entry_ref, from_ref, local_ref, map_ref, out_ref):
    same_head = block_ones(out_ref.shape[2])
    states = [composed(from_ref[s], entry_ref[s], same_head, True).astype(BF16) for s in range(out_ref.shape[0])]
    for s, result in enumerate(normed_heads(1, states, local_ref, map_ref)):
        out_ref[s] = result


def finish_kernel(other_ref, kept_ref, local_ref, map_ref, gain_ref, out_ref):
    states = [other_ref[s] for s in range(out_ref.shape[0])]
    for s, result in enumerate(normed_heads(0, states, local_ref, map_ref)):
        out_ref[s] = ((result + kept_ref[s]) * gain_ref[...]).astype(BF16)


def mix_kernel(blocks, index_ref, joined_ref, x_ref, *refs):
    w_refs, (up_ref, down_ref, gain_ref, own_ref) = refs[:blocks], refs[blocks : blocks + 4]
    *sent_refs, partial, total = refs[blocks + 4 :]
    strands, rows, _ = x_ref.shape
    width = own_ref.shape[1]
    gain = gain_ref[...]
    me = index_ref[0]
    attention = 0.0
    for step, w_ref in enumerate(w_refs):
        start = pl.multiple_of((me ^ step) * width, width)
        joined = jnp.concatenate([joined_ref[s, :, pl.ds(start, width)] for s in range(strands)], axis=0)
        attention = attention + mm(joined, w_ref[...])
    residuals = [x_ref[s].astype(F32) + attention[s * rows : (s + 1) * rows] for s in range(strands)]
    inner = jnp.concatenate([layer_norm(item, gain).astype(BF16) for item in residuals], axis=0)
    active = jnp.square(jnp.maximum(mm(inner, up_ref[...]), 0.0)).astype(BF16).astype(F32)
    added = sum(active[s * rows : (s + 1) * rows] for s in range(strands)).astype(BF16)
    partial[...] = mm(added, down_ref[...])
    total[...] = sum(residuals)

    def part(ref, which):
        return ref[:, pl.ds(pl.multiple_of(which * width, width), width)]

    own_ref[...] = part(total, me) + part(partial, me)
    for step, ref in enumerate(sent_refs):
        ref[...] = part(partial, me ^ (step + 1)).astype(BF16)


def call(kernel, out_shape, scratch=(), mib=12, us=10, **kwargs):
    return pl.pallas_call(
        kernel,
        out_shape=out_shape,
        scratch_shapes=list(scratch),
        cost_estimate=pl.CostEstimate(flops=us * 10**9, bytes_accessed=us * 10**6, transcendentals=0),
        compiler_params=pltpu.CompilerParams(vmem_limit_bytes=mib * MIB),
        **kwargs,
    )


def swapped(value, axis, mask):
    return lax.ppermute(value, axis, [(i, i ^ mask) for i in range(lax.axis_size(axis))])


def on_device(
    ids,
    hidden_fwd,
    hidden_rc,
    embed,
    ln1_gain,
    ln2_gain,
    mixing,
    w_receptance,
    w_key,
    w_value,
    decay_first_weight,
    decay_base,
    decay_second_weight,
    context_rate_first_weight,
    iclr_base,
    context_rate_second_weight,
    group_gain,
    w_output,
    ffn_key,
    ffn_value,
):
    rows, width = hidden_fwd.shape
    seq_count, mp_count = lax.axis_size("seq"), lax.axis_size("mp")
    strands, full = 2, ffn_key.shape[0]
    struct = jax.ShapeDtypeStruct

    mirror = [(i, seq_count - 1 - i) for i in range(seq_count)]
    rc_here = lax.ppermute(hidden_rc, "seq", mirror)
    params = (
        ln1_gain.reshape(1, full),
        mixing,
        w_key,
        w_value,
        decay_first_weight.T,
        context_rate_first_weight.T,
        decay_second_weight,
        context_rate_second_weight,
        decay_base.reshape(1, width),
        iclr_base.reshape(1, width),
    )
    strand, other = call(
        embed_kernel, (struct((rows, width), BF16), struct((rows, width), F32)), us=10, mib=4
    )(ids.reshape(1, rows), hidden_fwd, embed)
    rc_here, strand, other = lax.optimization_barrier((rc_here, strand, other))
    local = call(strands_kernel, struct((strands, rows, width), BF16), us=10, mib=4)(rc_here, strand, other)
    whole = lax.all_gather(local, "mp", axis=2, tiled=True)
    place = lax.axis_index("seq").astype(jnp.int32)
    parity = place % 2
    first, last = whole[:, 0], whole[:, rows - 1]
    near = lax.ppermute(jnp.where(parity == 1, first, last), "seq", [(i, i ^ 1) for i in range(seq_count)])
    bridges = [(i, i + 1) for i in range(1, seq_count - 1, 2)]
    bridges += [(j, i) for i, j in bridges]
    far = lax.ppermute(jnp.where(parity == 1, last, first), "seq", bridges)
    parity = parity.reshape(1)

    groups = 2 * strands
    f32_lanes, bf16_lanes = struct((groups, rows, width), F32), struct((strands, rows, width), BF16)
    parts_struct = struct((strands, 5, rows, width), BF16)
    here_struct = struct((strands, rows + 8, width), F32)
    state_struct = struct((strands, 2 * HEAD, width), BF16)
    entry_struct = struct((strands, HEAD, width), BF16)
    low_shape = (4 * decay_first_weight.shape[1], full)
    *lanes, normed, low, edge = call(
        project_kernel,
        (f32_lanes,) * 4
        + (
            struct((strands, rows + 16, full), F32),
            struct(low_shape, BF16),
            struct((groups, full), F32),
        ),
        scratch=[
            pltpu.VMEM((2, groups * rows, full), BF16),
            pltpu.VMEM((strands, rows + 16, low_shape[0] // 2), F32),
        ],
    )(whole, *params)

    sent, sent_parts, sent_here, edges, read_edge = call(
        functools.partial(chunk_kernel, True),
        (state_struct, parts_struct, here_struct, struct((4, groups, width), F32), struct((groups, full), F32)),
        in_specs=[SMEM_SPEC] + [VMEM_SPEC] * 16,
    )(parity, *lanes, near, far, edge, low, *params[:4], *params[6:])
    from_partner = swapped(sent, "seq", 1)
    kept, kept_parts, kept_here = call(
        functools.partial(chunk_kernel, False),
        (state_struct, parts_struct, here_struct),
        in_specs=[SMEM_SPEC] + [VMEM_SPEC] * 5,
    )(1 - parity, *lanes, edges)

    total = call(pair_kernel, state_struct, mib=4, us=1)(kept, from_partner)
    w_held, _ = lax.optimization_barrier((w_output, total))
    w_across = swapped(w_held, "mp", 2)
    read_edge, _ = lax.optimization_barrier((read_edge, total))
    receptances = call(
        receptance_kernel,
        f32_lanes,
        scratch=[pltpu.VMEM((1, groups * rows, full), BF16)],
        mib=6,
        us=3,
    )(normed, mixing, read_edge, w_receptance)
    prefix = []
    bits = range(1, seq_count.bit_length() - 1)
    for bit in bits:
        later = ((place >> bit) % 2 == place % 2).astype(jnp.int32).reshape(1)
        received = swapped(total, "seq", 1 << bit)
        if bit == bits[0]:
            received, receptances = lax.optimization_barrier((received, receptances))
        if bit == bits[-1]:
            break
        wide, total = call(
            functools.partial(advance_kernel, bool(prefix)),
            (struct(state_struct.shape, F32), entry_struct if bit + 1 == bits[-1] else state_struct),
            mib=4,
            us=1,
            in_specs=[SMEM_SPEC] + [VMEM_SPEC] * (2 + len(prefix)),
        )(later, total, received, *prefix)
        prefix = [wide]
    w_held, _ = lax.optimization_barrier((w_output, total))
    w_beside = swapped(w_held, "mp", 1)
    sent_parts, kept_parts, _ = lax.optimization_barrier((sent_parts, kept_parts, total))
    reads = call(
        read_kernel,
        (f32_lanes, struct(f32_lanes.shape, BF16)),
        mib=6,
        in_specs=[SMEM_SPEC] + [VMEM_SPEC] * 5,
    )(parity, receptances, sent_parts, kept_parts, sent_here, kept_here)
    received, reads = lax.optimization_barrier((received, reads))
    entry = call(
        functools.partial(entry_kernel, bool(prefix)),
        entry_struct,
        mib=4,
        us=1,
        in_specs=[SMEM_SPEC] + [VMEM_SPEC] * (1 + len(prefix)),
    )(later, received, *prefix)
    other = swapped(entry, "seq", 1)
    kept_heads = call(kept_kernel, struct(bf16_lanes.shape, F32), mib=6, us=3)(entry, from_partner, *reads)
    w_across, other, kept_heads = lax.optimization_barrier((w_across, other, kept_heads))
    w_opposite = swapped(w_across, "mp", 1)
    joined = call(finish_kernel, bf16_lanes, mib=6)(other, kept_heads, *reads, group_gain.reshape(1, width))
    joined_whole = lax.all_gather(joined, "mp", axis=2, tiled=True)

    w_blocks = (w_output, w_beside, w_across, w_opposite)
    position = lax.axis_index("mp").astype(jnp.int32).reshape(1)
    own, *sent = call(
        functools.partial(mix_kernel, mp_count),
        (struct((rows, width), F32),) + (struct((rows, width), BF16),) * (mp_count - 1),
        scratch=[
            pltpu.VMEM((rows, full), F32),
            pltpu.VMEM((rows, full), F32),
        ],
        mib=16,
        in_specs=[SMEM_SPEC] + [VMEM_SPEC] * (5 + mp_count),
    )(position, joined_whole, whole, *w_blocks, ffn_key, ffn_value, ln2_gain.reshape(1, full))
    merged = own
    for step, item in enumerate(sent):
        merged = merged + swapped(item, "mp", step + 1).astype(F32)
    return merged.astype(BF16)


def solution(mesh):
    in_specs = (
        P("seq"),
        P("seq", "mp"),
        P("seq", "mp"),
        P(None, "mp"),
        P(),
        P(),
        P(),
        P(None, "mp"),
        P(None, "mp"),
        P(None, "mp"),
        P(),
        P("mp"),
        P(None, "mp"),
        P(),
        P("mp"),
        P(None, "mp"),
        P("mp"),
        P("mp", None),
        P(None, "mp"),
        P("mp", None),
    )
    out_specs = P("seq", "mp")
    return jax.shard_map(
        on_device, mesh=mesh, in_specs=in_specs, out_specs=out_specs, check_vma=False
    )
```

```python
import functools

import jax
import jax.numpy as jnp
from jax import lax
from jax.experimental import pallas as pl
from jax.experimental.pallas import tpu as pltpu
from jax.sharding import PartitionSpec as P

HEAD = 64
DECAY_SCALE = 0.606531
NORM_EPS = 1e-05
GROUP_EPS = 0.00064
UNIT_EPS = 1e-06
F32 = jnp.float32
BF16 = jnp.bfloat16
MIB = 1024 * 1024
VMEM_SPEC = pl.BlockSpec(memory_space=pltpu.VMEM)
SMEM_SPEC = pl.BlockSpec(memory_space=pltpu.SMEM)


def mm(left, right):
    return jnp.dot(left, right, preferred_element_type=F32)


def mm_rows(left, right):
    return lax.dot_general(left, right, (((1,), (1,)), ((), ())), preferred_element_type=F32)


def mm_cols(left, right):
    return lax.dot_general(left, right, (((0,), (0,)), ((), ())), preferred_element_type=F32)


def halves(value):
    high = value.astype(BF16)
    return high, (value - high.astype(F32)).astype(BF16)


def head_sum(value, ones):
    high, low = halves(value)
    return mm(high, ones) + mm(low, ones)


def ids_of(shape, dim):
    return lax.broadcasted_iota(jnp.int32, shape, dim)


def block_ones(width):
    same = ids_of((width, width), 0) // HEAD == ids_of((width, width), 1) // HEAD
    return same


def spread(packed, same_head):
    tiled = jnp.concatenate([packed] * (packed.shape[1] // HEAD), axis=0)
    return jnp.where(same_head, tiled, jnp.zeros_like(tiled))


def layer_norm(values, gain):
    row_mean = jnp.mean(values, axis=-1, keepdims=True)
    centered = values - row_mean
    variance = jnp.mean(centered * centered, axis=-1, keepdims=True)
    return centered * lax.rsqrt(variance + NORM_EPS) * gain


def embed_kernel(ids_ref, fwd_ref, embed_ref, strand_ref, other_ref):
    rows = fwd_ref.shape[0]
    ids = ids_ref[...]
    letters = ids_of((embed_ref.shape[0], rows), 0)
    embed = embed_ref[...]

    def looked_up(values):
        onehot = (values == letters).astype(F32)
        return lax.dot_general(
            onehot,
            embed,
            (((0,), (0,)), ((), ())),
            precision=lax.Precision.HIGHEST,
            preferred_element_type=F32,
        )

    strand_ref[...] = (fwd_ref[...].astype(F32) + looked_up(ids)).astype(BF16)
    other_ref[...] = looked_up(3 - ids)


def strands_kernel(rc_ref, strand_ref, other_ref, out_ref):
    rows = rc_ref.shape[0]
    out_ref[0] = strand_ref[...]
    flip = (ids_of((rows, rows), 0) + ids_of((rows, rows), 1) == rows - 1).astype(F32)
    out_ref[1] = (mm(flip.astype(BF16), rc_ref[...]) + other_ref[...]).astype(BF16)


def inverse_of(pulls, rows):
    row_ids, col_ids = ids_of((rows, rows), 0), ids_of((rows, rows), 1)
    eye = (row_ids == col_ids).astype(F32)
    size = 1
    inverses = None
    while size < rows:
        within = (row_ids // (2 * size) == col_ids // (2 * size)) & (row_ids // size != col_ids // size)
        parts = [jnp.where(within, pull, 0.0) for pull in pulls]
        if size == 1:
            inverses = [eye + part for part in parts]
        else:
            lows = [inverse.astype(BF16) for inverse in inverses]
            products = [mm(part.astype(BF16), low).astype(BF16) for part, low in zip(parts, lows)]
            inverses = [inverse + mm(low, product) for inverse, low, product in zip(inverses, lows, products)]
        size *= 2
    return inverses


def gates(low, w_d2, w_c2, d_base, c_base):
    rank, width = w_d2.shape
    low = jnp.where(ids_of(low.shape, 1) < rank, jnp.tanh(low), low).astype(BF16)
    zero = jnp.zeros((rank, width), BF16)
    both = jnp.concatenate(
        [jnp.concatenate([w_d2, zero], axis=1), jnp.concatenate([zero, w_c2], axis=1)], axis=0
    )
    result = mm(low, both)
    log_decay = -DECAY_SCALE * jax.nn.sigmoid(d_base + result[:, :width])
    return log_decay, jax.nn.sigmoid(c_base + result[:, width:])


def project_kernel(x_ref, gain_ref, mixing_ref, w_k, w_v, w_d1, w_c1, w_d2, w_c2, d_base, c_base, *refs):
    outs, (normed, low_ref, edge_ref, mixed, shifts) = refs[:4], refs[4:]
    strands, rows, _ = x_ref.shape
    shape = outs[0].shape
    pad = 8
    gain = gain_ref[...]
    lows = [(w_d1[...].astype(F32), mixing_ref[3:4]), (w_c1[...].astype(F32), mixing_ref[4:5])]
    parts = [weight * (1.0 - share) for weight, share in lows] + [weight * share for weight, share in lows]
    low_ref[...] = jnp.concatenate(parts, axis=0).astype(BF16)
    half = low_ref.shape[0] // 2
    for s in range(strands):
        values = layer_norm(x_ref[s].astype(F32), gain)
        zero = jnp.zeros_like(values[:1])
        normed[s, pad : pad + rows, :] = values
        normed[s, pad - 1 : pad, :] = zero
        normed[s, pad + rows : pad + rows + 1, :] = zero
        edge_ref[s : s + 1, :] = values[:1]
        edge_ref[strands + s : strands + s + 1, :] = values[rows - 1 :]
        low = mm_rows(values.astype(BF16), low_ref[...])
        shifts[s, pad : pad + rows, :] = low[:, half:]
        shifts[s, pad - 1 : pad, :] = zero[:, :half]
        shifts[s, pad + rows : pad + rows + 1, :] = zero[:, :half]
        for d in range(2):
            shift = pad - 1 + 2 * d
            g = d * strands + s
            log_decay, rate = gates(
                low[:, :half] + shifts[s, shift : shift + rows, :], w_d2[...], w_c2[...], d_base[...], c_base[...]
            )
            outs[2][g] = log_decay
            outs[3][g] = rate
    blend(normed, mixing_ref, (1, 2), rows, mixed)
    outs[0][...] = mm(mixed[0], w_k[...]).reshape(shape)
    outs[1][...] = mm(mixed[1], w_v[...]).reshape(shape)


def blend(normed, mixing_ref, indices, rows, mixed):
    strands = normed.shape[0]
    step, pad = 16, 8
    for s in range(strands):
        for start in range(0, rows, step):
            center = normed[s, pad + start : pad + start + step, :]
            for d in range(2):
                shift = pad + start - 1 + 2 * d
                change = normed[s, shift : shift + step, :] - center
                place = (d * strands + s) * rows + start
                for slot, index in enumerate(indices):
                    weight = mixing_ref[index : index + 1, :]
                    mixed[slot, place : place + step, :] = (center + change * weight).astype(BF16)


def receptance_kernel(direction_ref, normed, mixing_ref, sent_edge_ref, kept_edge_ref, w_r, out_ref, mixed):
    groups, rows, _ = out_ref.shape
    blend(normed, mixing_ref, (0,), rows, mixed)
    out_ref[...] = mm(mixed[0], w_r[...]).reshape(out_ref.shape)
    edges = [sent_edge_ref[...], kept_edge_ref[...]]
    swap = direction_ref[0] == 1
    edges = [jnp.where(swap, edges[1 - d], edges[d]) for d in range(2)]
    edges = mm(jnp.concatenate(edges, axis=0).astype(BF16), w_r[...])
    for g in range(groups):
        row = 0 if g < groups // 2 else rows - 1
        out_ref[g, row : row + 1] = edges[g : g + 1]


def masked_heads(value, lane_head, heads):
    return jnp.concatenate([jnp.where(lane_head == h, value, 0.0).astype(BF16) for h in range(heads)], axis=0)


def chunk_kernel(direction_ref, *refs):
    lanes, (halo_ref, edge_ref, low_ref, gain_ref, mixing_ref, w_k, w_v, *gate_refs) = refs[:4], refs[4:15]
    state_ref, parts_ref, here_ref, read_edge_ref = refs[15:]
    strands, _, rows, width = parts_ref.shape
    heads = width // HEAD
    d = direction_ref[0]
    center = jnp.where(d == 1, edge_ref[strands:], edge_ref[:strands])
    halo = layer_norm(halo_ref[...].astype(F32), gain_ref[...])
    change = halo - center

    def mix(index):
        return (center + change * mixing_ref[index : index + 1, :]).astype(BF16)

    low = mm_rows(jnp.concatenate([center, halo], axis=0).astype(BF16), low_ref[...])
    half = low.shape[1] // 2
    low = low[:strands, :half] + low[strands:, half:]
    edges = [mm(mix(1), w_k[...]), mm(mix(2), w_v[...]), *gates(low, *[ref[...] for ref in gate_refs])]
    read_edge_ref[...] = center + change * mixing_ref[0:1, :]
    edge_row = d * (rows - 1)
    at_edge = ids_of((rows, width), 0) == edge_row
    order = (ids_of((rows, rows), 0) - ids_of((rows, rows), 1)) * (1 - 2 * d)
    strict, inclusive = order > 0, order >= 0
    same = block_ones(width)
    ones = same.astype(F32).astype(BF16)
    lane_head = ids_of((1, width), 1) // HEAD
    tri = inclusive.astype(F32).astype(BF16)

    def of_heads(value):
        return masked_heads(value, lane_head, heads)

    def prepared(s):
        g = d * strands + s

        def lane(index, ref):
            return jnp.where(at_edge, edges[index][s : s + 1], ref[g])

        key, value, log_decay, rate = [lane(index, ref) for index, ref in enumerate(lanes)]
        unit = key * lax.rsqrt(head_sum(key * key, ones) + UNIT_EPS)
        high, low = halves(log_decay)
        totals = mm(tri, high) + mm(tri, low)
        middle = totals[rows // 2 : rows // 2 + 1]
        final = jnp.where(d == 0, totals[rows - 1 : rows], totals[0:1])
        there = jnp.exp(middle - totals)
        left_prev = -unit * jnp.exp(totals - log_decay - middle)
        right_insert = rate * unit * there
        right_key = key * there
        from_start = jnp.exp(middle)
        to_end = jnp.exp(final - middle)
        left = left_prev.astype(BF16)
        insert_pulls, key_pulls = [], []
        for h in range(heads):
            mask = lane_head == h
            right = jnp.concatenate(
                [jnp.where(mask, right_insert, 0.0), jnp.where(mask, right_key, 0.0)], axis=0
            ).astype(BF16)
            scores = mm_rows(left, right)
            insert_pulls.append(jnp.where(strict, scores[:, :rows], 0.0))
            key_pulls.append(jnp.where(strict, scores[:, rows:], 0.0).astype(BF16))
        value_pull = mm(jnp.concatenate(key_pulls, axis=1), of_heads(value))
        value = value.astype(BF16)
        here_ref[s, :rows] = jnp.exp(totals - middle)
        here_ref[s, rows:] = jnp.broadcast_to(from_start, (here_ref.shape[1] - rows, width))
        parts_ref[s, 0] = right_insert.astype(BF16)
        parts_ref[s, 1] = right_key.astype(BF16)
        parts_ref[s, 2] = value
        tail_insert = (right_insert * to_end).astype(BF16)
        tail_key = (right_key * to_end).astype(BF16)
        solved_for = jnp.concatenate([of_heads(value_pull), of_heads(left_prev * from_start)], axis=1)
        end = mm_cols(tail_key, value)
        return insert_pulls, (solved_for, tail_insert, end, jnp.exp(final))

    prepared_all = [prepared(s) for s in range(strands)]
    inverses = inverse_of([pull for pulls, _ in prepared_all for pull in pulls], rows)
    for s, (_, (solved_for, tail_insert, end, kept)) in enumerate(prepared_all):
        own = inverses[s * heads : (s + 1) * heads]
        inverse = jnp.concatenate([item.astype(BF16) for item in own], axis=1)
        solved = mm(inverse, solved_for).astype(BF16)
        parts_ref[s, 3] = solved[:, :width]
        parts_ref[s, 4] = solved[:, width:]
        added = mm_cols(tail_insert, solved)
        ends = jnp.where(same, end + added[:, :width], 0.0)
        maps = jnp.where(same, added[:, width:], 0.0)
        end = sum(ends[h * HEAD : (h + 1) * HEAD] for h in range(heads))
        across = sum(maps[h * HEAD : (h + 1) * HEAD] for h in range(heads))
        diagonal = ids_of((HEAD, width), 0) == ids_of((HEAD, width), 1) % HEAD
        across = across + jnp.where(diagonal, kept, 0.0)
        state_ref[s] = jnp.concatenate([end, across], axis=0).astype(BF16)


def read_kernel(
    direction_ref, receptances, sent_ref, kept_ref, sent_here_ref, kept_here_ref, local_ref, map_ref
):
    strands, _, rows, width = sent_ref.shape
    heads = width // HEAD
    lane_head = ids_of((1, width), 1) // HEAD
    for role, (parts_ref, here_ref) in enumerate(((sent_ref, sent_here_ref), (kept_ref, kept_here_ref))):
        d = (direction_ref[0] + role) % 2
        inclusive = (ids_of((rows, rows), 0) - ids_of((rows, rows), 1)) * (1 - 2 * d) >= 0

        def group(s, carry):
            insert, key, value, pull, start = [parts_ref[s, i] for i in range(5)]
            left = receptances[d * strands + s] * here_ref[s, :rows]
            here = left.astype(BF16)
            reads = []
            for source in (insert, key):
                scores = mm_rows(here, masked_heads(source, lane_head, heads))
                parts = [scores[:, h * rows : (h + 1) * rows] for h in range(heads)]
                reads.append(jnp.concatenate([jnp.where(inclusive, p, 0.0).astype(BF16) for p in parts], axis=1))
            pull, start, value = [
                masked_heads(item, lane_head, heads) for item in (pull, start, value)
            ]
            g = role * strands + s
            local_ref[g] = mm(reads[0], pull) + mm(reads[1], value)
            map_ref[g] = (left * here_ref[s, rows : rows + 1] + mm(reads[0], start)).astype(BF16)
            return carry

        lax.fori_loop(0, strands, group, 0)


def composed(later, earlier, same_head, state_only=False):
    across = later[HEAD:].astype(BF16)
    state = mm(across, spread(earlier[:HEAD].astype(BF16), same_head)) + later[:HEAD].astype(F32)
    if state_only:
        return state
    return jnp.concatenate([state, mm(across, spread(earlier[HEAD:].astype(BF16), same_head))], axis=0)


def pair_kernel(keep_ref, from_ref, pair_ref):
    same_head = block_ones(keep_ref.shape[2])
    for s in range(keep_ref.shape[0]):
        pair_ref[s] = composed(keep_ref[s], from_ref[s], same_head).astype(BF16)


def advance_kernel(has_prefix, later_ref, total_ref, from_ref, *refs):
    *prefix_ref, wide_ref, next_ref = refs
    state_only = next_ref.shape[1] == HEAD
    same_head = block_ones(total_ref.shape[2])
    later = later_ref[0] == 1
    shape = total_ref.shape[1:]
    within = (ids_of(shape, 0) - HEAD) == ids_of(shape, 1) % HEAD
    for s in range(total_ref.shape[0]):
        own, other = total_ref[s], from_ref[s]
        total = composed(jnp.where(later, own, other), jnp.where(later, other, own), same_head, state_only)
        next_ref[s] = total.astype(BF16)
        ahead = jnp.where(later, other.astype(F32), within.astype(F32))
        if has_prefix:
            ahead = composed(prefix_ref[0][s], ahead, same_head)
        wide_ref[s] = ahead


def entry_kernel(has_prefix, later_ref, from_ref, *refs):
    *prefix_ref, entry_ref = refs
    same_head = block_ones(entry_ref.shape[2])
    for s in range(entry_ref.shape[0]):
        other = from_ref[s]
        ahead = jnp.where(later_ref[0] == 1, other, jnp.zeros_like(other))
        if has_prefix:
            ahead = composed(prefix_ref[0][s], ahead, same_head, True)
        entry_ref[s] = ahead.astype(BF16)


def normed_heads(role, states, local_ref, map_ref):
    strands, width = len(states), local_ref.shape[2]
    same_head = block_ones(width)
    ones = same_head.astype(F32).astype(BF16)
    for s, state in enumerate(states):
        g = role * strands + s
        wkv = local_ref[g] + mm(map_ref[g], spread(state, same_head))
        centered = wkv - head_sum(wkv, ones) * (1.0 / HEAD)
        variance = head_sum(centered * centered, ones) * (1.0 / HEAD)
        yield centered * lax.rsqrt(variance + GROUP_EPS)


def kept_kernel(entry_ref, from_ref, local_ref, map_ref, out_ref):
    same_head = block_ones(out_ref.shape[2])
    states = [composed(from_ref[s], entry_ref[s], same_head, True).astype(BF16) for s in range(out_ref.shape[0])]
    for s, result in enumerate(normed_heads(1, states, local_ref, map_ref)):
        out_ref[s] = result


def finish_kernel(other_ref, kept_ref, local_ref, map_ref, gain_ref, out_ref):
    states = [other_ref[s] for s in range(out_ref.shape[0])]
    for s, result in enumerate(normed_heads(0, states, local_ref, map_ref)):
        out_ref[s] = ((result + kept_ref[s]) * gain_ref[...]).astype(BF16)


def mix_kernel(blocks, index_ref, joined_ref, x_ref, *refs):
    w_refs, (up_ref, down_ref, gain_ref, own_ref) = refs[:blocks], refs[blocks : blocks + 4]
    *sent_refs, partial, total = refs[blocks + 4 :]
    strands, rows, _ = x_ref.shape
    width = own_ref.shape[1]
    gain = gain_ref[...]
    me = index_ref[0]
    attention = 0.0
    for step, w_ref in enumerate(w_refs):
        start = pl.multiple_of((me ^ step) * width, width)
        joined = jnp.concatenate([joined_ref[s, :, pl.ds(start, width)] for s in range(strands)], axis=0)
        attention = attention + mm(joined, w_ref[...])
    residuals = [x_ref[s].astype(F32) + attention[s * rows : (s + 1) * rows] for s in range(strands)]
    inner = jnp.concatenate([layer_norm(item, gain).astype(BF16) for item in residuals], axis=0)
    active = jnp.square(jnp.maximum(mm(inner, up_ref[...]), 0.0)).astype(BF16).astype(F32)
    added = sum(active[s * rows : (s + 1) * rows] for s in range(strands)).astype(BF16)
    partial[...] = mm(added, down_ref[...])
    total[...] = sum(residuals)

    def part(ref, which):
        return ref[:, pl.ds(pl.multiple_of(which * width, width), width)]

    own_ref[...] = part(total, me) + part(partial, me)
    for step, ref in enumerate(sent_refs):
        ref[...] = part(partial, me ^ (step + 1)).astype(BF16)


def call(kernel, out_shape, scratch=(), mib=12, us=10, **kwargs):
    return pl.pallas_call(
        kernel,
        out_shape=out_shape,
        scratch_shapes=list(scratch),
        cost_estimate=pl.CostEstimate(flops=us * 10**9, bytes_accessed=us * 10**6, transcendentals=0),
        compiler_params=pltpu.CompilerParams(vmem_limit_bytes=mib * MIB),
        **kwargs,
    )


def swapped(value, axis, mask):
    return lax.ppermute(value, axis, [(i, i ^ mask) for i in range(lax.axis_size(axis))])


def on_device(
    ids,
    hidden_fwd,
    hidden_rc,
    embed,
    ln1_gain,
    ln2_gain,
    mixing,
    w_receptance,
    w_key,
    w_value,
    decay_first_weight,
    decay_base,
    decay_second_weight,
    context_rate_first_weight,
    iclr_base,
    context_rate_second_weight,
    group_gain,
    w_output,
    ffn_key,
    ffn_value,
):
    rows, width = hidden_fwd.shape
    seq_count, mp_count = lax.axis_size("seq"), lax.axis_size("mp")
    strands, full = 2, ffn_key.shape[0]
    struct = jax.ShapeDtypeStruct

    mirror = [(i, seq_count - 1 - i) for i in range(seq_count)]
    rc_here = lax.ppermute(hidden_rc, "seq", mirror)
    params = (
        ln1_gain.reshape(1, full),
        mixing,
        w_key,
        w_value,
        decay_first_weight.T,
        context_rate_first_weight.T,
        decay_second_weight,
        context_rate_second_weight,
        decay_base.reshape(1, width),
        iclr_base.reshape(1, width),
    )
    strand, other = call(
        embed_kernel, (struct((rows, width), BF16), struct((rows, width), F32)), us=10, mib=4
    )(ids.reshape(1, rows), hidden_fwd, embed)
    rc_here, strand, other = lax.optimization_barrier((rc_here, strand, other))
    local = call(strands_kernel, struct((strands, rows, width), BF16), us=10, mib=4)(rc_here, strand, other)
    whole = lax.all_gather(local, "mp", axis=2, tiled=True)
    place = lax.axis_index("seq").astype(jnp.int32)
    parity = place % 2
    first, last = whole[:, 0], whole[:, rows - 1]
    bridges = [(i, i + 1) for i in range(1, seq_count - 1, 2)]
    bridges += [(j, i) for i, j in bridges]
    far = lax.ppermute(jnp.where(parity == 1, last, first), "seq", bridges)
    parity = parity.reshape(1)

    groups = 2 * strands
    f32_lanes, bf16_lanes = struct((groups, rows, width), F32), struct((strands, rows, width), BF16)
    parts_struct = struct((strands, 5, rows, width), BF16)
    here_struct = struct((strands, rows + 8, width), F32)
    state_struct = struct((strands, 2 * HEAD, width), BF16)
    entry_struct = struct((strands, HEAD, width), BF16)
    low_shape = (4 * decay_first_weight.shape[1], full)
    *lanes, normed, low, edge = call(
        project_kernel,
        (f32_lanes,) * 4
        + (
            struct((strands, rows + 16, full), F32),
            struct(low_shape, BF16),
            struct((groups, full), F32),
        ),
        scratch=[
            pltpu.VMEM((2, groups * rows, full), BF16),
            pltpu.VMEM((strands, rows + 16, low_shape[0] // 2), F32),
        ],
    )(whole, *params)

    beside, _ = lax.optimization_barrier((jnp.where(parity == 1, first, last), edge))
    near = swapped(beside, "seq", 1)

    def chunk(direction, halo):
        return call(
            chunk_kernel,
            (state_struct, parts_struct, here_struct, struct((strands, full), F32)),
            in_specs=[SMEM_SPEC] + [VMEM_SPEC] * 15,
        )(direction, *lanes, halo, edge, low, *params[:4], *params[6:])

    sent, sent_parts, sent_here, sent_edge = chunk(parity, far)
    from_partner = swapped(sent, "seq", 1)
    kept, kept_parts, kept_here, kept_edge = chunk(1 - parity, near)

    total = call(pair_kernel, state_struct, mib=4, us=1)(kept, from_partner)
    w_held, _ = lax.optimization_barrier((w_output, total))
    w_across = swapped(w_held, "mp", 2)
    kept_edge, _ = lax.optimization_barrier((kept_edge, total))
    receptances = call(
        receptance_kernel,
        f32_lanes,
        scratch=[pltpu.VMEM((1, groups * rows, full), BF16)],
        mib=6,
        us=3,
        in_specs=[SMEM_SPEC] + [VMEM_SPEC] * 5,
    )(parity, normed, mixing, sent_edge, kept_edge, w_receptance)
    prefix = []
    bits = range(1, seq_count.bit_length() - 1)
    for bit in bits:
        later = ((place >> bit) % 2 == place % 2).astype(jnp.int32).reshape(1)
        received = swapped(total, "seq", 1 << bit)
        if bit == bits[0]:
            received, receptances = lax.optimization_barrier((received, receptances))
        if bit == bits[-1]:
            break
        wide, total = call(
            functools.partial(advance_kernel, bool(prefix)),
            (struct(state_struct.shape, F32), entry_struct if bit + 1 == bits[-1] else state_struct),
            mib=4,
            us=1,
            in_specs=[SMEM_SPEC] + [VMEM_SPEC] * (2 + len(prefix)),
        )(later, total, received, *prefix)
        prefix = [wide]
    w_held, _ = lax.optimization_barrier((w_output, total))
    w_beside = swapped(w_held, "mp", 1)
    sent_parts, kept_parts, _ = lax.optimization_barrier((sent_parts, kept_parts, total))
    reads = call(
        read_kernel,
        (f32_lanes, struct(f32_lanes.shape, BF16)),
        mib=6,
        in_specs=[SMEM_SPEC] + [VMEM_SPEC] * 5,
    )(parity, receptances, sent_parts, kept_parts, sent_here, kept_here)
    received, reads = lax.optimization_barrier((received, reads))
    entry = call(
        functools.partial(entry_kernel, bool(prefix)),
        entry_struct,
        mib=4,
        us=1,
        in_specs=[SMEM_SPEC] + [VMEM_SPEC] * (1 + len(prefix)),
    )(later, received, *prefix)
    other = swapped(entry, "seq", 1)
    kept_heads = call(kept_kernel, struct(bf16_lanes.shape, F32), mib=6, us=3)(entry, from_partner, *reads)
    w_across, other, kept_heads = lax.optimization_barrier((w_across, other, kept_heads))
    w_opposite = swapped(w_across, "mp", 1)
    joined = call(finish_kernel, bf16_lanes, mib=6)(other, kept_heads, *reads, group_gain.reshape(1, width))
    joined_whole = lax.all_gather(joined, "mp", axis=2, tiled=True)

    w_blocks = (w_output, w_beside, w_across, w_opposite)
    position = lax.axis_index("mp").astype(jnp.int32).reshape(1)
    own, *sent = call(
        functools.partial(mix_kernel, mp_count),
        (struct((rows, width), F32),) + (struct((rows, width), BF16),) * (mp_count - 1),
        scratch=[
            pltpu.VMEM((rows, full), F32),
            pltpu.VMEM((rows, full), F32),
        ],
        mib=16,
        in_specs=[SMEM_SPEC] + [VMEM_SPEC] * (5 + mp_count),
    )(position, joined_whole, whole, *w_blocks, ffn_key, ffn_value, ln2_gain.reshape(1, full))
    merged = own
    for step, item in enumerate(sent):
        merged = merged + swapped(item, "mp", step + 1).astype(F32)
    return merged.astype(BF16)


def solution(mesh):
    in_specs = (
        P("seq"),
        P("seq", "mp"),
        P("seq", "mp"),
        P(None, "mp"),
        P(),
        P(),
        P(),
        P(None, "mp"),
        P(None, "mp"),
        P(None, "mp"),
        P(),
        P("mp"),
        P(None, "mp"),
        P(),
        P("mp"),
        P(None, "mp"),
        P("mp"),
        P("mp", None),
        P(None, "mp"),
        P("mp", None),
    )
    out_specs = P("seq", "mp")
    return jax.shard_map(
        on_device, mesh=mesh, in_specs=in_specs, out_specs=out_specs, check_vma=False
    )
```

```python
import functools

import jax
import jax.numpy as jnp
from jax import lax
from jax.experimental import pallas as pl
from jax.experimental.pallas import tpu as pltpu
from jax.sharding import PartitionSpec as P

HEAD = 64
DECAY_SCALE = 0.606531
NORM_EPS = 1e-05
GROUP_EPS = 0.00064
UNIT_EPS = 1e-06
F32 = jnp.float32
BF16 = jnp.bfloat16
MIB = 1024 * 1024
VMEM_SPEC = pl.BlockSpec(memory_space=pltpu.VMEM)
SMEM_SPEC = pl.BlockSpec(memory_space=pltpu.SMEM)


def mm(left, right):
    return jnp.dot(left, right, preferred_element_type=F32)


def mm_rows(left, right):
    return lax.dot_general(left, right, (((1,), (1,)), ((), ())), preferred_element_type=F32)


def mm_cols(left, right):
    return lax.dot_general(left, right, (((0,), (0,)), ((), ())), preferred_element_type=F32)


def halves(value):
    high = value.astype(BF16)
    return high, (value - high.astype(F32)).astype(BF16)


def head_sum(value, ones):
    high, low = halves(value)
    return mm(high, ones) + mm(low, ones)


def ids_of(shape, dim):
    return lax.broadcasted_iota(jnp.int32, shape, dim)


def block_ones(width):
    same = ids_of((width, width), 0) // HEAD == ids_of((width, width), 1) // HEAD
    return same


def spread(packed, same_head):
    tiled = jnp.concatenate([packed] * (packed.shape[1] // HEAD), axis=0)
    return jnp.where(same_head, tiled, jnp.zeros_like(tiled))


def layer_norm(values, gain):
    row_mean = jnp.mean(values, axis=-1, keepdims=True)
    centered = values - row_mean
    variance = jnp.mean(centered * centered, axis=-1, keepdims=True)
    return centered * lax.rsqrt(variance + NORM_EPS) * gain


def embed_kernel(ids_ref, fwd_ref, embed_ref, strand_ref, other_ref):
    rows = fwd_ref.shape[0]
    ids = ids_ref[...]
    letters = ids_of((embed_ref.shape[0], rows), 0)
    embed = embed_ref[...]

    def looked_up(values):
        onehot = (values == letters).astype(F32)
        return lax.dot_general(
            onehot,
            embed,
            (((0,), (0,)), ((), ())),
            precision=lax.Precision.HIGHEST,
            preferred_element_type=F32,
        )

    strand_ref[...] = (fwd_ref[...].astype(F32) + looked_up(ids)).astype(BF16)
    other_ref[...] = looked_up(3 - ids)


def strands_kernel(rc_ref, strand_ref, other_ref, out_ref):
    rows = rc_ref.shape[0]
    out_ref[0] = strand_ref[...]
    flip = (ids_of((rows, rows), 0) + ids_of((rows, rows), 1) == rows - 1).astype(F32)
    out_ref[1] = (mm(flip.astype(BF16), rc_ref[...]) + other_ref[...]).astype(BF16)


def inverse_of(pulls, rows):
    row_ids, col_ids = ids_of((rows, rows), 0), ids_of((rows, rows), 1)
    eye = (row_ids == col_ids).astype(F32)
    size = 1
    inverses = None
    while size < rows:
        within = (row_ids // (2 * size) == col_ids // (2 * size)) & (row_ids // size != col_ids // size)
        parts = [jnp.where(within, pull, 0.0) for pull in pulls]
        if size == 1:
            inverses = [eye + part for part in parts]
        else:
            lows = [inverse.astype(BF16) for inverse in inverses]
            products = [mm(part.astype(BF16), low).astype(BF16) for part, low in zip(parts, lows)]
            inverses = [inverse + mm(low, product) for inverse, low, product in zip(inverses, lows, products)]
        size *= 2
    return inverses


def gates(low, w_d2, w_c2, d_base, c_base):
    rank, width = w_d2.shape
    low = jnp.where(ids_of(low.shape, 1) < rank, jnp.tanh(low), low).astype(BF16)
    zero = jnp.zeros((rank, width), BF16)
    both = jnp.concatenate(
        [jnp.concatenate([w_d2, zero], axis=1), jnp.concatenate([zero, w_c2], axis=1)], axis=0
    )
    result = mm(low, both)
    log_decay = -DECAY_SCALE * jax.nn.sigmoid(d_base + result[:, :width])
    return log_decay, jax.nn.sigmoid(c_base + result[:, width:])


def project_kernel(x_ref, gain_ref, mixing_ref, w_k, w_v, w_d1, w_c1, w_d2, w_c2, d_base, c_base, *refs):
    outs, (normed, low_ref, edge_ref, mixed, shifts) = refs[:4], refs[4:]
    strands, rows, _ = x_ref.shape
    shape = outs[0].shape
    pad = 8
    gain = gain_ref[...]
    lows = [(w_d1[...].astype(F32), mixing_ref[3:4]), (w_c1[...].astype(F32), mixing_ref[4:5])]
    parts = [weight * (1.0 - share) for weight, share in lows] + [weight * share for weight, share in lows]
    low_ref[...] = jnp.concatenate(parts, axis=0).astype(BF16)
    half = low_ref.shape[0] // 2
    for s in range(strands):
        values = layer_norm(x_ref[s].astype(F32), gain)
        zero = jnp.zeros_like(values[:1])
        normed[s, pad : pad + rows, :] = values
        normed[s, pad - 1 : pad, :] = zero
        normed[s, pad + rows : pad + rows + 1, :] = zero
        edge_ref[s : s + 1, :] = values[:1]
        edge_ref[strands + s : strands + s + 1, :] = values[rows - 1 :]
        low = mm_rows(values.astype(BF16), low_ref[...])
        shifts[s, pad : pad + rows, :] = low[:, half:]
        shifts[s, pad - 1 : pad, :] = zero[:, :half]
        shifts[s, pad + rows : pad + rows + 1, :] = zero[:, :half]
        for d in range(2):
            shift = pad - 1 + 2 * d
            g = d * strands + s
            log_decay, rate = gates(
                low[:, :half] + shifts[s, shift : shift + rows, :], w_d2[...], w_c2[...], d_base[...], c_base[...]
            )
            outs[2][g] = log_decay
            outs[3][g] = rate
    blend(normed, mixing_ref, (1, 2), rows, mixed)
    outs[0][...] = mm(mixed[0], w_k[...]).reshape(shape)
    outs[1][...] = mm(mixed[1], w_v[...]).reshape(shape)


def blend(normed, mixing_ref, indices, rows, mixed):
    strands = normed.shape[0]
    step, pad = 16, 8
    for s in range(strands):
        for start in range(0, rows, step):
            center = normed[s, pad + start : pad + start + step, :]
            for d in range(2):
                shift = pad + start - 1 + 2 * d
                change = normed[s, shift : shift + step, :] - center
                place = (d * strands + s) * rows + start
                for slot, index in enumerate(indices):
                    weight = mixing_ref[index : index + 1, :]
                    mixed[slot, place : place + step, :] = (center + change * weight).astype(BF16)


def receptance_kernel(direction_ref, normed, mixing_ref, sent_edge_ref, kept_edge_ref, w_r, out_ref, mixed):
    groups, rows, _ = out_ref.shape
    blend(normed, mixing_ref, (0,), rows, mixed)
    out_ref[...] = mm(mixed[0], w_r[...]).reshape(out_ref.shape)
    edges = [sent_edge_ref[...], kept_edge_ref[...]]
    swap = direction_ref[0] == 1
    edges = [jnp.where(swap, edges[1 - d], edges[d]) for d in range(2)]
    edges = mm(jnp.concatenate(edges, axis=0).astype(BF16), w_r[...])
    for g in range(groups):
        row = 0 if g < groups // 2 else rows - 1
        out_ref[g, row : row + 1] = edges[g : g + 1]


def masked_heads(value, lane_head, heads):
    return jnp.concatenate([jnp.where(lane_head == h, value, 0.0).astype(BF16) for h in range(heads)], axis=0)


def chunk_kernel(direction_ref, *refs):
    lanes, (halo_ref, edge_ref, low_ref, gain_ref, mixing_ref, w_k, w_v, *gate_refs) = refs[:4], refs[4:15]
    state_ref, parts_ref, here_ref, read_edge_ref = refs[15:]
    strands, _, rows, width = parts_ref.shape
    heads = width // HEAD
    d = direction_ref[0]
    center = jnp.where(d == 1, edge_ref[strands:], edge_ref[:strands])
    halo = layer_norm(halo_ref[...].astype(F32), gain_ref[...])
    change = halo - center

    def mix(index):
        return (center + change * mixing_ref[index : index + 1, :]).astype(BF16)

    low = mm_rows(jnp.concatenate([center, halo], axis=0).astype(BF16), low_ref[...])
    half = low.shape[1] // 2
    low = low[:strands, :half] + low[strands:, half:]
    edges = [mm(mix(1), w_k[...]), mm(mix(2), w_v[...]), *gates(low, *[ref[...] for ref in gate_refs])]
    read_edge_ref[...] = center + change * mixing_ref[0:1, :]
    edge_row = d * (rows - 1)
    at_edge = ids_of((rows, width), 0) == edge_row
    order = (ids_of((rows, rows), 0) - ids_of((rows, rows), 1)) * (1 - 2 * d)
    strict, inclusive = order > 0, order >= 0
    same = block_ones(width)
    ones = same.astype(F32).astype(BF16)
    lane_head = ids_of((1, width), 1) // HEAD
    tri = inclusive.astype(F32).astype(BF16)

    def of_heads(value):
        return masked_heads(value, lane_head, heads)

    def prepared(s):
        g = d * strands + s

        def lane(index, ref):
            return jnp.where(at_edge, edges[index][s : s + 1], ref[g])

        key, value, log_decay, rate = [lane(index, ref) for index, ref in enumerate(lanes)]
        unit = key * lax.rsqrt(head_sum(key * key, ones) + UNIT_EPS)
        high, low = halves(log_decay)
        totals = mm(tri, high) + mm(tri, low)
        middle = totals[rows // 2 : rows // 2 + 1]
        final = jnp.where(d == 0, totals[rows - 1 : rows], totals[0:1])
        there = jnp.exp(middle - totals)
        left_prev = -unit * jnp.exp(totals - log_decay - middle)
        right_insert = rate * unit * there
        right_key = key * there
        from_start = jnp.exp(middle)
        to_end = jnp.exp(final - middle)
        left = left_prev.astype(BF16)
        insert_pulls, key_pulls = [], []
        for h in range(heads):
            mask = lane_head == h
            right = jnp.concatenate(
                [jnp.where(mask, right_insert, 0.0), jnp.where(mask, right_key, 0.0)], axis=0
            ).astype(BF16)
            scores = mm_rows(left, right)
            insert_pulls.append(jnp.where(strict, scores[:, :rows], 0.0))
            key_pulls.append(jnp.where(strict, scores[:, rows:], 0.0).astype(BF16))
        value_pull = mm(jnp.concatenate(key_pulls, axis=1), of_heads(value))
        value = value.astype(BF16)
        here_ref[s, :rows] = jnp.exp(totals - middle)
        here_ref[s, rows:] = jnp.broadcast_to(from_start, (here_ref.shape[1] - rows, width))
        parts_ref[s, 0] = right_insert.astype(BF16)
        parts_ref[s, 1] = right_key.astype(BF16)
        parts_ref[s, 2] = value
        tail_insert = (right_insert * to_end).astype(BF16)
        tail_key = (right_key * to_end).astype(BF16)
        solved_for = jnp.concatenate([of_heads(value_pull), of_heads(left_prev * from_start)], axis=1)
        end = mm_cols(tail_key, value)
        return insert_pulls, (solved_for, tail_insert, end, jnp.exp(final))

    prepared_all = [prepared(s) for s in range(strands)]
    inverses = inverse_of([pull for pulls, _ in prepared_all for pull in pulls], rows)
    for s, (_, (solved_for, tail_insert, end, kept)) in enumerate(prepared_all):
        own = inverses[s * heads : (s + 1) * heads]
        inverse = jnp.concatenate([item.astype(BF16) for item in own], axis=1)
        solved = mm(inverse, solved_for).astype(BF16)
        parts_ref[s, 3] = solved[:, :width]
        parts_ref[s, 4] = solved[:, width:]
        added = mm_cols(tail_insert, solved)
        ends = jnp.where(same, end + added[:, :width], 0.0)
        maps = jnp.where(same, added[:, width:], 0.0)
        end = sum(ends[h * HEAD : (h + 1) * HEAD] for h in range(heads))
        across = sum(maps[h * HEAD : (h + 1) * HEAD] for h in range(heads))
        diagonal = ids_of((HEAD, width), 0) == ids_of((HEAD, width), 1) % HEAD
        across = across + jnp.where(diagonal, kept, 0.0)
        state_ref[s] = jnp.concatenate([end, across], axis=0).astype(BF16)


def read_kernel(
    direction_ref, receptances, sent_ref, kept_ref, sent_here_ref, kept_here_ref, local_ref, map_ref
):
    strands, _, rows, width = sent_ref.shape
    heads = width // HEAD
    lane_head = ids_of((1, width), 1) // HEAD
    for role, (parts_ref, here_ref) in enumerate(((sent_ref, sent_here_ref), (kept_ref, kept_here_ref))):
        d = (direction_ref[0] + role) % 2
        inclusive = (ids_of((rows, rows), 0) - ids_of((rows, rows), 1)) * (1 - 2 * d) >= 0

        def group(s, carry):
            insert, key, value, pull, start = [parts_ref[s, i] for i in range(5)]
            left = receptances[d * strands + s] * here_ref[s, :rows]
            here = left.astype(BF16)
            reads = []
            for source in (insert, key):
                scores = mm_rows(here, masked_heads(source, lane_head, heads))
                parts = [scores[:, h * rows : (h + 1) * rows] for h in range(heads)]
                reads.append(jnp.concatenate([jnp.where(inclusive, p, 0.0).astype(BF16) for p in parts], axis=1))
            pull, start, value = [
                masked_heads(item, lane_head, heads) for item in (pull, start, value)
            ]
            g = role * strands + s
            local_ref[g] = mm(reads[0], pull) + mm(reads[1], value)
            map_ref[g] = left * here_ref[s, rows : rows + 1] + mm(reads[0], start)
            return carry

        lax.fori_loop(0, strands, group, 0)


def composed(later, earlier, same_head, state_only=False):
    across = later[HEAD:].astype(BF16)
    state = mm(across, spread(earlier[:HEAD].astype(BF16), same_head)) + later[:HEAD].astype(F32)
    if state_only:
        return state
    return jnp.concatenate([state, mm(across, spread(earlier[HEAD:].astype(BF16), same_head))], axis=0)


def pair_kernel(keep_ref, from_ref, pair_ref):
    same_head = block_ones(keep_ref.shape[2])
    for s in range(keep_ref.shape[0]):
        pair_ref[s] = composed(keep_ref[s], from_ref[s], same_head).astype(BF16)


def advance_kernel(has_prefix, later_ref, total_ref, from_ref, *refs):
    *prefix_ref, wide_ref, next_ref = refs
    state_only = next_ref.shape[1] == HEAD
    same_head = block_ones(total_ref.shape[2])
    later = later_ref[0] == 1
    shape = total_ref.shape[1:]
    within = (ids_of(shape, 0) - HEAD) == ids_of(shape, 1) % HEAD
    for s in range(total_ref.shape[0]):
        own, other = total_ref[s], from_ref[s]
        total = composed(jnp.where(later, own, other), jnp.where(later, other, own), same_head, state_only)
        next_ref[s] = total.astype(BF16)
        ahead = jnp.where(later, other.astype(F32), within.astype(F32))
        if has_prefix:
            ahead = composed(prefix_ref[0][s], ahead, same_head)
        wide_ref[s] = ahead


def entry_kernel(has_prefix, later_ref, from_ref, *refs):
    *prefix_ref, entry_ref = refs
    same_head = block_ones(entry_ref.shape[2])
    for s in range(entry_ref.shape[0]):
        other = from_ref[s]
        ahead = jnp.where(later_ref[0] == 1, other, jnp.zeros_like(other))
        if has_prefix:
            ahead = composed(prefix_ref[0][s], ahead, same_head, True)
        entry_ref[s] = ahead.astype(BF16)


def normed_heads(role, states, local_ref, map_ref):
    strands, width = len(states), local_ref.shape[2]
    same_head = block_ones(width)
    ones = same_head.astype(F32).astype(BF16)
    for s, state in enumerate(states):
        g = role * strands + s
        high, low = halves(map_ref[g])
        held, rest = [spread(item, same_head) for item in halves(state.astype(F32))]
        wkv = local_ref[g] + mm(high, held) + (mm(low, held) + mm(high, rest))
        centered = wkv - head_sum(wkv, ones) * (1.0 / HEAD)
        variance = head_sum(centered * centered, ones) * (1.0 / HEAD)
        yield centered * lax.rsqrt(variance + GROUP_EPS)


def kept_kernel(entry_ref, from_ref, local_ref, map_ref, out_ref):
    same_head = block_ones(out_ref.shape[2])
    states = [composed(from_ref[s], entry_ref[s], same_head, True) for s in range(out_ref.shape[0])]
    for s, result in enumerate(normed_heads(1, states, local_ref, map_ref)):
        out_ref[s] = result


def finish_kernel(other_ref, kept_ref, local_ref, map_ref, gain_ref, out_ref):
    states = [other_ref[s] for s in range(out_ref.shape[0])]
    for s, result in enumerate(normed_heads(0, states, local_ref, map_ref)):
        out_ref[s] = ((result + kept_ref[s]) * gain_ref[...]).astype(BF16)


def mix_kernel(blocks, index_ref, joined_ref, x_ref, *refs):
    w_refs, (up_ref, down_ref, gain_ref, own_ref) = refs[:blocks], refs[blocks : blocks + 4]
    *sent_refs, partial, total = refs[blocks + 4 :]
    strands, rows, _ = x_ref.shape
    width = own_ref.shape[1]
    gain = gain_ref[...]
    me = index_ref[0]
    attention = 0.0
    for step, w_ref in enumerate(w_refs):
        start = pl.multiple_of((me ^ step) * width, width)
        joined = jnp.concatenate([joined_ref[s, :, pl.ds(start, width)] for s in range(strands)], axis=0)
        attention = attention + mm(joined, w_ref[...])
    residuals = [x_ref[s].astype(F32) + attention[s * rows : (s + 1) * rows] for s in range(strands)]
    inner = jnp.concatenate([layer_norm(item, gain).astype(BF16) for item in residuals], axis=0)
    active = jnp.square(jnp.maximum(mm(inner, up_ref[...]), 0.0)).astype(BF16).astype(F32)
    added = sum(active[s * rows : (s + 1) * rows] for s in range(strands)).astype(BF16)
    partial[...] = mm(added, down_ref[...])
    total[...] = sum(residuals)

    def part(ref, which):
        return ref[:, pl.ds(pl.multiple_of(which * width, width), width)]

    own_ref[...] = part(total, me) + part(partial, me)
    for step, ref in enumerate(sent_refs):
        ref[...] = part(partial, me ^ (step + 1)).astype(BF16)


def call(kernel, out_shape, scratch=(), mib=12, us=10, **kwargs):
    return pl.pallas_call(
        kernel,
        out_shape=out_shape,
        scratch_shapes=list(scratch),
        cost_estimate=pl.CostEstimate(flops=us * 10**9, bytes_accessed=us * 10**6, transcendentals=0),
        compiler_params=pltpu.CompilerParams(vmem_limit_bytes=mib * MIB),
        **kwargs,
    )


def swapped(value, axis, mask):
    return lax.ppermute(value, axis, [(i, i ^ mask) for i in range(lax.axis_size(axis))])


def on_device(
    ids,
    hidden_fwd,
    hidden_rc,
    embed,
    ln1_gain,
    ln2_gain,
    mixing,
    w_receptance,
    w_key,
    w_value,
    decay_first_weight,
    decay_base,
    decay_second_weight,
    context_rate_first_weight,
    iclr_base,
    context_rate_second_weight,
    group_gain,
    w_output,
    ffn_key,
    ffn_value,
):
    rows, width = hidden_fwd.shape
    seq_count, mp_count = lax.axis_size("seq"), lax.axis_size("mp")
    strands, full = 2, ffn_key.shape[0]
    struct = jax.ShapeDtypeStruct

    mirror = [(i, seq_count - 1 - i) for i in range(seq_count)]
    rc_here = lax.ppermute(hidden_rc, "seq", mirror)
    params = (
        ln1_gain.reshape(1, full),
        mixing,
        w_key,
        w_value,
        decay_first_weight.T,
        context_rate_first_weight.T,
        decay_second_weight,
        context_rate_second_weight,
        decay_base.reshape(1, width),
        iclr_base.reshape(1, width),
    )
    strand, other = call(
        embed_kernel, (struct((rows, width), BF16), struct((rows, width), F32)), us=10, mib=4
    )(ids.reshape(1, rows), hidden_fwd, embed)
    rc_here, strand, other = lax.optimization_barrier((rc_here, strand, other))
    local = call(strands_kernel, struct((strands, rows, width), BF16), us=10, mib=4)(rc_here, strand, other)
    whole = lax.all_gather(local, "mp", axis=2, tiled=True)
    place = lax.axis_index("seq").astype(jnp.int32)
    parity = place % 2
    first, last = whole[:, 0], whole[:, rows - 1]
    bridges = [(i, i + 1) for i in range(1, seq_count - 1, 2)]
    bridges += [(j, i) for i, j in bridges]
    far = lax.ppermute(jnp.where(parity == 1, last, first), "seq", bridges)
    parity = parity.reshape(1)

    groups = 2 * strands
    f32_lanes, bf16_lanes = struct((groups, rows, width), F32), struct((strands, rows, width), BF16)
    parts_struct = struct((strands, 5, rows, width), BF16)
    here_struct = struct((strands, rows + 8, width), F32)
    state_struct = struct((strands, 2 * HEAD, width), BF16)
    entry_struct = struct((strands, HEAD, width), BF16)
    low_shape = (4 * decay_first_weight.shape[1], full)
    *lanes, normed, low, edge = call(
        project_kernel,
        (f32_lanes,) * 4
        + (
            struct((strands, rows + 16, full), F32),
            struct(low_shape, BF16),
            struct((groups, full), F32),
        ),
        scratch=[
            pltpu.VMEM((2, groups * rows, full), BF16),
            pltpu.VMEM((strands, rows + 16, low_shape[0] // 2), F32),
        ],
    )(whole, *params)

    beside, _ = lax.optimization_barrier((jnp.where(parity == 1, first, last), edge))
    near = swapped(beside, "seq", 1)

    def chunk(direction, halo):
        return call(
            chunk_kernel,
            (state_struct, parts_struct, here_struct, struct((strands, full), F32)),
            in_specs=[SMEM_SPEC] + [VMEM_SPEC] * 15,
        )(direction, *lanes, halo, edge, low, *params[:4], *params[6:])

    sent, sent_parts, sent_here, sent_edge = chunk(parity, far)
    from_partner = swapped(sent, "seq", 1)
    kept, kept_parts, kept_here, kept_edge = chunk(1 - parity, near)

    total = call(pair_kernel, state_struct, mib=4, us=1)(kept, from_partner)
    w_held, _ = lax.optimization_barrier((w_output, total))
    w_across = swapped(w_held, "mp", 2)
    kept_edge, _ = lax.optimization_barrier((kept_edge, total))
    receptances = call(
        receptance_kernel,
        f32_lanes,
        scratch=[pltpu.VMEM((1, groups * rows, full), BF16)],
        mib=6,
        us=3,
        in_specs=[SMEM_SPEC] + [VMEM_SPEC] * 5,
    )(parity, normed, mixing, sent_edge, kept_edge, w_receptance)
    prefix = []
    bits = range(1, seq_count.bit_length() - 1)
    for bit in bits:
        later = ((place >> bit) % 2 == place % 2).astype(jnp.int32).reshape(1)
        received = swapped(total, "seq", 1 << bit)
        if bit == bits[0]:
            received, receptances = lax.optimization_barrier((received, receptances))
        if bit == bits[-1]:
            break
        wide, total = call(
            functools.partial(advance_kernel, bool(prefix)),
            (struct(state_struct.shape, F32), entry_struct if bit + 1 == bits[-1] else state_struct),
            mib=4,
            us=1,
            in_specs=[SMEM_SPEC] + [VMEM_SPEC] * (2 + len(prefix)),
        )(later, total, received, *prefix)
        prefix = [wide]
    w_held, _ = lax.optimization_barrier((w_output, total))
    w_beside = swapped(w_held, "mp", 1)
    sent_parts, kept_parts, _ = lax.optimization_barrier((sent_parts, kept_parts, total))
    reads = call(
        read_kernel,
        (f32_lanes, f32_lanes),
        mib=6,
        in_specs=[SMEM_SPEC] + [VMEM_SPEC] * 5,
    )(parity, receptances, sent_parts, kept_parts, sent_here, kept_here)
    received, reads = lax.optimization_barrier((received, reads))
    entry = call(
        functools.partial(entry_kernel, bool(prefix)),
        entry_struct,
        mib=4,
        us=1,
        in_specs=[SMEM_SPEC] + [VMEM_SPEC] * (1 + len(prefix)),
    )(later, received, *prefix)
    other = swapped(entry, "seq", 1)
    kept_heads = call(kept_kernel, struct(bf16_lanes.shape, F32), mib=6, us=3)(entry, from_partner, *reads)
    w_across, other, kept_heads = lax.optimization_barrier((w_across, other, kept_heads))
    w_opposite = swapped(w_across, "mp", 1)
    joined = call(finish_kernel, bf16_lanes, mib=6)(other, kept_heads, *reads, group_gain.reshape(1, width))
    joined_whole = lax.all_gather(joined, "mp", axis=2, tiled=True)

    w_blocks = (w_output, w_beside, w_across, w_opposite)
    position = lax.axis_index("mp").astype(jnp.int32).reshape(1)
    own, *sent = call(
        functools.partial(mix_kernel, mp_count),
        (struct((rows, width), F32),) + (struct((rows, width), BF16),) * (mp_count - 1),
        scratch=[
            pltpu.VMEM((rows, full), F32),
            pltpu.VMEM((rows, full), F32),
        ],
        mib=16,
        in_specs=[SMEM_SPEC] + [VMEM_SPEC] * (5 + mp_count),
    )(position, joined_whole, whole, *w_blocks, ffn_key, ffn_value, ln2_gain.reshape(1, full))
    merged = own
    for step, item in enumerate(sent):
        merged = merged + swapped(item, "mp", step + 1).astype(F32)
    return merged.astype(BF16)


def solution(mesh):
    in_specs = (
        P("seq"),
        P("seq", "mp"),
        P("seq", "mp"),
        P(None, "mp"),
        P(),
        P(),
        P(),
        P(None, "mp"),
        P(None, "mp"),
        P(None, "mp"),
        P(),
        P("mp"),
        P(None, "mp"),
        P(),
        P("mp"),
        P(None, "mp"),
        P("mp"),
        P("mp", None),
        P(None, "mp"),
        P("mp", None),
    )
    out_specs = P("seq", "mp")
    return jax.shard_map(
        on_device, mesh=mesh, in_specs=in_specs, out_specs=out_specs, check_vma=False
    )
```

```python
import functools

import jax
import jax.numpy as jnp
from jax import lax
from jax.experimental import pallas as pl
from jax.experimental.pallas import tpu as pltpu
from jax.sharding import PartitionSpec as P

HEAD = 64
DECAY_SCALE = 0.606531
NORM_EPS = 1e-05
GROUP_EPS = 0.00064
UNIT_EPS = 1e-06
F32 = jnp.float32
BF16 = jnp.bfloat16
MIB = 1024 * 1024
VMEM_SPEC = pl.BlockSpec(memory_space=pltpu.VMEM)
SMEM_SPEC = pl.BlockSpec(memory_space=pltpu.SMEM)


def mm(left, right):
    return jnp.dot(left, right, preferred_element_type=F32)


def mm_rows(left, right):
    return lax.dot_general(left, right, (((1,), (1,)), ((), ())), preferred_element_type=F32)


def mm_cols(left, right):
    return lax.dot_general(left, right, (((0,), (0,)), ((), ())), preferred_element_type=F32)


def halves(value):
    high = value.astype(BF16)
    return high, (value - high.astype(F32)).astype(BF16)


def head_sum(value, ones):
    high, low = halves(value)
    return mm(high, ones) + mm(low, ones)


def ids_of(shape, dim):
    return lax.broadcasted_iota(jnp.int32, shape, dim)


def block_ones(width):
    same = ids_of((width, width), 0) // HEAD == ids_of((width, width), 1) // HEAD
    return same


def spread(packed, same_head):
    tiled = jnp.concatenate([packed] * (packed.shape[1] // HEAD), axis=0)
    return jnp.where(same_head, tiled, jnp.zeros_like(tiled))


def layer_norm(values, gain):
    row_mean = jnp.mean(values, axis=-1, keepdims=True)
    centered = values - row_mean
    variance = jnp.mean(centered * centered, axis=-1, keepdims=True)
    return centered * lax.rsqrt(variance + NORM_EPS) * gain


def embed_kernel(ids_ref, fwd_ref, embed_ref, strand_ref, other_ref):
    rows = fwd_ref.shape[0]
    ids = ids_ref[...]
    letters = ids_of((embed_ref.shape[0], rows), 0)
    embed = embed_ref[...]

    def looked_up(values):
        onehot = (values == letters).astype(F32)
        return lax.dot_general(
            onehot,
            embed,
            (((0,), (0,)), ((), ())),
            precision=lax.Precision.HIGHEST,
            preferred_element_type=F32,
        )

    strand_ref[...] = (fwd_ref[...].astype(F32) + looked_up(ids)).astype(BF16)
    other_ref[...] = looked_up(3 - ids)


def strands_kernel(rc_ref, strand_ref, other_ref, out_ref):
    rows = rc_ref.shape[0]
    out_ref[0] = strand_ref[...]
    flip = (ids_of((rows, rows), 0) + ids_of((rows, rows), 1) == rows - 1).astype(F32)
    out_ref[1] = (mm(flip.astype(BF16), rc_ref[...]) + other_ref[...]).astype(BF16)


def inverse_of(pulls, rows):
    row_ids, col_ids = ids_of((rows, rows), 0), ids_of((rows, rows), 1)
    eye = (row_ids == col_ids).astype(F32)
    size = 1
    inverses = None
    while size < rows:
        within = (row_ids // (2 * size) == col_ids // (2 * size)) & (row_ids // size != col_ids // size)
        parts = [jnp.where(within, pull, 0.0) for pull in pulls]
        if size == 1:
            inverses = [eye + part for part in parts]
        else:
            lows = [inverse.astype(BF16) for inverse in inverses]
            products = [mm(part.astype(BF16), low).astype(BF16) for part, low in zip(parts, lows)]
            inverses = [inverse + mm(low, product) for inverse, low, product in zip(inverses, lows, products)]
        size *= 2
    return inverses


def gates(low, w_d2, w_c2, d_base, c_base):
    rank, width = w_d2.shape
    low = jnp.where(ids_of(low.shape, 1) < rank, jnp.tanh(low), low).astype(BF16)
    zero = jnp.zeros((rank, width), BF16)
    both = jnp.concatenate(
        [jnp.concatenate([w_d2, zero], axis=1), jnp.concatenate([zero, w_c2], axis=1)], axis=0
    )
    result = mm(low, both)
    log_decay = -DECAY_SCALE * jax.nn.sigmoid(d_base + result[:, :width])
    return log_decay, jax.nn.sigmoid(c_base + result[:, width:])


def project_kernel(x_ref, gain_ref, mixing_ref, w_k, w_v, w_d1, w_c1, w_d2, w_c2, d_base, c_base, *refs):
    outs, (rows_ref, normed, low_ref, edge_ref, mixed, shifts) = refs[:5], refs[5:]
    prev_ref, insert_ref, key_ref, value_ref, here_ref = outs
    strands, rows, _ = x_ref.shape
    shape = outs[0].shape
    pad = 8
    gain = gain_ref[...]
    lows = [(w_d1[...].astype(F32), mixing_ref[3:4]), (w_c1[...].astype(F32), mixing_ref[4:5])]
    parts = [weight * (1.0 - share) for weight, share in lows] + [weight * share for weight, share in lows]
    low_ref[...] = jnp.concatenate(parts, axis=0).astype(BF16)
    half = low_ref.shape[0] // 2
    gated = {}
    for s in range(strands):
        values = layer_norm(x_ref[s].astype(F32), gain)
        zero = jnp.zeros_like(values[:1])
        normed[s, pad : pad + rows, :] = values
        normed[s, pad - 1 : pad, :] = zero
        normed[s, pad + rows : pad + rows + 1, :] = zero
        edge_ref[s : s + 1, :] = values[:1]
        edge_ref[strands + s : strands + s + 1, :] = values[rows - 1 :]
        low = mm_rows(values.astype(BF16), low_ref[...])
        shifts[s, pad : pad + rows, :] = low[:, half:]
        shifts[s, pad - 1 : pad, :] = zero[:, :half]
        shifts[s, pad + rows : pad + rows + 1, :] = zero[:, :half]
        for d in range(2):
            shift = pad - 1 + 2 * d
            g = d * strands + s
            gated[g] = gates(
                low[:, :half] + shifts[s, shift : shift + rows, :], w_d2[...], w_c2[...], d_base[...], c_base[...]
            )
    blend(normed, mixing_ref, (1, 2), rows, mixed)
    keys = mm(mixed[0], w_k[...])
    value_ref[...] = mm(mixed[1], w_v[...]).reshape(shape)
    ones = block_ones(shape[2]).astype(F32).astype(BF16)
    order = ids_of((rows, rows), 0) - ids_of((rows, rows), 1)
    row_ids = ids_of(shape[1:], 0)
    for g in range(shape[0]):
        d = g // strands
        edge = d * (rows - 1)
        key = keys[g * rows : (g + 1) * rows]
        log_decay, rate = gated[g]
        unit = key * lax.rsqrt(head_sum(key * key, ones) + UNIT_EPS)
        log_decay = jnp.where(row_ids == edge, 0.0, log_decay)
        tri = ((order if d == 0 else -order) >= 0).astype(F32).astype(BF16)
        high, low = halves(log_decay)
        totals = mm(tri, high) + mm(tri, low)
        middle = totals[rows // 2 : rows // 2 + 1]
        there = jnp.exp(middle - totals)
        prev_ref[g] = -unit * jnp.exp(totals - log_decay - middle)
        insert_ref[g] = rate * unit * there
        key_ref[g] = key * there
        here_ref[g] = jnp.exp(totals - middle)
        final = rows - 1 - edge
        rows_ref[g, 0:1] = there[edge : edge + 1]
        rows_ref[g, 1:2] = middle
        rows_ref[g, 2:3] = totals[final : final + 1]


def blend(normed, mixing_ref, indices, rows, mixed):
    strands = normed.shape[0]
    step, pad = 16, 8
    for s in range(strands):
        for start in range(0, rows, step):
            center = normed[s, pad + start : pad + start + step, :]
            for d in range(2):
                shift = pad + start - 1 + 2 * d
                change = normed[s, shift : shift + step, :] - center
                place = (d * strands + s) * rows + start
                for slot, index in enumerate(indices):
                    weight = mixing_ref[index : index + 1, :]
                    mixed[slot, place : place + step, :] = (center + change * weight).astype(BF16)


def receptance_kernel(direction_ref, normed, mixing_ref, sent_edge_ref, kept_edge_ref, w_r, out_ref, mixed):
    groups, rows, _ = out_ref.shape
    blend(normed, mixing_ref, (0,), rows, mixed)
    out_ref[...] = mm(mixed[0], w_r[...]).reshape(out_ref.shape)
    edges = [sent_edge_ref[...], kept_edge_ref[...]]
    swap = direction_ref[0] == 1
    edges = [jnp.where(swap, edges[1 - d], edges[d]) for d in range(2)]
    edges = mm(jnp.concatenate(edges, axis=0).astype(BF16), w_r[...])
    for g in range(groups):
        row = 0 if g < groups // 2 else rows - 1
        out_ref[g, row : row + 1] = edges[g : g + 1]


def masked_heads(value, lane_head, heads):
    return jnp.concatenate([jnp.where(lane_head == h, value, 0.0).astype(BF16) for h in range(heads)], axis=0)


def chunk_kernel(direction_ref, *refs):
    prev_ref, insert_ref, key_ref, value_ref, rows_ref = refs[:5]
    halo_ref, edge_ref, low_ref, gain_ref, mixing_ref, w_k, w_v, *gate_refs = refs[5:16]
    state_ref, parts_ref, start_ref, read_edge_ref = refs[16:]
    strands, _, rows, width = parts_ref.shape
    heads = width // HEAD
    d = direction_ref[0]
    center = jnp.where(d == 1, edge_ref[strands:], edge_ref[:strands])
    halo = layer_norm(halo_ref[...].astype(F32), gain_ref[...])
    change = halo - center

    def mix(index):
        return (center + change * mixing_ref[index : index + 1, :]).astype(BF16)

    low = mm_rows(jnp.concatenate([center, halo], axis=0).astype(BF16), low_ref[...])
    half = low.shape[1] // 2
    low = low[:strands, :half] + low[strands:, half:]
    edge_key, edge_value = mm(mix(1), w_k[...]), mm(mix(2), w_v[...])
    edge_decay, edge_rate = gates(low, *[ref[...] for ref in gate_refs])
    read_edge_ref[...] = center + change * mixing_ref[0:1, :]
    edge_row = d * (rows - 1)
    at_edge = ids_of((rows, width), 0) == edge_row
    order = (ids_of((rows, rows), 0) - ids_of((rows, rows), 1)) * (1 - 2 * d)
    strict = order > 0
    same = block_ones(width)
    ones = same.astype(F32).astype(BF16)
    lane_head = ids_of((1, width), 1) // HEAD
    edge_unit = edge_key * lax.rsqrt(head_sum(edge_key * edge_key, ones) + UNIT_EPS)

    def of_heads(value):
        return masked_heads(value, lane_head, heads)

    def prepared(s):
        g = d * strands + s

        def patched(ref, row):
            return jnp.where(at_edge, row, ref[g])

        one = slice(s, s + 1)
        there, middle, final = [rows_ref[g, i : i + 1] for i in range(3)]
        from_start = jnp.exp(middle + edge_decay[one])
        to_end = jnp.exp(final - middle)
        final = final + edge_decay[one]
        left_prev = patched(prev_ref, -edge_unit[one] * jnp.exp(-middle - edge_decay[one]))
        right_insert = patched(insert_ref, edge_rate[one] * edge_unit[one] * there)
        right_key = patched(key_ref, edge_key[one] * there)
        value = patched(value_ref, edge_value[one])
        left = left_prev.astype(BF16)
        insert_pulls, key_pulls = [], []
        for h in range(heads):
            mask = lane_head == h
            right = jnp.concatenate(
                [jnp.where(mask, right_insert, 0.0), jnp.where(mask, right_key, 0.0)], axis=0
            ).astype(BF16)
            scores = mm_rows(left, right)
            insert_pulls.append(jnp.where(strict, scores[:, :rows], 0.0))
            key_pulls.append(jnp.where(strict, scores[:, rows:], 0.0).astype(BF16))
        value_pull = mm(jnp.concatenate(key_pulls, axis=1), of_heads(value))
        value = value.astype(BF16)
        start_ref[s] = jnp.broadcast_to(from_start, start_ref.shape[1:])
        parts_ref[s, 0] = right_insert.astype(BF16)
        parts_ref[s, 1] = right_key.astype(BF16)
        parts_ref[s, 2] = value
        tail_insert = (right_insert * to_end).astype(BF16)
        tail_key = (right_key * to_end).astype(BF16)
        solved_for = jnp.concatenate([of_heads(value_pull), of_heads(left_prev * from_start)], axis=1)
        end = mm_cols(tail_key, value)
        return insert_pulls, (solved_for, tail_insert, end, jnp.exp(final))

    prepared_all = [prepared(s) for s in range(strands)]
    inverses = inverse_of([pull for pulls, _ in prepared_all for pull in pulls], rows)
    for s, (_, (solved_for, tail_insert, end, kept)) in enumerate(prepared_all):
        own = inverses[s * heads : (s + 1) * heads]
        inverse = jnp.concatenate([item.astype(BF16) for item in own], axis=1)
        solved = mm(inverse, solved_for).astype(BF16)
        parts_ref[s, 3] = solved[:, :width]
        parts_ref[s, 4] = solved[:, width:]
        added = mm_cols(tail_insert, solved)
        ends = jnp.where(same, end + added[:, :width], 0.0)
        maps = jnp.where(same, added[:, width:], 0.0)
        end = sum(ends[h * HEAD : (h + 1) * HEAD] for h in range(heads))
        across = sum(maps[h * HEAD : (h + 1) * HEAD] for h in range(heads))
        diagonal = ids_of((HEAD, width), 0) == ids_of((HEAD, width), 1) % HEAD
        across = across + jnp.where(diagonal, kept, 0.0)
        state_ref[s] = jnp.concatenate([end, across], axis=0).astype(BF16)


def read_kernel(
    direction_ref, receptances, here_ref, sent_ref, kept_ref, sent_start_ref, kept_start_ref, local_ref, map_ref
):
    strands, _, rows, width = sent_ref.shape
    heads = width // HEAD
    lane_head = ids_of((1, width), 1) // HEAD
    for role, (parts_ref, start_ref) in enumerate(((sent_ref, sent_start_ref), (kept_ref, kept_start_ref))):
        d = (direction_ref[0] + role) % 2
        inclusive = (ids_of((rows, rows), 0) - ids_of((rows, rows), 1)) * (1 - 2 * d) >= 0

        def group(s, carry):
            insert, key, value, pull, start = [parts_ref[s, i] for i in range(5)]
            left = receptances[d * strands + s] * here_ref[d * strands + s]
            here = left.astype(BF16)
            reads = []
            for source in (insert, key):
                scores = mm_rows(here, masked_heads(source, lane_head, heads))
                parts = [scores[:, h * rows : (h + 1) * rows] for h in range(heads)]
                reads.append(jnp.concatenate([jnp.where(inclusive, p, 0.0).astype(BF16) for p in parts], axis=1))
            pull, start, value = [
                masked_heads(item, lane_head, heads) for item in (pull, start, value)
            ]
            g = role * strands + s
            local_ref[g] = mm(reads[0], pull) + mm(reads[1], value)
            map_ref[g] = left * start_ref[s, 0:1] + mm(reads[0], start)
            return carry

        lax.fori_loop(0, strands, group, 0)


def composed(later, earlier, same_head, state_only=False):
    across = later[HEAD:].astype(BF16)
    state = mm(across, spread(earlier[:HEAD].astype(BF16), same_head)) + later[:HEAD].astype(F32)
    if state_only:
        return state
    return jnp.concatenate([state, mm(across, spread(earlier[HEAD:].astype(BF16), same_head))], axis=0)


def pair_kernel(keep_ref, from_ref, pair_ref):
    same_head = block_ones(keep_ref.shape[2])
    for s in range(keep_ref.shape[0]):
        pair_ref[s] = composed(keep_ref[s], from_ref[s], same_head).astype(BF16)


def advance_kernel(has_prefix, later_ref, total_ref, from_ref, *refs):
    *prefix_ref, wide_ref, next_ref = refs
    state_only = next_ref.shape[1] == HEAD
    same_head = block_ones(total_ref.shape[2])
    later = later_ref[0] == 1
    shape = total_ref.shape[1:]
    within = (ids_of(shape, 0) - HEAD) == ids_of(shape, 1) % HEAD
    for s in range(total_ref.shape[0]):
        own, other = total_ref[s], from_ref[s]
        total = composed(jnp.where(later, own, other), jnp.where(later, other, own), same_head, state_only)
        next_ref[s] = total.astype(BF16)
        ahead = jnp.where(later, other.astype(F32), within.astype(F32))
        if has_prefix:
            ahead = composed(prefix_ref[0][s], ahead, same_head)
        wide_ref[s] = ahead


def entry_kernel(has_prefix, later_ref, from_ref, *refs):
    *prefix_ref, entry_ref = refs
    same_head = block_ones(entry_ref.shape[2])
    for s in range(entry_ref.shape[0]):
        other = from_ref[s]
        ahead = jnp.where(later_ref[0] == 1, other, jnp.zeros_like(other))
        if has_prefix:
            ahead = composed(prefix_ref[0][s], ahead, same_head, True)
        entry_ref[s] = ahead.astype(BF16)


def normed_heads(role, states, local_ref, map_ref):
    strands, width = len(states), local_ref.shape[2]
    same_head = block_ones(width)
    ones = same_head.astype(F32).astype(BF16)
    for s, state in enumerate(states):
        g = role * strands + s
        high, low = halves(map_ref[g])
        held, rest = [spread(item, same_head) for item in halves(state.astype(F32))]
        wkv = local_ref[g] + mm(high, held) + (mm(low, held) + mm(high, rest))
        centered = wkv - head_sum(wkv, ones) * (1.0 / HEAD)
        variance = head_sum(centered * centered, ones) * (1.0 / HEAD)
        yield centered * lax.rsqrt(variance + GROUP_EPS)


def kept_kernel(entry_ref, from_ref, local_ref, map_ref, out_ref):
    same_head = block_ones(out_ref.shape[2])
    states = [composed(from_ref[s], entry_ref[s], same_head, True) for s in range(out_ref.shape[0])]
    for s, result in enumerate(normed_heads(1, states, local_ref, map_ref)):
        out_ref[s] = result


def finish_kernel(other_ref, kept_ref, local_ref, map_ref, gain_ref, out_ref):
    states = [other_ref[s] for s in range(out_ref.shape[0])]
    for s, result in enumerate(normed_heads(0, states, local_ref, map_ref)):
        out_ref[s] = ((result + kept_ref[s]) * gain_ref[...]).astype(BF16)


def mix_kernel(blocks, index_ref, joined_ref, x_ref, *refs):
    w_refs, (up_ref, down_ref, gain_ref, own_ref) = refs[:blocks], refs[blocks : blocks + 4]
    *sent_refs, partial, total = refs[blocks + 4 :]
    strands, rows, _ = x_ref.shape
    width = own_ref.shape[1]
    gain = gain_ref[...]
    me = index_ref[0]
    attention = 0.0
    for step, w_ref in enumerate(w_refs):
        start = pl.multiple_of((me ^ step) * width, width)
        joined = jnp.concatenate([joined_ref[s, :, pl.ds(start, width)] for s in range(strands)], axis=0)
        attention = attention + mm(joined, w_ref[...])
    residuals = [x_ref[s].astype(F32) + attention[s * rows : (s + 1) * rows] for s in range(strands)]
    inner = jnp.concatenate([layer_norm(item, gain).astype(BF16) for item in residuals], axis=0)
    active = jnp.square(jnp.maximum(mm(inner, up_ref[...]), 0.0)).astype(BF16).astype(F32)
    added = sum(active[s * rows : (s + 1) * rows] for s in range(strands)).astype(BF16)
    partial[...] = mm(added, down_ref[...])
    total[...] = sum(residuals)

    def part(ref, which):
        return ref[:, pl.ds(pl.multiple_of(which * width, width), width)]

    own_ref[...] = part(total, me) + part(partial, me)
    for step, ref in enumerate(sent_refs):
        ref[...] = part(partial, me ^ (step + 1)).astype(BF16)


def call(kernel, out_shape, scratch=(), mib=12, us=10, **kwargs):
    return pl.pallas_call(
        kernel,
        out_shape=out_shape,
        scratch_shapes=list(scratch),
        cost_estimate=pl.CostEstimate(flops=us * 10**9, bytes_accessed=us * 10**6, transcendentals=0),
        compiler_params=pltpu.CompilerParams(vmem_limit_bytes=mib * MIB),
        **kwargs,
    )


def swapped(value, axis, mask):
    return lax.ppermute(value, axis, [(i, i ^ mask) for i in range(lax.axis_size(axis))])


def on_device(
    ids,
    hidden_fwd,
    hidden_rc,
    embed,
    ln1_gain,
    ln2_gain,
    mixing,
    w_receptance,
    w_key,
    w_value,
    decay_first_weight,
    decay_base,
    decay_second_weight,
    context_rate_first_weight,
    iclr_base,
    context_rate_second_weight,
    group_gain,
    w_output,
    ffn_key,
    ffn_value,
):
    rows, width = hidden_fwd.shape
    seq_count, mp_count = lax.axis_size("seq"), lax.axis_size("mp")
    strands, full = 2, ffn_key.shape[0]
    struct = jax.ShapeDtypeStruct

    mirror = [(i, seq_count - 1 - i) for i in range(seq_count)]
    rc_here = lax.ppermute(hidden_rc, "seq", mirror)
    params = (
        ln1_gain.reshape(1, full),
        mixing,
        w_key,
        w_value,
        decay_first_weight.T,
        context_rate_first_weight.T,
        decay_second_weight,
        context_rate_second_weight,
        decay_base.reshape(1, width),
        iclr_base.reshape(1, width),
    )
    strand, other = call(
        embed_kernel, (struct((rows, width), BF16), struct((rows, width), F32)), us=10, mib=4
    )(ids.reshape(1, rows), hidden_fwd, embed)
    rc_here, strand, other = lax.optimization_barrier((rc_here, strand, other))
    local = call(strands_kernel, struct((strands, rows, width), BF16), us=10, mib=4)(rc_here, strand, other)
    whole = lax.all_gather(local, "mp", axis=2, tiled=True)
    place = lax.axis_index("seq").astype(jnp.int32)
    parity = place % 2
    first, last = whole[:, 0], whole[:, rows - 1]
    bridges = [(i, i + 1) for i in range(1, seq_count - 1, 2)]
    bridges += [(j, i) for i, j in bridges]
    far = lax.ppermute(jnp.where(parity == 1, last, first), "seq", bridges)
    parity = parity.reshape(1)

    groups = 2 * strands
    f32_lanes, bf16_lanes = struct((groups, rows, width), F32), struct((strands, rows, width), BF16)
    parts_struct = struct((strands, 5, rows, width), BF16)
    start_struct = struct((strands, 8, width), F32)
    state_struct = struct((strands, 2 * HEAD, width), BF16)
    entry_struct = struct((strands, HEAD, width), BF16)
    low_shape = (4 * decay_first_weight.shape[1], full)
    *lanes, here, spans, normed, low, edge = call(
        project_kernel,
        (f32_lanes,) * 5
        + (
            struct((groups, 8, width), F32),
            struct((strands, rows + 16, full), F32),
            struct(low_shape, BF16),
            struct((groups, full), F32),
        ),
        scratch=[
            pltpu.VMEM((2, groups * rows, full), BF16),
            pltpu.VMEM((strands, rows + 16, low_shape[0] // 2), F32),
        ],
    )(whole, *params)

    beside, _ = lax.optimization_barrier((jnp.where(parity == 1, first, last), edge))
    near = swapped(beside, "seq", 1)

    def chunk(direction, halo):
        return call(
            chunk_kernel,
            (state_struct, parts_struct, start_struct, struct((strands, full), F32)),
            in_specs=[SMEM_SPEC] + [VMEM_SPEC] * 16,
        )(direction, *lanes, spans, halo, edge, low, *params[:4], *params[6:])

    sent, sent_parts, sent_start, sent_edge = chunk(parity, far)
    from_partner = swapped(sent, "seq", 1)
    kept, kept_parts, kept_start, kept_edge = chunk(1 - parity, near)

    total = call(pair_kernel, state_struct, mib=4, us=1)(kept, from_partner)
    w_held, _ = lax.optimization_barrier((w_output, total))
    w_across = swapped(w_held, "mp", 2)
    kept_edge, _ = lax.optimization_barrier((kept_edge, total))
    receptances = call(
        receptance_kernel,
        f32_lanes,
        scratch=[pltpu.VMEM((1, groups * rows, full), BF16)],
        mib=6,
        us=3,
        in_specs=[SMEM_SPEC] + [VMEM_SPEC] * 5,
    )(parity, normed, mixing, sent_edge, kept_edge, w_receptance)
    prefix = []
    bits = range(1, seq_count.bit_length() - 1)
    for bit in bits:
        later = ((place >> bit) % 2 == place % 2).astype(jnp.int32).reshape(1)
        received = swapped(total, "seq", 1 << bit)
        if bit == bits[0]:
            received, receptances = lax.optimization_barrier((received, receptances))
        if bit == bits[-1]:
            break
        wide, total = call(
            functools.partial(advance_kernel, bool(prefix)),
            (struct(state_struct.shape, F32), entry_struct if bit + 1 == bits[-1] else state_struct),
            mib=4,
            us=1,
            in_specs=[SMEM_SPEC] + [VMEM_SPEC] * (2 + len(prefix)),
        )(later, total, received, *prefix)
        prefix = [wide]
    w_held, _ = lax.optimization_barrier((w_output, total))
    w_beside = swapped(w_held, "mp", 1)
    sent_parts, kept_parts, _ = lax.optimization_barrier((sent_parts, kept_parts, total))
    reads = call(
        read_kernel,
        (f32_lanes, f32_lanes),
        mib=6,
        in_specs=[SMEM_SPEC] + [VMEM_SPEC] * 6,
    )(parity, receptances, here, sent_parts, kept_parts, sent_start, kept_start)
    received, reads = lax.optimization_barrier((received, reads))
    entry = call(
        functools.partial(entry_kernel, bool(prefix)),
        entry_struct,
        mib=4,
        us=1,
        in_specs=[SMEM_SPEC] + [VMEM_SPEC] * (1 + len(prefix)),
    )(later, received, *prefix)
    other = swapped(entry, "seq", 1)
    kept_heads = call(kept_kernel, struct(bf16_lanes.shape, F32), mib=6, us=3)(entry, from_partner, *reads)
    w_across, other, kept_heads = lax.optimization_barrier((w_across, other, kept_heads))
    w_opposite = swapped(w_across, "mp", 1)
    joined = call(finish_kernel, bf16_lanes, mib=6)(other, kept_heads, *reads, group_gain.reshape(1, width))
    joined_whole = lax.all_gather(joined, "mp", axis=2, tiled=True)

    w_blocks = (w_output, w_beside, w_across, w_opposite)
    position = lax.axis_index("mp").astype(jnp.int32).reshape(1)
    own, *sent = call(
        functools.partial(mix_kernel, mp_count),
        (struct((rows, width), F32),) + (struct((rows, width), BF16),) * (mp_count - 1),
        scratch=[
            pltpu.VMEM((rows, full), F32),
            pltpu.VMEM((rows, full), F32),
        ],
        mib=16,
        in_specs=[SMEM_SPEC] + [VMEM_SPEC] * (5 + mp_count),
    )(position, joined_whole, whole, *w_blocks, ffn_key, ffn_value, ln2_gain.reshape(1, full))
    merged = own
    for step, item in enumerate(sent):
        merged = merged + swapped(item, "mp", step + 1).astype(F32)
    return merged.astype(BF16)


def solution(mesh):
    in_specs = (
        P("seq"),
        P("seq", "mp"),
        P("seq", "mp"),
        P(None, "mp"),
        P(),
        P(),
        P(),
        P(None, "mp"),
        P(None, "mp"),
        P(None, "mp"),
        P(),
        P("mp"),
        P(None, "mp"),
        P(),
        P("mp"),
        P(None, "mp"),
        P("mp"),
        P("mp", None),
        P(None, "mp"),
        P("mp", None),
    )
    out_specs = P("seq", "mp")
    return jax.shard_map(
        on_device, mesh=mesh, in_specs=in_specs, out_specs=out_specs, check_vma=False
    )
```

```python
import functools

import jax
import jax.numpy as jnp
from jax import lax
from jax.experimental import pallas as pl
from jax.experimental.pallas import tpu as pltpu
from jax.sharding import PartitionSpec as P

HEAD = 64
DECAY_SCALE = 0.606531
NORM_EPS = 1e-05
GROUP_EPS = 0.00064
UNIT_EPS = 1e-06
F32 = jnp.float32
BF16 = jnp.bfloat16
MIB = 1024 * 1024
VMEM_SPEC = pl.BlockSpec(memory_space=pltpu.VMEM)
SMEM_SPEC = pl.BlockSpec(memory_space=pltpu.SMEM)


def mm(left, right):
    return jnp.dot(left, right, preferred_element_type=F32)


def mm_rows(left, right):
    return lax.dot_general(left, right, (((1,), (1,)), ((), ())), preferred_element_type=F32)


def mm_cols(left, right):
    return lax.dot_general(left, right, (((0,), (0,)), ((), ())), preferred_element_type=F32)


def halves(value):
    high = value.astype(BF16)
    return high, (value - high.astype(F32)).astype(BF16)


def head_sum(value, ones):
    high, low = halves(value)
    return mm(high, ones) + mm(low, ones)


def ids_of(shape, dim):
    return lax.broadcasted_iota(jnp.int32, shape, dim)


def block_ones(width):
    same = ids_of((width, width), 0) // HEAD == ids_of((width, width), 1) // HEAD
    return same


def spread(packed, same_head):
    tiled = jnp.concatenate([packed] * (packed.shape[1] // HEAD), axis=0)
    return jnp.where(same_head, tiled, jnp.zeros_like(tiled))


def layer_norm(values, gain):
    row_mean = jnp.mean(values, axis=-1, keepdims=True)
    centered = values - row_mean
    variance = jnp.mean(centered * centered, axis=-1, keepdims=True)
    return centered * lax.rsqrt(variance + NORM_EPS) * gain


def embed_kernel(ids_ref, fwd_ref, embed_ref, strand_ref, other_ref):
    rows = fwd_ref.shape[0]
    ids = ids_ref[...]
    letters = ids_of((embed_ref.shape[0], rows), 0)
    embed = embed_ref[...]

    def looked_up(values):
        onehot = (values == letters).astype(F32)
        return lax.dot_general(
            onehot,
            embed,
            (((0,), (0,)), ((), ())),
            precision=lax.Precision.HIGHEST,
            preferred_element_type=F32,
        )

    strand_ref[...] = (fwd_ref[...].astype(F32) + looked_up(ids)).astype(BF16)
    other_ref[...] = looked_up(3 - ids)


def strands_kernel(rc_ref, strand_ref, other_ref, out_ref):
    rows = rc_ref.shape[0]
    out_ref[0] = strand_ref[...]
    flip = (ids_of((rows, rows), 0) + ids_of((rows, rows), 1) == rows - 1).astype(F32)
    out_ref[1] = (mm(flip.astype(BF16), rc_ref[...]) + other_ref[...]).astype(BF16)


def inverse_of(pulls, rows):
    row_ids, col_ids = ids_of((rows, rows), 0), ids_of((rows, rows), 1)
    eye = (row_ids == col_ids).astype(F32)
    size = 1
    inverses = None
    while size < rows:
        within = (row_ids // (2 * size) == col_ids // (2 * size)) & (row_ids // size != col_ids // size)
        parts = [jnp.where(within, pull, 0.0) for pull in pulls]
        if size == 1:
            inverses = [eye + part for part in parts]
        else:
            lows = [inverse.astype(BF16) for inverse in inverses]
            products = [mm(part.astype(BF16), low).astype(BF16) for part, low in zip(parts, lows)]
            inverses = [inverse + mm(low, product) for inverse, low, product in zip(inverses, lows, products)]
        size *= 2
    return inverses


def gates(low, w_d2, w_c2, d_base, c_base):
    rank, width = w_d2.shape
    low = jnp.where(ids_of(low.shape, 1) < rank, jnp.tanh(low), low).astype(BF16)
    zero = jnp.zeros((rank, width), BF16)
    both = jnp.concatenate(
        [jnp.concatenate([w_d2, zero], axis=1), jnp.concatenate([zero, w_c2], axis=1)], axis=0
    )
    result = mm(low, both)
    log_decay = -DECAY_SCALE * jax.nn.sigmoid(d_base + result[:, :width])
    return log_decay, jax.nn.sigmoid(c_base + result[:, width:])


def project_kernel(x_ref, gain_ref, mixing_ref, w_k, w_v, w_d1, w_c1, w_d2, w_c2, d_base, c_base, *refs):
    outs, (rows_ref, normed, low_ref, edge_ref, mixed, shifts) = refs[:5], refs[5:]
    prev_ref, insert_ref, key_ref, value_ref, here_ref = outs
    strands, rows, _ = x_ref.shape
    shape = outs[0].shape
    pad = 8
    gain = gain_ref[...]
    lows = [(w_d1[...].astype(F32), mixing_ref[3:4]), (w_c1[...].astype(F32), mixing_ref[4:5])]
    parts = [weight * (1.0 - share) for weight, share in lows] + [weight * share for weight, share in lows]
    low_ref[...] = jnp.concatenate(parts, axis=0).astype(BF16)
    half = low_ref.shape[0] // 2
    gated = {}
    for s in range(strands):
        values = layer_norm(x_ref[s].astype(F32), gain)
        zero = jnp.zeros_like(values[:1])
        normed[s, pad : pad + rows, :] = values
        normed[s, pad - 1 : pad, :] = zero
        normed[s, pad + rows : pad + rows + 1, :] = zero
        edge_ref[s : s + 1, :] = values[:1]
        edge_ref[strands + s : strands + s + 1, :] = values[rows - 1 :]
        low = mm_rows(values.astype(BF16), low_ref[...])
        shifts[s, pad : pad + rows, :] = low[:, half:]
        shifts[s, pad - 1 : pad, :] = zero[:, :half]
        shifts[s, pad + rows : pad + rows + 1, :] = zero[:, :half]
        for d in range(2):
            shift = pad - 1 + 2 * d
            g = d * strands + s
            gated[g] = gates(
                low[:, :half] + shifts[s, shift : shift + rows, :], w_d2[...], w_c2[...], d_base[...], c_base[...]
            )
    blend(normed, mixing_ref, (1, 2), rows, mixed)
    keys = mm(mixed[0], w_k[...])
    value_ref[...] = mm(mixed[1], w_v[...]).reshape(shape)
    ones = block_ones(shape[2]).astype(F32).astype(BF16)
    order = ids_of((rows, rows), 0) - ids_of((rows, rows), 1)
    row_ids = ids_of(shape[1:], 0)
    for g in range(shape[0]):
        d = g // strands
        edge = d * (rows - 1)
        key = keys[g * rows : (g + 1) * rows]
        log_decay, rate = gated[g]
        unit = key * lax.rsqrt(head_sum(key * key, ones) + UNIT_EPS)
        log_decay = jnp.where(row_ids == edge, 0.0, log_decay)
        tri = ((order if d == 0 else -order) >= 0).astype(F32).astype(BF16)
        high, low = halves(log_decay)
        totals = mm(tri, high) + mm(tri, low)
        middle = totals[rows // 2 : rows // 2 + 1]
        there = jnp.exp(middle - totals)
        prev_ref[g] = -unit * jnp.exp(totals - log_decay - middle)
        insert_ref[g] = rate * unit * there
        key_ref[g] = key * there
        here_ref[g] = jnp.exp(totals - middle)
        final = rows - 1 - edge
        rows_ref[g, 0:1] = there[edge : edge + 1]
        rows_ref[g, 1:2] = middle
        rows_ref[g, 2:3] = totals[final : final + 1]


def blend(normed, mixing_ref, indices, rows, mixed):
    strands = normed.shape[0]
    step, pad = 16, 8
    for s in range(strands):
        for start in range(0, rows, step):
            center = normed[s, pad + start : pad + start + step, :]
            for d in range(2):
                shift = pad + start - 1 + 2 * d
                change = normed[s, shift : shift + step, :] - center
                place = (d * strands + s) * rows + start
                for slot, index in enumerate(indices):
                    weight = mixing_ref[index : index + 1, :]
                    mixed[slot, place : place + step, :] = (center + change * weight).astype(BF16)


def receptance_kernel(direction_ref, normed, mixing_ref, sent_edge_ref, kept_edge_ref, w_r, out_ref, mixed):
    groups, rows, _ = out_ref.shape
    blend(normed, mixing_ref, (0,), rows, mixed)
    out_ref[...] = mm(mixed[0], w_r[...]).reshape(out_ref.shape)
    edges = [sent_edge_ref[...], kept_edge_ref[...]]
    swap = direction_ref[0] == 1
    edges = [jnp.where(swap, edges[1 - d], edges[d]) for d in range(2)]
    edges = mm(jnp.concatenate(edges, axis=0).astype(BF16), w_r[...])
    for g in range(groups):
        row = 0 if g < groups // 2 else rows - 1
        out_ref[g, row : row + 1] = edges[g : g + 1]


def masked_heads(value, lane_head, heads):
    return jnp.concatenate([jnp.where(lane_head == h, value, 0.0).astype(BF16) for h in range(heads)], axis=0)


def chunk_kernel(direction_ref, *refs):
    prev_ref, insert_ref, key_ref, value_ref, rows_ref = refs[:5]
    halo_ref, edge_ref, low_ref, gain_ref, mixing_ref, w_k, w_v, *gate_refs = refs[5:16]
    state_ref, parts_ref, start_ref, read_edge_ref = refs[16:]
    strands, _, rows, width = parts_ref.shape
    heads = width // HEAD
    d = direction_ref[0]
    center = jnp.where(d == 1, edge_ref[strands:], edge_ref[:strands])
    halo = layer_norm(halo_ref[...].astype(F32), gain_ref[...])
    change = halo - center

    def mix(index):
        return (center + change * mixing_ref[index : index + 1, :]).astype(BF16)

    low = mm_rows(jnp.concatenate([center, halo], axis=0).astype(BF16), low_ref[...])
    half = low.shape[1] // 2
    low = low[:strands, :half] + low[strands:, half:]
    edge_key, edge_value = mm(mix(1), w_k[...]), mm(mix(2), w_v[...])
    edge_decay, edge_rate = gates(low, *[ref[...] for ref in gate_refs])
    read_edge_ref[...] = center + change * mixing_ref[0:1, :]
    edge_row = d * (rows - 1)
    at_edge = ids_of((rows, width), 0) == edge_row
    order = (ids_of((rows, rows), 0) - ids_of((rows, rows), 1)) * (1 - 2 * d)
    strict = order > 0
    same = block_ones(width)
    ones = same.astype(F32).astype(BF16)
    lane_head = ids_of((1, width), 1) // HEAD
    edge_unit = edge_key * lax.rsqrt(head_sum(edge_key * edge_key, ones) + UNIT_EPS)

    def of_heads(value):
        return masked_heads(value, lane_head, heads)

    def prepared(s):
        g = d * strands + s

        def patched(ref, row):
            return jnp.where(at_edge, row, ref[g])

        one = slice(s, s + 1)
        there, middle, final = [rows_ref[g, i : i + 1] for i in range(3)]
        from_start = jnp.exp(middle + edge_decay[one])
        to_end = jnp.exp(final - middle)
        final = final + edge_decay[one]
        left_prev = patched(prev_ref, -edge_unit[one] * jnp.exp(-middle - edge_decay[one]))
        right_insert = patched(insert_ref, edge_rate[one] * edge_unit[one] * there)
        right_key = patched(key_ref, edge_key[one] * there)
        value = patched(value_ref, edge_value[one])
        left = left_prev.astype(BF16)
        insert_pulls, key_pulls = [], []
        for h in range(heads):
            mask = lane_head == h
            right = jnp.concatenate(
                [jnp.where(mask, right_insert, 0.0), jnp.where(mask, right_key, 0.0)], axis=0
            ).astype(BF16)
            scores = mm_rows(left, right)
            insert_pulls.append(jnp.where(strict, scores[:, :rows], 0.0))
            key_pulls.append(jnp.where(strict, scores[:, rows:], 0.0).astype(BF16))
        value_pull = mm(jnp.concatenate(key_pulls, axis=1), of_heads(value))
        value = value.astype(BF16)
        start_ref[s] = jnp.broadcast_to(from_start, start_ref.shape[1:])
        parts_ref[s, 0] = right_insert.astype(BF16)
        parts_ref[s, 1] = right_key.astype(BF16)
        parts_ref[s, 2] = value
        tail_insert = (right_insert * to_end).astype(BF16)
        tail_key = (right_key * to_end).astype(BF16)
        solved_for = jnp.concatenate([of_heads(value_pull), of_heads(left_prev * from_start)], axis=1)
        end = mm_cols(tail_key, value)
        return insert_pulls, (solved_for, tail_insert, end, jnp.exp(final))

    prepared_all = [prepared(s) for s in range(strands)]
    inverses = inverse_of([pull for pulls, _ in prepared_all for pull in pulls], rows)
    for s, (_, (solved_for, tail_insert, end, kept)) in enumerate(prepared_all):
        own = inverses[s * heads : (s + 1) * heads]
        inverse = jnp.concatenate([item.astype(BF16) for item in own], axis=1)
        solved = mm(inverse, solved_for).astype(BF16)
        parts_ref[s, 3] = solved[:, :width]
        parts_ref[s, 4] = solved[:, width:]
        added = mm_cols(tail_insert, solved)
        ends = jnp.where(same, end + added[:, :width], 0.0)
        maps = jnp.where(same, added[:, width:], 0.0)
        end = sum(ends[h * HEAD : (h + 1) * HEAD] for h in range(heads))
        across = sum(maps[h * HEAD : (h + 1) * HEAD] for h in range(heads))
        diagonal = ids_of((HEAD, width), 0) == ids_of((HEAD, width), 1) % HEAD
        across = across + jnp.where(diagonal, kept, 0.0)
        state_ref[s] = jnp.concatenate([end, across], axis=0).astype(BF16)


def read_kernel(
    direction_ref, receptances, here_ref, sent_ref, kept_ref, sent_start_ref, kept_start_ref, local_ref, map_ref
):
    strands, _, rows, width = sent_ref.shape
    heads = width // HEAD
    lane_head = ids_of((1, width), 1) // HEAD
    for role, (parts_ref, start_ref) in enumerate(((sent_ref, sent_start_ref), (kept_ref, kept_start_ref))):
        d = (direction_ref[0] + role) % 2
        inclusive = (ids_of((rows, rows), 0) - ids_of((rows, rows), 1)) * (1 - 2 * d) >= 0

        def group(s, carry):
            insert, key, value, pull, start = [parts_ref[s, i] for i in range(5)]
            left = receptances[d * strands + s] * here_ref[d * strands + s]
            here = left.astype(BF16)
            reads = []
            for source in (insert, key):
                scores = mm_rows(here, masked_heads(source, lane_head, heads))
                parts = [scores[:, h * rows : (h + 1) * rows] for h in range(heads)]
                reads.append(jnp.concatenate([jnp.where(inclusive, p, 0.0).astype(BF16) for p in parts], axis=1))
            pull, start, value = [
                masked_heads(item, lane_head, heads) for item in (pull, start, value)
            ]
            g = role * strands + s
            local_ref[g] = mm(reads[0], pull) + mm(reads[1], value)
            map_ref[g] = left * start_ref[s, 0:1] + mm(reads[0], start)
            return carry

        lax.fori_loop(0, strands, group, 0)


def composed(later, earlier, same_head, state_only=False):
    across = later[HEAD:].astype(BF16)
    state = mm(across, spread(earlier[:HEAD].astype(BF16), same_head)) + later[:HEAD].astype(F32)
    if state_only:
        return state
    return jnp.concatenate([state, mm(across, spread(earlier[HEAD:].astype(BF16), same_head))], axis=0)


def pair_kernel(keep_ref, from_ref, pair_ref):
    same_head = block_ones(keep_ref.shape[2])
    for s in range(keep_ref.shape[0]):
        pair_ref[s] = composed(keep_ref[s], from_ref[s], same_head).astype(BF16)


def advance_kernel(has_prefix, later_ref, total_ref, from_ref, *refs):
    *prefix_ref, wide_ref, next_ref = refs
    state_only = next_ref.shape[1] == HEAD
    same_head = block_ones(total_ref.shape[2])
    later = later_ref[0] == 1
    shape = total_ref.shape[1:]
    within = (ids_of(shape, 0) - HEAD) == ids_of(shape, 1) % HEAD
    for s in range(total_ref.shape[0]):
        own, other = total_ref[s], from_ref[s]
        total = composed(jnp.where(later, own, other), jnp.where(later, other, own), same_head, state_only)
        next_ref[s] = total.astype(BF16)
        ahead = jnp.where(later, other.astype(F32), within.astype(F32))
        if has_prefix:
            ahead = composed(prefix_ref[0][s], ahead, same_head)
        wide_ref[s] = ahead


def entry_kernel(has_prefix, later_ref, from_ref, *refs):
    *prefix_ref, entry_ref = refs
    same_head = block_ones(entry_ref.shape[2])
    for s in range(entry_ref.shape[0]):
        other = from_ref[s]
        ahead = jnp.where(later_ref[0] == 1, other, jnp.zeros_like(other))
        if has_prefix:
            ahead = composed(prefix_ref[0][s], ahead, same_head, True)
        entry_ref[s] = ahead.astype(BF16)


def normed_heads(role, states, local_ref, map_ref):
    strands, width = len(states), local_ref.shape[2]
    same_head = block_ones(width)
    ones = same_head.astype(F32).astype(BF16)
    for s, state in enumerate(states):
        g = role * strands + s
        high, low = halves(map_ref[g])
        held, rest = [spread(item, same_head) for item in halves(state.astype(F32))]
        wkv = local_ref[g] + mm(high, held) + (mm(low, held) + mm(high, rest))
        centered = wkv - head_sum(wkv, ones) * (1.0 / HEAD)
        variance = head_sum(centered * centered, ones) * (1.0 / HEAD)
        yield centered * lax.rsqrt(variance + GROUP_EPS)


def kept_kernel(entry_ref, from_ref, local_ref, map_ref, out_ref):
    same_head = block_ones(out_ref.shape[2])
    states = [composed(from_ref[s], entry_ref[s], same_head, True) for s in range(out_ref.shape[0])]
    for s, result in enumerate(normed_heads(1, states, local_ref, map_ref)):
        out_ref[s] = result


def finish_kernel(other_ref, kept_ref, local_ref, map_ref, gain_ref, out_ref):
    states = [other_ref[s] for s in range(out_ref.shape[0])]
    for s, result in enumerate(normed_heads(0, states, local_ref, map_ref)):
        out_ref[s] = ((result + kept_ref[s]) * gain_ref[...]).astype(BF16)


def mix_kernel(blocks, index_ref, joined_ref, x_ref, *refs):
    w_refs, (up_ref, down_ref, gain_ref, own_ref) = refs[:blocks], refs[blocks : blocks + 4]
    *sent_refs, partial, total = refs[blocks + 4 :]
    strands, rows, _ = x_ref.shape
    width = own_ref.shape[1]
    gain = gain_ref[...]
    me = index_ref[0]
    attention = 0.0
    for step, w_ref in enumerate(w_refs):
        start = pl.multiple_of((me ^ step) * width, width)
        joined = jnp.concatenate([joined_ref[s, :, pl.ds(start, width)] for s in range(strands)], axis=0)
        attention = attention + mm(joined, w_ref[...])
    residuals = [x_ref[s].astype(F32) + attention[s * rows : (s + 1) * rows] for s in range(strands)]
    inner = jnp.concatenate([layer_norm(item, gain).astype(BF16) for item in residuals], axis=0)
    active = jnp.square(jnp.maximum(mm(inner, up_ref[...]), 0.0)).astype(BF16).astype(F32)
    added = sum(active[s * rows : (s + 1) * rows] for s in range(strands)).astype(BF16)
    partial[...] = mm(added, down_ref[...])
    total[...] = sum(residuals)

    def part(ref, which):
        return ref[:, pl.ds(pl.multiple_of(which * width, width), width)]

    own_ref[...] = part(total, me) + part(partial, me)
    for step, ref in enumerate(sent_refs):
        ref[...] = part(partial, me ^ (step + 1)).astype(BF16)


def call(kernel, out_shape, scratch=(), mib=12, us=10, **kwargs):
    return pl.pallas_call(
        kernel,
        out_shape=out_shape,
        scratch_shapes=list(scratch),
        cost_estimate=pl.CostEstimate(flops=us * 10**9, bytes_accessed=us * 10**6, transcendentals=0),
        compiler_params=pltpu.CompilerParams(vmem_limit_bytes=mib * MIB),
        **kwargs,
    )


def swapped(value, axis, mask):
    return lax.ppermute(value, axis, [(i, i ^ mask) for i in range(lax.axis_size(axis))])


def on_device(
    ids,
    hidden_fwd,
    hidden_rc,
    embed,
    ln1_gain,
    ln2_gain,
    mixing,
    w_receptance,
    w_key,
    w_value,
    decay_first_weight,
    decay_base,
    decay_second_weight,
    context_rate_first_weight,
    iclr_base,
    context_rate_second_weight,
    group_gain,
    w_output,
    ffn_key,
    ffn_value,
):
    rows, width = hidden_fwd.shape
    seq_count, mp_count = lax.axis_size("seq"), lax.axis_size("mp")
    strands, full = 2, ffn_key.shape[0]
    struct = jax.ShapeDtypeStruct

    mirror = [(i, seq_count - 1 - i) for i in range(seq_count)]
    rc_here = lax.ppermute(hidden_rc, "seq", mirror)
    params = (
        ln1_gain.reshape(1, full),
        mixing,
        w_key,
        w_value,
        decay_first_weight.T,
        context_rate_first_weight.T,
        decay_second_weight,
        context_rate_second_weight,
        decay_base.reshape(1, width),
        iclr_base.reshape(1, width),
    )
    strand, other = call(
        embed_kernel, (struct((rows, width), BF16), struct((rows, width), F32)), us=10, mib=4
    )(ids.reshape(1, rows), hidden_fwd, embed)
    rc_here, strand, other = lax.optimization_barrier((rc_here, strand, other))
    local = call(strands_kernel, struct((strands, rows, width), BF16), us=10, mib=4)(rc_here, strand, other)
    whole = lax.all_gather(local, "mp", axis=2, tiled=True)
    place = lax.axis_index("seq").astype(jnp.int32)
    parity = place % 2
    first, last = whole[:, 0], whole[:, rows - 1]
    bridges = [(i, i + 1) for i in range(1, seq_count - 1, 2)]
    bridges += [(j, i) for i, j in bridges]
    far = lax.ppermute(jnp.where(parity == 1, last, first), "seq", bridges)
    parity = parity.reshape(1)

    groups = 2 * strands
    f32_lanes, bf16_lanes = struct((groups, rows, width), F32), struct((strands, rows, width), BF16)
    parts_struct = struct((strands, 5, rows, width), BF16)
    start_struct = struct((strands, 8, width), F32)
    state_struct = struct((strands, 2 * HEAD, width), BF16)
    entry_struct = struct((strands, HEAD, width), BF16)
    low_shape = (4 * decay_first_weight.shape[1], full)
    *lanes, here, spans, normed, low, edge = call(
        project_kernel,
        (f32_lanes,) * 5
        + (
            struct((groups, 8, width), F32),
            struct((strands, rows + 16, full), F32),
            struct(low_shape, BF16),
            struct((groups, full), F32),
        ),
        scratch=[
            pltpu.VMEM((2, groups * rows, full), BF16),
            pltpu.VMEM((strands, rows + 16, low_shape[0] // 2), F32),
        ],
    )(whole, *params)

    beside, w_held, _ = lax.optimization_barrier((jnp.where(parity == 1, first, last), w_output, edge))
    w_across = swapped(w_held, "mp", 2)
    near = swapped(beside, "seq", 1)

    def chunk(direction, halo):
        return call(
            chunk_kernel,
            (state_struct, parts_struct, start_struct, struct((strands, full), F32)),
            in_specs=[SMEM_SPEC] + [VMEM_SPEC] * 16,
        )(direction, *lanes, spans, halo, edge, low, *params[:4], *params[6:])

    sent, sent_parts, sent_start, sent_edge = chunk(parity, far)
    from_partner = swapped(sent, "seq", 1)
    kept, kept_parts, kept_start, kept_edge = chunk(1 - parity, near)

    total = call(pair_kernel, state_struct, mib=4, us=1)(kept, from_partner)
    kept_edge, _ = lax.optimization_barrier((kept_edge, total))
    receptances = call(
        receptance_kernel,
        f32_lanes,
        scratch=[pltpu.VMEM((1, groups * rows, full), BF16)],
        mib=6,
        us=3,
        in_specs=[SMEM_SPEC] + [VMEM_SPEC] * 5,
    )(parity, normed, mixing, sent_edge, kept_edge, w_receptance)
    prefix = []
    bits = range(1, seq_count.bit_length() - 1)
    for bit in bits:
        later = ((place >> bit) % 2 == place % 2).astype(jnp.int32).reshape(1)
        received = swapped(total, "seq", 1 << bit)
        if bit == bits[0]:
            received, receptances = lax.optimization_barrier((received, receptances))
        if bit == bits[-1]:
            break
        wide, total = call(
            functools.partial(advance_kernel, bool(prefix)),
            (struct(state_struct.shape, F32), entry_struct if bit + 1 == bits[-1] else state_struct),
            mib=4,
            us=1,
            in_specs=[SMEM_SPEC] + [VMEM_SPEC] * (2 + len(prefix)),
        )(later, total, received, *prefix)
        prefix = [wide]
    sent_parts, kept_parts, w_across, w_held, _ = lax.optimization_barrier(
        (sent_parts, kept_parts, w_across, w_output, total)
    )
    w_beside, w_opposite = swapped(w_held, "mp", 1), swapped(w_across, "mp", 1)
    reads = call(
        read_kernel,
        (f32_lanes, f32_lanes),
        mib=6,
        in_specs=[SMEM_SPEC] + [VMEM_SPEC] * 6,
    )(parity, receptances, here, sent_parts, kept_parts, sent_start, kept_start)
    received, reads = lax.optimization_barrier((received, reads))
    entry = call(
        functools.partial(entry_kernel, bool(prefix)),
        entry_struct,
        mib=4,
        us=1,
        in_specs=[SMEM_SPEC] + [VMEM_SPEC] * (1 + len(prefix)),
    )(later, received, *prefix)
    other = swapped(entry, "seq", 1)
    kept_heads = call(kept_kernel, struct(bf16_lanes.shape, F32), mib=6, us=3)(entry, from_partner, *reads)
    w_beside, w_opposite, other, kept_heads = lax.optimization_barrier((w_beside, w_opposite, other, kept_heads))
    joined = call(finish_kernel, bf16_lanes, mib=6)(other, kept_heads, *reads, group_gain.reshape(1, width))
    joined_whole = lax.all_gather(joined, "mp", axis=2, tiled=True)

    w_blocks = (w_output, w_beside, w_across, w_opposite)
    position = lax.axis_index("mp").astype(jnp.int32).reshape(1)
    own, *sent = call(
        functools.partial(mix_kernel, mp_count),
        (struct((rows, width), F32),) + (struct((rows, width), BF16),) * (mp_count - 1),
        scratch=[
            pltpu.VMEM((rows, full), F32),
            pltpu.VMEM((rows, full), F32),
        ],
        mib=16,
        in_specs=[SMEM_SPEC] + [VMEM_SPEC] * (5 + mp_count),
    )(position, joined_whole, whole, *w_blocks, ffn_key, ffn_value, ln2_gain.reshape(1, full))
    merged = own
    for step, item in enumerate(sent):
        merged = merged + swapped(item, "mp", step + 1).astype(F32)
    return merged.astype(BF16)


def solution(mesh):
    in_specs = (
        P("seq"),
        P("seq", "mp"),
        P("seq", "mp"),
        P(None, "mp"),
        P(),
        P(),
        P(),
        P(None, "mp"),
        P(None, "mp"),
        P(None, "mp"),
        P(),
        P("mp"),
        P(None, "mp"),
        P(),
        P("mp"),
        P(None, "mp"),
        P("mp"),
        P("mp", None),
        P(None, "mp"),
        P("mp", None),
    )
    out_specs = P("seq", "mp")
    return jax.shard_map(
        on_device, mesh=mesh, in_specs=in_specs, out_specs=out_specs, check_vma=False
    )
```

```python
import functools

import jax
import jax.numpy as jnp
from jax import lax
from jax.experimental import pallas as pl
from jax.experimental.pallas import tpu as pltpu
from jax.sharding import PartitionSpec as P

HEAD = 64
DECAY_SCALE = 0.606531
NORM_EPS = 1e-05
GROUP_EPS = 0.00064
UNIT_EPS = 1e-06
F32 = jnp.float32
BF16 = jnp.bfloat16
MIB = 1024 * 1024
VMEM_SPEC = pl.BlockSpec(memory_space=pltpu.VMEM)
SMEM_SPEC = pl.BlockSpec(memory_space=pltpu.SMEM)


def mm(left, right):
    return jnp.dot(left, right, preferred_element_type=F32)


def mm_rows(left, right):
    return lax.dot_general(left, right, (((1,), (1,)), ((), ())), preferred_element_type=F32)


def mm_cols(left, right):
    return lax.dot_general(left, right, (((0,), (0,)), ((), ())), preferred_element_type=F32)


def halves(value):
    high = value.astype(BF16)
    return high, (value - high.astype(F32)).astype(BF16)


def head_sum(value, ones):
    high, low = halves(value)
    return mm(high, ones) + mm(low, ones)


def ids_of(shape, dim):
    return lax.broadcasted_iota(jnp.int32, shape, dim)


def block_ones(width):
    same = ids_of((width, width), 0) // HEAD == ids_of((width, width), 1) // HEAD
    return same


def spread(packed, same_head):
    tiled = jnp.concatenate([packed] * (packed.shape[1] // HEAD), axis=0)
    return jnp.where(same_head, tiled, jnp.zeros_like(tiled))


def layer_norm(values, gain):
    row_mean = jnp.mean(values, axis=-1, keepdims=True)
    centered = values - row_mean
    variance = jnp.mean(centered * centered, axis=-1, keepdims=True)
    return centered * lax.rsqrt(variance + NORM_EPS) * gain


def embed_kernel(ids_ref, fwd_ref, embed_ref, strand_ref, other_ref):
    rows = fwd_ref.shape[0]
    ids = ids_ref[...]
    letters = ids_of((embed_ref.shape[0], rows), 0)
    embed = embed_ref[...]

    def looked_up(values):
        onehot = (values == letters).astype(F32)
        return lax.dot_general(
            onehot,
            embed,
            (((0,), (0,)), ((), ())),
            precision=lax.Precision.HIGHEST,
            preferred_element_type=F32,
        )

    strand_ref[...] = (fwd_ref[...].astype(F32) + looked_up(ids)).astype(BF16)
    other_ref[...] = looked_up(3 - ids)


def strands_kernel(rc_ref, strand_ref, other_ref, out_ref):
    rows = rc_ref.shape[0]
    out_ref[0] = strand_ref[...]
    flip = (ids_of((rows, rows), 0) + ids_of((rows, rows), 1) == rows - 1).astype(F32)
    out_ref[1] = (mm(flip.astype(BF16), rc_ref[...]) + other_ref[...]).astype(BF16)


def inverse_of(pulls, rows):
    row_ids, col_ids = ids_of((rows, rows), 0), ids_of((rows, rows), 1)
    eye = (row_ids == col_ids).astype(F32)
    size = 1
    inverses = None
    while size < rows:
        within = (row_ids // (2 * size) == col_ids // (2 * size)) & (row_ids // size != col_ids // size)
        parts = [jnp.where(within, pull, 0.0) for pull in pulls]
        if size == 1:
            inverses = [eye + part for part in parts]
        else:
            lows = [inverse.astype(BF16) for inverse in inverses]
            products = [mm(part.astype(BF16), low).astype(BF16) for part, low in zip(parts, lows)]
            inverses = [inverse + mm(low, product) for inverse, low, product in zip(inverses, lows, products)]
        size *= 2
    return inverses


def gates(low, w_d2, w_c2, d_base, c_base):
    rank, width = w_d2.shape
    low = jnp.where(ids_of(low.shape, 1) < rank, jnp.tanh(low), low).astype(BF16)
    zero = jnp.zeros((rank, width), BF16)
    both = jnp.concatenate(
        [jnp.concatenate([w_d2, zero], axis=1), jnp.concatenate([zero, w_c2], axis=1)], axis=0
    )
    result = mm(low, both)
    log_decay = -DECAY_SCALE * jax.nn.sigmoid(d_base + result[:, :width])
    return log_decay, jax.nn.sigmoid(c_base + result[:, width:])


def project_kernel(x_ref, gain_ref, mixing_ref, w_k, w_v, w_d1, w_c1, w_d2, w_c2, d_base, c_base, *refs):
    outs, (normed, low_ref, edge_ref, mixed, shifts) = refs[:4], refs[4:]
    strands, rows, _ = x_ref.shape
    shape = outs[0].shape
    pad = 8
    gain = gain_ref[...]
    lows = [(w_d1[...].astype(F32), mixing_ref[3:4]), (w_c1[...].astype(F32), mixing_ref[4:5])]
    parts = [weight * (1.0 - share) for weight, share in lows] + [weight * share for weight, share in lows]
    low_ref[...] = jnp.concatenate(parts, axis=0).astype(BF16)
    half = low_ref.shape[0] // 2
    for s in range(strands):
        values = layer_norm(x_ref[s].astype(F32), gain)
        zero = jnp.zeros_like(values[:1])
        normed[s, pad : pad + rows, :] = values
        normed[s, pad - 1 : pad, :] = zero
        normed[s, pad + rows : pad + rows + 1, :] = zero
        edge_ref[s : s + 1, :] = values[:1]
        edge_ref[strands + s : strands + s + 1, :] = values[rows - 1 :]
        low = mm_rows(values.astype(BF16), low_ref[...])
        shifts[s, pad : pad + rows, :] = low[:, half:]
        shifts[s, pad - 1 : pad, :] = zero[:, :half]
        shifts[s, pad + rows : pad + rows + 1, :] = zero[:, :half]
        for d in range(2):
            shift = pad - 1 + 2 * d
            g = d * strands + s
            log_decay, rate = gates(
                low[:, :half] + shifts[s, shift : shift + rows, :], w_d2[...], w_c2[...], d_base[...], c_base[...]
            )
            outs[2][g] = log_decay
            outs[3][g] = rate
    blend(normed, mixing_ref, (1, 2), rows, mixed)
    outs[0][...] = mm(mixed[0], w_k[...]).reshape(shape)
    outs[1][...] = mm(mixed[1], w_v[...]).reshape(shape)


def blend(normed, mixing_ref, indices, rows, mixed):
    strands = normed.shape[0]
    step, pad = 16, 8
    for s in range(strands):
        for start in range(0, rows, step):
            center = normed[s, pad + start : pad + start + step, :]
            for d in range(2):
                shift = pad + start - 1 + 2 * d
                change = normed[s, shift : shift + step, :] - center
                place = (d * strands + s) * rows + start
                for slot, index in enumerate(indices):
                    weight = mixing_ref[index : index + 1, :]
                    mixed[slot, place : place + step, :] = (center + change * weight).astype(BF16)


def receptance_kernel(direction_ref, normed, mixing_ref, sent_edge_ref, kept_edge_ref, w_r, out_ref, mixed):
    groups, rows, _ = out_ref.shape
    blend(normed, mixing_ref, (0,), rows, mixed)
    out_ref[...] = mm(mixed[0], w_r[...]).reshape(out_ref.shape)
    edges = [sent_edge_ref[...], kept_edge_ref[...]]
    swap = direction_ref[0] == 1
    edges = [jnp.where(swap, edges[1 - d], edges[d]) for d in range(2)]
    edges = mm(jnp.concatenate(edges, axis=0).astype(BF16), w_r[...])
    for g in range(groups):
        row = 0 if g < groups // 2 else rows - 1
        out_ref[g, row : row + 1] = edges[g : g + 1]


def masked_heads(value, lane_head, heads):
    return jnp.concatenate([jnp.where(lane_head == h, value, 0.0).astype(BF16) for h in range(heads)], axis=0)


def chunk_kernel(direction_ref, *refs):
    lanes, (halo_ref, edge_ref, low_ref, gain_ref, mixing_ref, w_k, w_v, *gate_refs) = refs[:4], refs[4:15]
    state_ref, parts_ref, here_ref, read_edge_ref = refs[15:]
    strands, _, rows, width = parts_ref.shape
    heads = width // HEAD
    d = direction_ref[0]
    center = jnp.where(d == 1, edge_ref[strands:], edge_ref[:strands])
    halo = layer_norm(halo_ref[...].astype(F32), gain_ref[...])
    change = halo - center

    def mix(index):
        return (center + change * mixing_ref[index : index + 1, :]).astype(BF16)

    low = mm_rows(jnp.concatenate([center, halo], axis=0).astype(BF16), low_ref[...])
    half = low.shape[1] // 2
    low = low[:strands, :half] + low[strands:, half:]
    edges = [mm(mix(1), w_k[...]), mm(mix(2), w_v[...]), *gates(low, *[ref[...] for ref in gate_refs])]
    read_edge_ref[...] = center + change * mixing_ref[0:1, :]
    edge_row = d * (rows - 1)
    at_edge = ids_of((rows, width), 0) == edge_row
    order = (ids_of((rows, rows), 0) - ids_of((rows, rows), 1)) * (1 - 2 * d)
    strict, inclusive = order > 0, order >= 0
    same = block_ones(width)
    ones = same.astype(F32).astype(BF16)
    lane_head = ids_of((1, width), 1) // HEAD
    tri = inclusive.astype(F32).astype(BF16)

    def of_heads(value):
        return masked_heads(value, lane_head, heads)

    def prepared(s):
        g = d * strands + s

        def lane(index, ref):
            return jnp.where(at_edge, edges[index][s : s + 1], ref[g])

        key, value, log_decay, rate = [lane(index, ref) for index, ref in enumerate(lanes)]
        unit = key * lax.rsqrt(head_sum(key * key, ones) + UNIT_EPS)
        high, low = halves(log_decay)
        totals = mm(tri, high) + mm(tri, low)
        middle = totals[rows // 2 : rows // 2 + 1]
        final = jnp.where(d == 0, totals[rows - 1 : rows], totals[0:1])
        there = jnp.exp(middle - totals)
        left_prev = -unit * jnp.exp(totals - log_decay - middle)
        right_insert = rate * unit * there
        right_key = key * there
        from_start = jnp.exp(middle)
        to_end = jnp.exp(final - middle)
        left = left_prev.astype(BF16)
        insert_pulls, key_pulls = [], []
        for h in range(heads):
            mask = lane_head == h
            right = jnp.concatenate(
                [jnp.where(mask, right_insert, 0.0), jnp.where(mask, right_key, 0.0)], axis=0
            ).astype(BF16)
            scores = mm_rows(left, right)
            insert_pulls.append(jnp.where(strict, scores[:, :rows], 0.0))
            key_pulls.append(jnp.where(strict, scores[:, rows:], 0.0).astype(BF16))
        value_pull = mm(jnp.concatenate(key_pulls, axis=1), of_heads(value))
        value = value.astype(BF16)
        here_ref[s, :rows] = jnp.exp(totals - middle)
        here_ref[s, rows:] = jnp.broadcast_to(from_start, (here_ref.shape[1] - rows, width))
        parts_ref[s, 0] = right_insert.astype(BF16)
        parts_ref[s, 1] = right_key.astype(BF16)
        parts_ref[s, 2] = value
        tail_insert = (right_insert * to_end).astype(BF16)
        tail_key = (right_key * to_end).astype(BF16)
        solved_for = jnp.concatenate([of_heads(value_pull), of_heads(left_prev * from_start)], axis=1)
        end = mm_cols(tail_key, value)
        return insert_pulls, (solved_for, tail_insert, end, jnp.exp(final))

    prepared_all = [prepared(s) for s in range(strands)]
    inverses = inverse_of([pull for pulls, _ in prepared_all for pull in pulls], rows)
    for s, (_, (solved_for, tail_insert, end, kept)) in enumerate(prepared_all):
        own = inverses[s * heads : (s + 1) * heads]
        inverse = jnp.concatenate([item.astype(BF16) for item in own], axis=1)
        solved = mm(inverse, solved_for).astype(BF16)
        parts_ref[s, 3] = solved[:, :width]
        parts_ref[s, 4] = solved[:, width:]
        added = mm_cols(tail_insert, solved)
        ends = jnp.where(same, end + added[:, :width], 0.0)
        maps = jnp.where(same, added[:, width:], 0.0)
        end = sum(ends[h * HEAD : (h + 1) * HEAD] for h in range(heads))
        across = sum(maps[h * HEAD : (h + 1) * HEAD] for h in range(heads))
        diagonal = ids_of((HEAD, width), 0) == ids_of((HEAD, width), 1) % HEAD
        across = across + jnp.where(diagonal, kept, 0.0)
        state_ref[s] = jnp.concatenate([end, across], axis=0).astype(BF16)


def read_kernel(
    direction_ref, receptances, sent_ref, kept_ref, sent_here_ref, kept_here_ref, local_ref, map_ref
):
    strands, _, rows, width = sent_ref.shape
    heads = width // HEAD
    lane_head = ids_of((1, width), 1) // HEAD
    for role, (parts_ref, here_ref) in enumerate(((sent_ref, sent_here_ref), (kept_ref, kept_here_ref))):
        d = (direction_ref[0] + role) % 2
        inclusive = (ids_of((rows, rows), 0) - ids_of((rows, rows), 1)) * (1 - 2 * d) >= 0

        def group(s, carry):
            insert, key, value, pull, start = [parts_ref[s, i] for i in range(5)]
            left = receptances[d * strands + s] * here_ref[s, :rows]
            here = left.astype(BF16)
            reads = []
            for source in (insert, key):
                scores = mm_rows(here, masked_heads(source, lane_head, heads))
                parts = [scores[:, h * rows : (h + 1) * rows] for h in range(heads)]
                reads.append(jnp.concatenate([jnp.where(inclusive, p, 0.0).astype(BF16) for p in parts], axis=1))
            pull, start, value = [
                masked_heads(item, lane_head, heads) for item in (pull, start, value)
            ]
            g = role * strands + s
            local_ref[g] = mm(reads[0], pull) + mm(reads[1], value)
            map_ref[g] = left * here_ref[s, rows : rows + 1] + mm(reads[0], start)
            return carry

        lax.fori_loop(0, strands, group, 0)


def composed(later, earlier, same_head, state_only=False):
    across = later[HEAD:].astype(BF16)
    state = mm(across, spread(earlier[:HEAD].astype(BF16), same_head)) + later[:HEAD].astype(F32)
    if state_only:
        return state
    return jnp.concatenate([state, mm(across, spread(earlier[HEAD:].astype(BF16), same_head))], axis=0)


def pair_kernel(keep_ref, from_ref, pair_ref):
    same_head = block_ones(keep_ref.shape[2])
    for s in range(keep_ref.shape[0]):
        pair_ref[s] = composed(keep_ref[s], from_ref[s], same_head).astype(BF16)


def advance_kernel(has_prefix, later_ref, total_ref, from_ref, *refs):
    *prefix_ref, wide_ref, next_ref = refs
    state_only = next_ref.shape[1] == HEAD
    same_head = block_ones(total_ref.shape[2])
    later = later_ref[0] == 1
    shape = total_ref.shape[1:]
    within = (ids_of(shape, 0) - HEAD) == ids_of(shape, 1) % HEAD
    for s in range(total_ref.shape[0]):
        own, other = total_ref[s], from_ref[s]
        total = composed(jnp.where(later, own, other), jnp.where(later, other, own), same_head, state_only)
        next_ref[s] = total.astype(BF16)
        ahead = jnp.where(later, other.astype(F32), within.astype(F32))
        if has_prefix:
            ahead = composed(prefix_ref[0][s], ahead, same_head)
        wide_ref[s] = ahead


def entry_kernel(has_prefix, later_ref, from_ref, *refs):
    *prefix_ref, entry_ref = refs
    same_head = block_ones(entry_ref.shape[2])
    for s in range(entry_ref.shape[0]):
        other = from_ref[s]
        ahead = jnp.where(later_ref[0] == 1, other, jnp.zeros_like(other))
        if has_prefix:
            ahead = composed(prefix_ref[0][s], ahead, same_head, True)
        entry_ref[s] = ahead.astype(BF16)


def normed_heads(role, states, local_ref, map_ref):
    strands, width = len(states), local_ref.shape[2]
    same_head = block_ones(width)
    ones = same_head.astype(F32).astype(BF16)
    for s, state in enumerate(states):
        g = role * strands + s
        high, low = halves(map_ref[g])
        held, rest = [spread(item, same_head) for item in halves(state.astype(F32))]
        wkv = local_ref[g] + mm(high, held) + (mm(low, held) + mm(high, rest))
        centered = wkv - head_sum(wkv, ones) * (1.0 / HEAD)
        variance = head_sum(centered * centered, ones) * (1.0 / HEAD)
        yield centered * lax.rsqrt(variance + GROUP_EPS)


def kept_kernel(entry_ref, from_ref, local_ref, map_ref, out_ref):
    same_head = block_ones(out_ref.shape[2])
    states = [composed(from_ref[s], entry_ref[s], same_head, True) for s in range(out_ref.shape[0])]
    for s, result in enumerate(normed_heads(1, states, local_ref, map_ref)):
        out_ref[s] = result


def finish_kernel(other_ref, kept_ref, local_ref, map_ref, gain_ref, out_ref):
    states = [other_ref[s] for s in range(out_ref.shape[0])]
    for s, result in enumerate(normed_heads(0, states, local_ref, map_ref)):
        out_ref[s] = ((result + kept_ref[s]) * gain_ref[...]).astype(BF16)


def mix_kernel(blocks, index_ref, joined_ref, x_ref, *refs):
    w_refs, (up_ref, down_ref, gain_ref, own_ref) = refs[:blocks], refs[blocks : blocks + 4]
    added_ref, *sent_refs, total = refs[blocks + 4 :]
    strands, rows, _ = x_ref.shape
    width = own_ref.shape[1]
    gain = gain_ref[...]
    me = index_ref[0]
    attention = 0.0
    for step, w_ref in enumerate(w_refs):
        start = pl.multiple_of((me ^ step) * width, width)
        joined = jnp.concatenate([joined_ref[s, :, pl.ds(start, width)] for s in range(strands)], axis=0)
        attention = attention + mm(joined, w_ref[...])
    residuals = [x_ref[s].astype(F32) + attention[s * rows : (s + 1) * rows] for s in range(strands)]
    inner = jnp.concatenate([layer_norm(item, gain).astype(BF16) for item in residuals], axis=0)
    active = jnp.square(jnp.maximum(mm(inner, up_ref[...]), 0.0)).astype(BF16).astype(F32)
    added = sum(active[s * rows : (s + 1) * rows] for s in range(strands)).astype(BF16)
    added_ref[...] = added
    for mask, ref in enumerate(sent_refs, blocks - len(sent_refs)):
        ref[...] = mm(added, columns_of(down_ref, me ^ mask, width)).astype(BF16)
    total[...] = sum(residuals)
    own_ref[...] = columns_of(total, me, width)


def columns_of(ref, which, width):
    return ref[:, pl.ds(pl.multiple_of(which * width, width), width)]


def near_kernel(index_ref, added_ref, held_ref, down_ref, own_ref, *sent_refs):
    me, width = index_ref[0], own_ref.shape[1]
    added = added_ref[...]
    for mask, ref in enumerate(sent_refs, 1):
        ref[...] = mm(added, columns_of(down_ref, me ^ mask, width)).astype(BF16)
    own_ref[...] = held_ref[...] + mm(added, columns_of(down_ref, me, width))


def call(kernel, out_shape, scratch=(), mib=12, us=10, **kwargs):
    return pl.pallas_call(
        kernel,
        out_shape=out_shape,
        scratch_shapes=list(scratch),
        cost_estimate=pl.CostEstimate(flops=us * 10**9, bytes_accessed=us * 10**6, transcendentals=0),
        compiler_params=pltpu.CompilerParams(vmem_limit_bytes=mib * MIB),
        **kwargs,
    )


def swapped(value, axis, mask):
    return lax.ppermute(value, axis, [(i, i ^ mask) for i in range(lax.axis_size(axis))])


def on_device(
    ids,
    hidden_fwd,
    hidden_rc,
    embed,
    ln1_gain,
    ln2_gain,
    mixing,
    w_receptance,
    w_key,
    w_value,
    decay_first_weight,
    decay_base,
    decay_second_weight,
    context_rate_first_weight,
    iclr_base,
    context_rate_second_weight,
    group_gain,
    w_output,
    ffn_key,
    ffn_value,
):
    rows, width = hidden_fwd.shape
    seq_count, mp_count = lax.axis_size("seq"), lax.axis_size("mp")
    strands, full = 2, ffn_key.shape[0]
    struct = jax.ShapeDtypeStruct

    mirror = [(i, seq_count - 1 - i) for i in range(seq_count)]
    rc_here = lax.ppermute(hidden_rc, "seq", mirror)
    params = (
        ln1_gain.reshape(1, full),
        mixing,
        w_key,
        w_value,
        decay_first_weight.T,
        context_rate_first_weight.T,
        decay_second_weight,
        context_rate_second_weight,
        decay_base.reshape(1, width),
        iclr_base.reshape(1, width),
    )
    strand, other = call(
        embed_kernel, (struct((rows, width), BF16), struct((rows, width), F32)), us=10, mib=4
    )(ids.reshape(1, rows), hidden_fwd, embed)
    rc_here, strand, other = lax.optimization_barrier((rc_here, strand, other))
    local = call(strands_kernel, struct((strands, rows, width), BF16), us=10, mib=4)(rc_here, strand, other)
    whole = lax.all_gather(local, "mp", axis=2, tiled=True)
    place = lax.axis_index("seq").astype(jnp.int32)
    parity = place % 2
    first, last = whole[:, 0], whole[:, rows - 1]
    bridges = [(i, i + 1) for i in range(1, seq_count - 1, 2)]
    bridges += [(j, i) for i, j in bridges]
    far = lax.ppermute(jnp.where(parity == 1, last, first), "seq", bridges)
    parity = parity.reshape(1)

    groups = 2 * strands
    f32_lanes, bf16_lanes = struct((groups, rows, width), F32), struct((strands, rows, width), BF16)
    parts_struct = struct((strands, 5, rows, width), BF16)
    here_struct = struct((strands, rows + 8, width), F32)
    state_struct = struct((strands, 2 * HEAD, width), BF16)
    entry_struct = struct((strands, HEAD, width), BF16)
    low_shape = (4 * decay_first_weight.shape[1], full)
    *lanes, normed, low, edge = call(
        project_kernel,
        (f32_lanes,) * 4
        + (
            struct((strands, rows + 16, full), F32),
            struct(low_shape, BF16),
            struct((groups, full), F32),
        ),
        scratch=[
            pltpu.VMEM((2, groups * rows, full), BF16),
            pltpu.VMEM((strands, rows + 16, low_shape[0] // 2), F32),
        ],
    )(whole, *params)

    beside, _ = lax.optimization_barrier((jnp.where(parity == 1, first, last), edge))
    near = swapped(beside, "seq", 1)

    def chunk(direction, halo):
        return call(
            chunk_kernel,
            (state_struct, parts_struct, here_struct, struct((strands, full), F32)),
            in_specs=[SMEM_SPEC] + [VMEM_SPEC] * 15,
        )(direction, *lanes, halo, edge, low, *params[:4], *params[6:])

    sent, sent_parts, sent_here, sent_edge = chunk(parity, far)
    from_partner = swapped(sent, "seq", 1)
    kept, kept_parts, kept_here, kept_edge = chunk(1 - parity, near)

    total = call(pair_kernel, state_struct, mib=4, us=1)(kept, from_partner)
    w_held, _ = lax.optimization_barrier((w_output, total))
    w_across = swapped(w_held, "mp", 2)
    kept_edge, _ = lax.optimization_barrier((kept_edge, total))
    receptances = call(
        receptance_kernel,
        f32_lanes,
        scratch=[pltpu.VMEM((1, groups * rows, full), BF16)],
        mib=6,
        us=3,
        in_specs=[SMEM_SPEC] + [VMEM_SPEC] * 5,
    )(parity, normed, mixing, sent_edge, kept_edge, w_receptance)
    prefix = []
    bits = range(1, seq_count.bit_length() - 1)
    for bit in bits:
        later = ((place >> bit) % 2 == place % 2).astype(jnp.int32).reshape(1)
        received = swapped(total, "seq", 1 << bit)
        if bit == bits[0]:
            received, receptances = lax.optimization_barrier((received, receptances))
        if bit == bits[-1]:
            break
        wide, total = call(
            functools.partial(advance_kernel, bool(prefix)),
            (struct(state_struct.shape, F32), entry_struct if bit + 1 == bits[-1] else state_struct),
            mib=4,
            us=1,
            in_specs=[SMEM_SPEC] + [VMEM_SPEC] * (2 + len(prefix)),
        )(later, total, received, *prefix)
        prefix = [wide]
    w_held, _ = lax.optimization_barrier((w_output, total))
    w_beside = swapped(w_held, "mp", 1)
    sent_parts, kept_parts, _ = lax.optimization_barrier((sent_parts, kept_parts, total))
    reads = call(
        read_kernel,
        (f32_lanes, f32_lanes),
        mib=6,
        in_specs=[SMEM_SPEC] + [VMEM_SPEC] * 5,
    )(parity, receptances, sent_parts, kept_parts, sent_here, kept_here)
    received, reads = lax.optimization_barrier((received, reads))
    entry = call(
        functools.partial(entry_kernel, bool(prefix)),
        entry_struct,
        mib=4,
        us=1,
        in_specs=[SMEM_SPEC] + [VMEM_SPEC] * (1 + len(prefix)),
    )(later, received, *prefix)
    other = swapped(entry, "seq", 1)
    kept_heads = call(kept_kernel, struct(bf16_lanes.shape, F32), mib=6, us=3)(entry, from_partner, *reads)
    w_across, other, kept_heads = lax.optimization_barrier((w_across, other, kept_heads))
    w_opposite = swapped(w_across, "mp", 1)
    joined = call(finish_kernel, bf16_lanes, mib=6)(other, kept_heads, *reads, group_gain.reshape(1, width))
    joined_whole = lax.all_gather(joined, "mp", axis=2, tiled=True)

    w_blocks = (w_output, w_beside, w_across, w_opposite)
    position = lax.axis_index("mp").astype(jnp.int32).reshape(1)
    near_count = mp_count // 2
    own_struct, sent_struct = struct((rows, width), F32), struct((rows, width), BF16)
    held, added, *far_parts = call(
        functools.partial(mix_kernel, mp_count),
        (own_struct, struct((rows, ffn_key.shape[1]), BF16)) + (sent_struct,) * near_count,
        scratch=[pltpu.VMEM((rows, full), F32)],
        mib=16,
        in_specs=[SMEM_SPEC] + [VMEM_SPEC] * (5 + mp_count),
    )(position, joined_whole, whole, *w_blocks, ffn_key, ffn_value, ln2_gain.reshape(1, full))
    arrivals = [swapped(item, "mp", mask) for mask, item in enumerate(far_parts, near_count)]
    own, *near_parts = call(
        near_kernel,
        (own_struct,) + (sent_struct,) * (near_count - 1),
        mib=6,
        us=1,
        in_specs=[SMEM_SPEC] + [VMEM_SPEC] * 3,
    )(position, added, held, ffn_value)
    arrivals += [swapped(item, "mp", mask) for mask, item in enumerate(near_parts, 1)]
    merged = own
    for item in reversed(arrivals):
        merged = merged + item.astype(F32)
    return merged.astype(BF16)


def solution(mesh):
    in_specs = (
        P("seq"),
        P("seq", "mp"),
        P("seq", "mp"),
        P(None, "mp"),
        P(),
        P(),
        P(),
        P(None, "mp"),
        P(None, "mp"),
        P(None, "mp"),
        P(),
        P("mp"),
        P(None, "mp"),
        P(),
        P("mp"),
        P(None, "mp"),
        P("mp"),
        P("mp", None),
        P(None, "mp"),
        P("mp", None),
    )
    out_specs = P("seq", "mp")
    return jax.shard_map(
        on_device, mesh=mesh, in_specs=in_specs, out_specs=out_specs, check_vma=False
    )
```

```python
import functools

import jax
import jax.numpy as jnp
from jax import lax
from jax.experimental import pallas as pl
from jax.experimental.pallas import tpu as pltpu
from jax.sharding import PartitionSpec as P

HEAD = 64
DECAY_SCALE = 0.606531
NORM_EPS = 1e-05
GROUP_EPS = 0.00064
UNIT_EPS = 1e-06
F32 = jnp.float32
BF16 = jnp.bfloat16
MIB = 1024 * 1024
VMEM_SPEC = pl.BlockSpec(memory_space=pltpu.VMEM)
SMEM_SPEC = pl.BlockSpec(memory_space=pltpu.SMEM)


def mm(left, right):
    return jnp.dot(left, right, preferred_element_type=F32)


def mm_rows(left, right):
    return lax.dot_general(left, right, (((1,), (1,)), ((), ())), preferred_element_type=F32)


def mm_cols(left, right):
    return lax.dot_general(left, right, (((0,), (0,)), ((), ())), preferred_element_type=F32)


def halves(value):
    high = value.astype(BF16)
    return high, (value - high.astype(F32)).astype(BF16)


def head_sum(value, ones):
    high, low = halves(value)
    return mm(high, ones) + mm(low, ones)


def ids_of(shape, dim):
    return lax.broadcasted_iota(jnp.int32, shape, dim)


def block_ones(width):
    same = ids_of((width, width), 0) // HEAD == ids_of((width, width), 1) // HEAD
    return same


def spread(packed, same_head):
    tiled = jnp.concatenate([packed] * (packed.shape[1] // HEAD), axis=0)
    return jnp.where(same_head, tiled, jnp.zeros_like(tiled))


def layer_norm(values, gain):
    row_mean = jnp.mean(values, axis=-1, keepdims=True)
    centered = values - row_mean
    variance = jnp.mean(centered * centered, axis=-1, keepdims=True)
    return centered * lax.rsqrt(variance + NORM_EPS) * gain


def embed_kernel(ids_ref, fwd_ref, embed_ref, strand_ref, other_ref):
    rows = fwd_ref.shape[0]
    ids = ids_ref[...]
    letters = ids_of((embed_ref.shape[0], rows), 0)
    embed = embed_ref[...]

    def looked_up(values):
        onehot = (values == letters).astype(F32)
        return lax.dot_general(
            onehot,
            embed,
            (((0,), (0,)), ((), ())),
            precision=lax.Precision.HIGHEST,
            preferred_element_type=F32,
        )

    strand_ref[...] = (fwd_ref[...].astype(F32) + looked_up(ids)).astype(BF16)
    other_ref[...] = looked_up(3 - ids)


def strands_kernel(rc_ref, strand_ref, other_ref, out_ref):
    rows = rc_ref.shape[0]
    out_ref[0] = strand_ref[...]
    flip = (ids_of((rows, rows), 0) + ids_of((rows, rows), 1) == rows - 1).astype(F32)
    out_ref[1] = (mm(flip.astype(BF16), rc_ref[...]) + other_ref[...]).astype(BF16)


def inverse_of(pulls, rows):
    row_ids, col_ids = ids_of((rows, rows), 0), ids_of((rows, rows), 1)
    eye = (row_ids == col_ids).astype(F32)
    size = 1
    inverses = None
    while size < rows:
        within = (row_ids // (2 * size) == col_ids // (2 * size)) & (row_ids // size != col_ids // size)
        parts = [jnp.where(within, pull, 0.0) for pull in pulls]
        if size == 1:
            inverses = [eye + part for part in parts]
        else:
            lows = [inverse.astype(BF16) for inverse in inverses]
            products = [mm(part.astype(BF16), low).astype(BF16) for part, low in zip(parts, lows)]
            inverses = [inverse + mm(low, product) for inverse, low, product in zip(inverses, lows, products)]
        size *= 2
    return inverses


def gates(low, w_d2, w_c2, d_base, c_base):
    rank, width = w_d2.shape
    low = jnp.where(ids_of(low.shape, 1) < rank, jnp.tanh(low), low).astype(BF16)
    zero = jnp.zeros((rank, width), BF16)
    both = jnp.concatenate(
        [jnp.concatenate([w_d2, zero], axis=1), jnp.concatenate([zero, w_c2], axis=1)], axis=0
    )
    result = mm(low, both)
    log_decay = -DECAY_SCALE * jax.nn.sigmoid(d_base + result[:, :width])
    return log_decay, jax.nn.sigmoid(c_base + result[:, width:])


def project_kernel(x_ref, gain_ref, mixing_ref, w_k, w_v, w_d1, w_c1, w_d2, w_c2, d_base, c_base, *refs):
    outs, (rows_ref, normed, low_ref, edge_ref, mixed, shifts) = refs[:5], refs[5:]
    prev_ref, insert_ref, key_ref, value_ref, here_ref = outs
    strands, rows, _ = x_ref.shape
    shape = outs[0].shape
    pad = 8
    gain = gain_ref[...]
    lows = [(w_d1[...].astype(F32), mixing_ref[3:4]), (w_c1[...].astype(F32), mixing_ref[4:5])]
    parts = [weight * (1.0 - share) for weight, share in lows] + [weight * share for weight, share in lows]
    low_ref[...] = jnp.concatenate(parts, axis=0).astype(BF16)
    half = low_ref.shape[0] // 2
    gated = {}
    for s in range(strands):
        values = layer_norm(x_ref[s].astype(F32), gain)
        zero = jnp.zeros_like(values[:1])
        normed[s, pad : pad + rows, :] = values
        normed[s, pad - 1 : pad, :] = zero
        normed[s, pad + rows : pad + rows + 1, :] = zero
        edge_ref[s : s + 1, :] = values[:1]
        edge_ref[strands + s : strands + s + 1, :] = values[rows - 1 :]
        low = mm_rows(values.astype(BF16), low_ref[...])
        shifts[s, pad : pad + rows, :] = low[:, half:]
        shifts[s, pad - 1 : pad, :] = zero[:, :half]
        shifts[s, pad + rows : pad + rows + 1, :] = zero[:, :half]
        for d in range(2):
            shift = pad - 1 + 2 * d
            g = d * strands + s
            gated[g] = gates(
                low[:, :half] + shifts[s, shift : shift + rows, :], w_d2[...], w_c2[...], d_base[...], c_base[...]
            )
    blend(normed, mixing_ref, (1, 2), rows, mixed)
    keys = mm(mixed[0], w_k[...])
    value_ref[...] = mm(mixed[1], w_v[...]).reshape(shape)
    ones = block_ones(shape[2]).astype(F32).astype(BF16)
    order = ids_of((rows, rows), 0) - ids_of((rows, rows), 1)
    row_ids = ids_of(shape[1:], 0)
    for g in range(shape[0]):
        d = g // strands
        edge = d * (rows - 1)
        key = keys[g * rows : (g + 1) * rows]
        log_decay, rate = gated[g]
        unit = key * lax.rsqrt(head_sum(key * key, ones) + UNIT_EPS)
        log_decay = jnp.where(row_ids == edge, 0.0, log_decay)
        tri = ((order if d == 0 else -order) >= 0).astype(F32).astype(BF16)
        high, low = halves(log_decay)
        totals = mm(tri, high) + mm(tri, low)
        middle = totals[rows // 2 : rows // 2 + 1]
        there = jnp.exp(middle - totals)
        prev_ref[g] = -unit * jnp.exp(totals - log_decay - middle)
        insert_ref[g] = rate * unit * there
        key_ref[g] = key * there
        here_ref[g] = jnp.exp(totals - middle)
        final = rows - 1 - edge
        rows_ref[g, 0:1] = there[edge : edge + 1]
        rows_ref[g, 1:2] = middle
        rows_ref[g, 2:3] = totals[final : final + 1]


def blend(normed, mixing_ref, indices, rows, mixed):
    strands = normed.shape[0]
    step, pad = 16, 8
    for s in range(strands):
        for start in range(0, rows, step):
            center = normed[s, pad + start : pad + start + step, :]
            for d in range(2):
                shift = pad + start - 1 + 2 * d
                change = normed[s, shift : shift + step, :] - center
                place = (d * strands + s) * rows + start
                for slot, index in enumerate(indices):
                    weight = mixing_ref[index : index + 1, :]
                    mixed[slot, place : place + step, :] = (center + change * weight).astype(BF16)


def receptance_kernel(direction_ref, normed, mixing_ref, sent_edge_ref, kept_edge_ref, w_r, out_ref, mixed):
    groups, rows, _ = out_ref.shape
    blend(normed, mixing_ref, (0,), rows, mixed)
    out_ref[...] = mm(mixed[0], w_r[...]).reshape(out_ref.shape)
    edges = [sent_edge_ref[...], kept_edge_ref[...]]
    swap = direction_ref[0] == 1
    edges = [jnp.where(swap, edges[1 - d], edges[d]) for d in range(2)]
    edges = mm(jnp.concatenate(edges, axis=0).astype(BF16), w_r[...])
    for g in range(groups):
        row = 0 if g < groups // 2 else rows - 1
        out_ref[g, row : row + 1] = edges[g : g + 1]


def masked_heads(value, lane_head, heads):
    return jnp.concatenate([jnp.where(lane_head == h, value, 0.0).astype(BF16) for h in range(heads)], axis=0)


def chunk_kernel(direction_ref, *refs):
    prev_ref, insert_ref, key_ref, value_ref, rows_ref = refs[:5]
    halo_ref, edge_ref, low_ref, gain_ref, mixing_ref, w_k, w_v, *gate_refs = refs[5:16]
    state_ref, parts_ref, start_ref, read_edge_ref = refs[16:]
    strands, _, rows, width = parts_ref.shape
    heads = width // HEAD
    d = direction_ref[0]
    center = jnp.where(d == 1, edge_ref[strands:], edge_ref[:strands])
    halo = layer_norm(halo_ref[...].astype(F32), gain_ref[...])
    change = halo - center

    def mix(index):
        return (center + change * mixing_ref[index : index + 1, :]).astype(BF16)

    low = mm_rows(jnp.concatenate([center, halo], axis=0).astype(BF16), low_ref[...])
    half = low.shape[1] // 2
    low = low[:strands, :half] + low[strands:, half:]
    edge_key, edge_value = mm(mix(1), w_k[...]), mm(mix(2), w_v[...])
    edge_decay, edge_rate = gates(low, *[ref[...] for ref in gate_refs])
    read_edge_ref[...] = center + change * mixing_ref[0:1, :]
    edge_row = d * (rows - 1)
    at_edge = ids_of((rows, width), 0) == edge_row
    order = (ids_of((rows, rows), 0) - ids_of((rows, rows), 1)) * (1 - 2 * d)
    strict = order > 0
    same = block_ones(width)
    ones = same.astype(F32).astype(BF16)
    lane_head = ids_of((1, width), 1) // HEAD
    edge_unit = edge_key * lax.rsqrt(head_sum(edge_key * edge_key, ones) + UNIT_EPS)

    def of_heads(value):
        return masked_heads(value, lane_head, heads)

    def prepared(s):
        g = d * strands + s

        def patched(ref, row):
            return jnp.where(at_edge, row, ref[g])

        one = slice(s, s + 1)
        there, middle, final = [rows_ref[g, i : i + 1] for i in range(3)]
        from_start = jnp.exp(middle + edge_decay[one])
        to_end = jnp.exp(final - middle)
        final = final + edge_decay[one]
        left_prev = patched(prev_ref, -edge_unit[one] * jnp.exp(-middle - edge_decay[one]))
        right_insert = patched(insert_ref, edge_rate[one] * edge_unit[one] * there)
        right_key = patched(key_ref, edge_key[one] * there)
        value = patched(value_ref, edge_value[one])
        left = left_prev.astype(BF16)
        insert_pulls, key_pulls = [], []
        for h in range(heads):
            mask = lane_head == h
            right = jnp.concatenate(
                [jnp.where(mask, right_insert, 0.0), jnp.where(mask, right_key, 0.0)], axis=0
            ).astype(BF16)
            scores = mm_rows(left, right)
            insert_pulls.append(jnp.where(strict, scores[:, :rows], 0.0))
            key_pulls.append(jnp.where(strict, scores[:, rows:], 0.0).astype(BF16))
        value_pull = mm(jnp.concatenate(key_pulls, axis=1), of_heads(value))
        value = value.astype(BF16)
        start_ref[s] = jnp.broadcast_to(from_start, start_ref.shape[1:])
        parts_ref[s, 0] = right_insert.astype(BF16)
        parts_ref[s, 1] = right_key.astype(BF16)
        parts_ref[s, 2] = value
        tail_insert = (right_insert * to_end).astype(BF16)
        tail_key = (right_key * to_end).astype(BF16)
        solved_for = jnp.concatenate([of_heads(value_pull), of_heads(left_prev * from_start)], axis=1)
        end = mm_cols(tail_key, value)
        return insert_pulls, (solved_for, tail_insert, end, jnp.exp(final))

    prepared_all = [prepared(s) for s in range(strands)]
    inverses = inverse_of([pull for pulls, _ in prepared_all for pull in pulls], rows)
    for s, (_, (solved_for, tail_insert, end, kept)) in enumerate(prepared_all):
        own = inverses[s * heads : (s + 1) * heads]
        inverse = jnp.concatenate([item.astype(BF16) for item in own], axis=1)
        solved = mm(inverse, solved_for).astype(BF16)
        parts_ref[s, 3] = solved[:, :width]
        parts_ref[s, 4] = solved[:, width:]
        added = mm_cols(tail_insert, solved)
        ends = jnp.where(same, end + added[:, :width], 0.0)
        maps = jnp.where(same, added[:, width:], 0.0)
        end = sum(ends[h * HEAD : (h + 1) * HEAD] for h in range(heads))
        across = sum(maps[h * HEAD : (h + 1) * HEAD] for h in range(heads))
        diagonal = ids_of((HEAD, width), 0) == ids_of((HEAD, width), 1) % HEAD
        across = across + jnp.where(diagonal, kept, 0.0)
        state_ref[s] = jnp.concatenate([end, across], axis=0).astype(BF16)


def read_kernel(
    direction_ref, receptances, here_ref, sent_ref, kept_ref, sent_start_ref, kept_start_ref, local_ref, map_ref
):
    strands, _, rows, width = sent_ref.shape
    heads = width // HEAD
    lane_head = ids_of((1, width), 1) // HEAD
    for role, (parts_ref, start_ref) in enumerate(((sent_ref, sent_start_ref), (kept_ref, kept_start_ref))):
        d = (direction_ref[0] + role) % 2
        inclusive = (ids_of((rows, rows), 0) - ids_of((rows, rows), 1)) * (1 - 2 * d) >= 0

        def group(s, carry):
            insert, key, value, pull, start = [parts_ref[s, i] for i in range(5)]
            left = receptances[d * strands + s] * here_ref[d * strands + s]
            here = left.astype(BF16)
            reads = []
            for source in (insert, key):
                scores = mm_rows(here, masked_heads(source, lane_head, heads))
                parts = [scores[:, h * rows : (h + 1) * rows] for h in range(heads)]
                reads.append(jnp.concatenate([jnp.where(inclusive, p, 0.0).astype(BF16) for p in parts], axis=1))
            pull, start, value = [
                masked_heads(item, lane_head, heads) for item in (pull, start, value)
            ]
            g = role * strands + s
            local_ref[g] = mm(reads[0], pull) + mm(reads[1], value)
            map_ref[g] = left * start_ref[s, 0:1] + mm(reads[0], start)
            return carry

        lax.fori_loop(0, strands, group, 0)


def composed(later, earlier, same_head, state_only=False):
    across = later[HEAD:].astype(BF16)
    state = mm(across, spread(earlier[:HEAD].astype(BF16), same_head)) + later[:HEAD].astype(F32)
    if state_only:
        return state
    return jnp.concatenate([state, mm(across, spread(earlier[HEAD:].astype(BF16), same_head))], axis=0)


def pair_kernel(keep_ref, from_ref, pair_ref):
    same_head = block_ones(keep_ref.shape[2])
    for s in range(keep_ref.shape[0]):
        pair_ref[s] = composed(keep_ref[s], from_ref[s], same_head).astype(BF16)


def advance_kernel(has_prefix, later_ref, total_ref, from_ref, *refs):
    *prefix_ref, wide_ref, next_ref = refs
    state_only = next_ref.shape[1] == HEAD
    same_head = block_ones(total_ref.shape[2])
    later = later_ref[0] == 1
    shape = total_ref.shape[1:]
    within = (ids_of(shape, 0) - HEAD) == ids_of(shape, 1) % HEAD
    for s in range(total_ref.shape[0]):
        own, other = total_ref[s], from_ref[s]
        total = composed(jnp.where(later, own, other), jnp.where(later, other, own), same_head, state_only)
        next_ref[s] = total.astype(BF16)
        ahead = jnp.where(later, other.astype(F32), within.astype(F32))
        if has_prefix:
            ahead = composed(prefix_ref[0][s], ahead, same_head)
        wide_ref[s] = ahead


def entry_kernel(has_prefix, later_ref, from_ref, *refs):
    *prefix_ref, entry_ref = refs
    same_head = block_ones(entry_ref.shape[2])
    for s in range(entry_ref.shape[0]):
        other = from_ref[s]
        ahead = jnp.where(later_ref[0] == 1, other, jnp.zeros_like(other))
        if has_prefix:
            ahead = composed(prefix_ref[0][s], ahead, same_head, True)
        entry_ref[s] = ahead.astype(BF16)


def normed_heads(role, states, local_ref, map_ref):
    strands, width = len(states), local_ref.shape[2]
    same_head = block_ones(width)
    ones = same_head.astype(F32).astype(BF16)
    for s, state in enumerate(states):
        g = role * strands + s
        high, low = halves(map_ref[g])
        held, rest = [spread(item, same_head) for item in halves(state.astype(F32))]
        wkv = local_ref[g] + mm(high, held) + (mm(low, held) + mm(high, rest))
        centered = wkv - head_sum(wkv, ones) * (1.0 / HEAD)
        variance = head_sum(centered * centered, ones) * (1.0 / HEAD)
        yield centered * lax.rsqrt(variance + GROUP_EPS)


def kept_kernel(entry_ref, from_ref, local_ref, map_ref, out_ref):
    same_head = block_ones(out_ref.shape[2])
    states = [composed(from_ref[s], entry_ref[s], same_head, True) for s in range(out_ref.shape[0])]
    for s, result in enumerate(normed_heads(1, states, local_ref, map_ref)):
        out_ref[s] = result


def finish_kernel(other_ref, kept_ref, local_ref, map_ref, gain_ref, out_ref):
    states = [other_ref[s] for s in range(out_ref.shape[0])]
    for s, result in enumerate(normed_heads(0, states, local_ref, map_ref)):
        out_ref[s] = ((result + kept_ref[s]) * gain_ref[...]).astype(BF16)


def mix_kernel(blocks, index_ref, joined_ref, x_ref, *refs):
    w_refs, (up_ref, down_ref, gain_ref, own_ref) = refs[:blocks], refs[blocks : blocks + 4]
    added_ref, *sent_refs, total = refs[blocks + 4 :]
    strands, rows, _ = x_ref.shape
    width = own_ref.shape[1]
    gain = gain_ref[...]
    me = index_ref[0]
    attention = 0.0
    for step, w_ref in enumerate(w_refs):
        start = pl.multiple_of((me ^ step) * width, width)
        joined = jnp.concatenate([joined_ref[s, :, pl.ds(start, width)] for s in range(strands)], axis=0)
        attention = attention + mm(joined, w_ref[...])
    residuals = [x_ref[s].astype(F32) + attention[s * rows : (s + 1) * rows] for s in range(strands)]
    inner = jnp.concatenate([layer_norm(item, gain).astype(BF16) for item in residuals], axis=0)
    active = jnp.square(jnp.maximum(mm(inner, up_ref[...]), 0.0)).astype(BF16).astype(F32)
    added = sum(active[s * rows : (s + 1) * rows] for s in range(strands)).astype(BF16)
    added_ref[...] = added
    for mask, ref in enumerate(sent_refs, blocks - len(sent_refs)):
        ref[...] = mm(added, columns_of(down_ref, me ^ mask, width)).astype(BF16)
    total[...] = sum(residuals)
    own_ref[...] = columns_of(total, me, width)


def columns_of(ref, which, width):
    return ref[:, pl.ds(pl.multiple_of(which * width, width), width)]


def near_kernel(index_ref, added_ref, held_ref, down_ref, own_ref, *sent_refs):
    me, width = index_ref[0], own_ref.shape[1]
    added = added_ref[...]
    for mask, ref in enumerate(sent_refs, 1):
        ref[...] = mm(added, columns_of(down_ref, me ^ mask, width)).astype(BF16)
    own_ref[...] = held_ref[...] + mm(added, columns_of(down_ref, me, width))


def call(kernel, out_shape, scratch=(), mib=12, us=10, **kwargs):
    return pl.pallas_call(
        kernel,
        out_shape=out_shape,
        scratch_shapes=list(scratch),
        cost_estimate=pl.CostEstimate(flops=us * 10**9, bytes_accessed=us * 10**6, transcendentals=0),
        compiler_params=pltpu.CompilerParams(vmem_limit_bytes=mib * MIB),
        **kwargs,
    )


def swapped(value, axis, mask):
    return lax.ppermute(value, axis, [(i, i ^ mask) for i in range(lax.axis_size(axis))])


def on_device(
    ids,
    hidden_fwd,
    hidden_rc,
    embed,
    ln1_gain,
    ln2_gain,
    mixing,
    w_receptance,
    w_key,
    w_value,
    decay_first_weight,
    decay_base,
    decay_second_weight,
    context_rate_first_weight,
    iclr_base,
    context_rate_second_weight,
    group_gain,
    w_output,
    ffn_key,
    ffn_value,
):
    rows, width = hidden_fwd.shape
    seq_count, mp_count = lax.axis_size("seq"), lax.axis_size("mp")
    strands, full = 2, ffn_key.shape[0]
    struct = jax.ShapeDtypeStruct

    mirror = [(i, seq_count - 1 - i) for i in range(seq_count)]
    rc_here = lax.ppermute(hidden_rc, "seq", mirror)
    params = (
        ln1_gain.reshape(1, full),
        mixing,
        w_key,
        w_value,
        decay_first_weight.T,
        context_rate_first_weight.T,
        decay_second_weight,
        context_rate_second_weight,
        decay_base.reshape(1, width),
        iclr_base.reshape(1, width),
    )
    strand, other = call(
        embed_kernel, (struct((rows, width), BF16), struct((rows, width), F32)), us=10, mib=4
    )(ids.reshape(1, rows), hidden_fwd, embed)
    rc_here, strand, other = lax.optimization_barrier((rc_here, strand, other))
    local = call(strands_kernel, struct((strands, rows, width), BF16), us=10, mib=4)(rc_here, strand, other)
    whole = lax.all_gather(local, "mp", axis=2, tiled=True)
    place = lax.axis_index("seq").astype(jnp.int32)
    parity = place % 2
    first, last = whole[:, 0], whole[:, rows - 1]
    bridges = [(i, i + 1) for i in range(1, seq_count - 1, 2)]
    bridges += [(j, i) for i, j in bridges]
    far = lax.ppermute(jnp.where(parity == 1, last, first), "seq", bridges)
    parity = parity.reshape(1)

    groups = 2 * strands
    f32_lanes, bf16_lanes = struct((groups, rows, width), F32), struct((strands, rows, width), BF16)
    parts_struct = struct((strands, 5, rows, width), BF16)
    start_struct = struct((strands, 8, width), F32)
    state_struct = struct((strands, 2 * HEAD, width), BF16)
    entry_struct = struct((strands, HEAD, width), BF16)
    low_shape = (4 * decay_first_weight.shape[1], full)
    *lanes, here, spans, normed, low, edge = call(
        project_kernel,
        (f32_lanes,) * 5
        + (
            struct((groups, 8, width), F32),
            struct((strands, rows + 16, full), F32),
            struct(low_shape, BF16),
            struct((groups, full), F32),
        ),
        scratch=[
            pltpu.VMEM((2, groups * rows, full), BF16),
            pltpu.VMEM((strands, rows + 16, low_shape[0] // 2), F32),
        ],
    )(whole, *params)

    beside, _ = lax.optimization_barrier((jnp.where(parity == 1, first, last), edge))
    near = swapped(beside, "seq", 1)

    def chunk(direction, halo):
        return call(
            chunk_kernel,
            (state_struct, parts_struct, start_struct, struct((strands, full), F32)),
            in_specs=[SMEM_SPEC] + [VMEM_SPEC] * 16,
        )(direction, *lanes, spans, halo, edge, low, *params[:4], *params[6:])

    sent, sent_parts, sent_start, sent_edge = chunk(parity, far)
    from_partner = swapped(sent, "seq", 1)
    kept, kept_parts, kept_start, kept_edge = chunk(1 - parity, near)

    total = call(pair_kernel, state_struct, mib=4, us=1)(kept, from_partner)
    w_held, _ = lax.optimization_barrier((w_output, total))
    w_across = swapped(w_held, "mp", 2)
    kept_edge, _ = lax.optimization_barrier((kept_edge, total))
    receptances = call(
        receptance_kernel,
        f32_lanes,
        scratch=[pltpu.VMEM((1, groups * rows, full), BF16)],
        mib=6,
        us=3,
        in_specs=[SMEM_SPEC] + [VMEM_SPEC] * 5,
    )(parity, normed, mixing, sent_edge, kept_edge, w_receptance)
    prefix = []
    bits = range(1, seq_count.bit_length() - 1)
    for bit in bits:
        later = ((place >> bit) % 2 == place % 2).astype(jnp.int32).reshape(1)
        received = swapped(total, "seq", 1 << bit)
        if bit == bits[0]:
            received, receptances = lax.optimization_barrier((received, receptances))
        if bit == bits[-1]:
            break
        wide, total = call(
            functools.partial(advance_kernel, bool(prefix)),
            (struct(state_struct.shape, F32), entry_struct if bit + 1 == bits[-1] else state_struct),
            mib=4,
            us=1,
            in_specs=[SMEM_SPEC] + [VMEM_SPEC] * (2 + len(prefix)),
        )(later, total, received, *prefix)
        prefix = [wide]
    w_held, _ = lax.optimization_barrier((w_output, total))
    w_beside = swapped(w_held, "mp", 1)
    sent_parts, kept_parts, _ = lax.optimization_barrier((sent_parts, kept_parts, total))
    reads = call(
        read_kernel,
        (f32_lanes, f32_lanes),
        mib=6,
        in_specs=[SMEM_SPEC] + [VMEM_SPEC] * 6,
    )(parity, receptances, here, sent_parts, kept_parts, sent_start, kept_start)
    received, reads = lax.optimization_barrier((received, reads))
    entry = call(
        functools.partial(entry_kernel, bool(prefix)),
        entry_struct,
        mib=4,
        us=1,
        in_specs=[SMEM_SPEC] + [VMEM_SPEC] * (1 + len(prefix)),
    )(later, received, *prefix)
    other = swapped(entry, "seq", 1)
    kept_heads = call(kept_kernel, struct(bf16_lanes.shape, F32), mib=6, us=3)(entry, from_partner, *reads)
    w_across, other, kept_heads = lax.optimization_barrier((w_across, other, kept_heads))
    w_opposite = swapped(w_across, "mp", 1)
    joined = call(finish_kernel, bf16_lanes, mib=6)(other, kept_heads, *reads, group_gain.reshape(1, width))
    joined_whole = lax.all_gather(joined, "mp", axis=2, tiled=True)

    w_blocks = (w_output, w_beside, w_across, w_opposite)
    position = lax.axis_index("mp").astype(jnp.int32).reshape(1)
    near_count = mp_count // 2
    own_struct, sent_struct = struct((rows, width), F32), struct((rows, width), BF16)
    held, added, *far_parts = call(
        functools.partial(mix_kernel, mp_count),
        (own_struct, struct((rows, ffn_key.shape[1]), BF16)) + (sent_struct,) * near_count,
        scratch=[pltpu.VMEM((rows, full), F32)],
        mib=16,
        in_specs=[SMEM_SPEC] + [VMEM_SPEC] * (5 + mp_count),
    )(position, joined_whole, whole, *w_blocks, ffn_key, ffn_value, ln2_gain.reshape(1, full))
    arrivals = [swapped(item, "mp", mask) for mask, item in enumerate(far_parts, near_count)]
    own, *near_parts = call(
        near_kernel,
        (own_struct,) + (sent_struct,) * (near_count - 1),
        mib=6,
        us=1,
        in_specs=[SMEM_SPEC] + [VMEM_SPEC] * 3,
    )(position, added, held, ffn_value)
    arrivals += [swapped(item, "mp", mask) for mask, item in enumerate(near_parts, 1)]
    merged = own
    for item in reversed(arrivals):
        merged = merged + item.astype(F32)
    return merged.astype(BF16)


def solution(mesh):
    in_specs = (
        P("seq"),
        P("seq", "mp"),
        P("seq", "mp"),
        P(None, "mp"),
        P(),
        P(),
        P(),
        P(None, "mp"),
        P(None, "mp"),
        P(None, "mp"),
        P(),
        P("mp"),
        P(None, "mp"),
        P(),
        P("mp"),
        P(None, "mp"),
        P("mp"),
        P("mp", None),
        P(None, "mp"),
        P("mp", None),
    )
    out_specs = P("seq", "mp")
    return jax.shard_map(
        on_device, mesh=mesh, in_specs=in_specs, out_specs=out_specs, check_vma=False
    )
```
